32 devices in a mesh: dp: 8 (over z, x), mp: 4 (over y, core).
Axes of the slice: x: 2, y: 2, z: 4, core: 2. Of those that a mesh axis runs over, the one named last changes fastest.
Arguments:
- layer_in: float32 [4096, 768], P(('dp', 'mp')), may hold values from -6 to 6
- node_counts: int32 [32], P('dp'), may hold values from 32 to 127, as said below
- spatial_ids: int32 [32, 128, 128], P('dp'), may hold values from 0 to 20
- path_ids: int32 [32, 5, 128, 128], P('dp'), may hold values from 0 to 1535
- ln1_gain: float32 [768], replicated, may hold values from 0.25 to 1.75
- ln1_bias: float32 [768], replicated, may hold values from -3 to 3
- w_q: bfloat16 [768, 768], P('dp', 'mp'), may hold values from -0.21875 to 0.21875
- w_k: bfloat16 [768, 768], P('dp', 'mp'), may hold values from -0.21875 to 0.21875
- w_v: bfloat16 [768, 768], P('dp', 'mp'), may hold values from -0.21875 to 0.21875
- q_bias: float32 [768], P('mp'), may hold values from -3 to 3
- v_bias: float32 [768], P('mp'), may hold values from -3 to 3
- spatial_table: bfloat16 [22, 32], replicated, may hold values from -4 to 4
- edge_table: bfloat16 [1536, 32], P('dp'), may hold values from -4 to 4
- w_o: bfloat16 [768, 768], P('dp', 'mp'), may hold values from -0.875 to 0.875
- o_bias: float32 [768], replicated, may hold values from -3 to 3
- ln2_gain: float32 [768], replicated, may hold values from 0.25 to 1.75
- ln2_bias: float32 [768], replicated, may hold values from -3 to 3
- w_in: bfloat16 [768, 768], P('dp', 'mp'), may hold values from -0.21875 to 0.21875
- in_bias: float32 [768], P('mp'), may hold values from -3 to 3
- w_out: bfloat16 [768, 768], P('dp', 'mp'), may hold values from -0.3125 to 0.3125
- out_bias: float32 [768], replicated, may hold values from -3 to 3
- cotangent: float32 [4096, 768], P(('dp', 'mp')), may hold values from -6 to 6
Outputs:
- layer_out: float32 [4096, 768], P(('dp', 'mp'))
- grad_layer_in: float32 [4096, 768], P(('dp', 'mp'))
- grad_ln1_gain: float32 [768], replicated
- grad_ln1_bias: float32 [768], replicated
- grad_w_q: float32 [768, 768], P('dp', 'mp')
- grad_w_k: float32 [768, 768], P('dp', 'mp')
- grad_w_v: float32 [768, 768], P('dp', 'mp')
- grad_q_bias: float32 [768], P('mp')
- grad_v_bias: float32 [768], P('mp')
- grad_spatial_table: float32 [22, 32], P(None, 'mp')
- grad_edge_table: float32 [1536, 32], P('dp', 'mp')
- grad_w_o: float32 [768, 768], P('dp', 'mp')
- grad_o_bias: float32 [768], replicated
- grad_ln2_gain: float32 [768], replicated
- grad_ln2_bias: float32 [768], replicated
- grad_w_in: float32 [768, 768], P('dp', 'mp')
- grad_in_bias: float32 [768], P('mp')
- grad_w_out: float32 [768, 768], P('dp', 'mp')
- grad_out_bias: float32 [768], replicated
The draws below stay inside these ranges and needn't reach their ends.
Inputs may be any that keep to these rules, and one draw needn't show every extreme that they name: Graph g holds its virtual node in slot 0 and its nodes in slots 1 to node_counts[g]; later slots are padding. `spatial_ids`: bucket 22 - 2 stands for unreachable pairs; bucket 22 - 1 is never given.
All inputs are finite; a program needn't handle non-finite values.
Results may differ from the reference program's by a relative error of at most 0.012.
Values may be sent and summed in bfloat16 or wider, within the bound.
No kernel may reach another device: no remote copies, remote signals or barrier semaphores. Data moves between devices by JAX's collectives and lax.ppermute only.
A program may use at most 64 MiB of HBM per device.

```python
import jax
import jax.numpy as jnp
from jax import lax

D = 768
HEADS = 32
HDIM = 24
FF = 768
EDGES = 1536
SPATIAL = 22
PATH = 5
SLOT = 128
GRAPHS = 32
TOKENS = 4096


def draw_node_counts(key, part):
    key = jax.random.fold_in(key, 7)
    first, second = jax.random.split(key)
    counts = jax.random.randint(first, (GRAPHS,), SLOT // 4, SLOT, dtype=jnp.int32)
    fullest = jax.random.randint(second, (), 0, GRAPHS, dtype=jnp.int32)
    places = jnp.arange(GRAPHS, dtype=jnp.int32)
    return jnp.where(places == fullest, SLOT - 1, counts).astype(jnp.int32)


def plant(entries, rng, low, largest):
    place = [jax.random.randint(jax.random.fold_in(rng, axis), (), 0, length) for axis, length in enumerate(entries.shape)]
    longest = entries.shape.index(max(entries.shape))
    next_to = place[:longest] + [(place[longest] + 1) % entries.shape[longest]] + place[longest + 1:]
    return entries.at[tuple(place)].set(low).at[tuple(next_to)].set(largest)


def levels(key, dims, cuts, low, top_value):
    level, own = 1.0, jax.random.fold_in(key, 6)
    for axis_at, parts in cuts:
        heights = jnp.exp(jax.random.uniform(jax.random.fold_in(own, axis_at), (parts,), jnp.float32, low / len(cuts), top_value / len(cuts)))
        level = level * jnp.repeat(heights, dims[axis_at] // parts).reshape([-1 if axis == axis_at else 1 for axis in range(len(dims))])
    return level


def scatter_about(own_key, shape, scale, most, cuts=(), held_as=jnp.bfloat16):
    values = jax.random.normal(own_key, shape, jnp.float32) * scale
    if len(cuts) > 0:
        values = levels(own_key, shape, cuts, -0.22, 0.18) * values
    return jnp.clip(values, min=-most, max=most).astype(held_as)


def setup_inputs(seed: int = 0) -> dict:
    arg_keys = jax.random.split(jax.random.key(seed), 23)
    layer_in = scatter_about(arg_keys[0], (TOKENS, D), 1.0, 6.0, ((0, 32),), jnp.float32)
    node_counts = draw_node_counts(jax.random.fold_in(arg_keys[22], 71), 0)
    spatial_ids = plant(jax.random.randint(arg_keys[2], (GRAPHS, SLOT, SLOT), 0, SPATIAL - 1), jax.random.fold_in(arg_keys[2], 1), 0, (SPATIAL - 1) - 1).astype(jnp.int32)
    path_ids = plant(jax.random.randint(arg_keys[3], (GRAPHS, PATH, SLOT, SLOT), 0, EDGES), jax.random.fold_in(arg_keys[3], 1), 0, EDGES - 1).astype(jnp.int32)
    ln1_gain = jnp.clip(1.0 + 0.15 * jax.random.normal(arg_keys[4], (D,), jnp.float32), 0.25, 1.75)
    ln1_bias = scatter_about(arg_keys[5], (D,), 0.5, 3.0, (), jnp.float32)
    w_q = scatter_about(arg_keys[6], (D, D), D ** -0.5, 0.21875, ((0, 8), (1, 4)))
    w_k = scatter_about(arg_keys[7], (D, D), D ** -0.5, 0.21875, ((0, 8), (1, 4)))
    w_v = scatter_about(arg_keys[8], (D, D), D ** -0.5, 0.21875, ((0, 8), (1, 4)))
    q_bias = scatter_about(arg_keys[9], (D,), 0.5, 3.0, ((0, 4),), jnp.float32)
    v_bias = scatter_about(arg_keys[10], (D,), 0.5, 3.0, ((0, 4),), jnp.float32)
    spatial_table = scatter_about(arg_keys[11], (SPATIAL, HEADS), 1.0, 4.0)
    edge_table = scatter_about(arg_keys[12], (EDGES, HEADS), 1.0, 4.0, ((0, 8),))
    w_o = scatter_about(arg_keys[13], (D, D), (D // 16) ** -0.5, 0.875, ((0, 8), (1, 4)))
    o_bias = scatter_about(arg_keys[14], (D,), 0.5, 3.0, (), jnp.float32)
    ln2_gain = jnp.clip(1.0 + 0.15 * jax.random.normal(arg_keys[15], (D,), jnp.float32), 0.25, 1.75)
    ln2_bias = scatter_about(arg_keys[16], (D,), 0.5, 3.0, (), jnp.float32)
    w_in = scatter_about(arg_keys[17], (D, FF), D ** -0.5, 0.21875, ((0, 8), (1, 4)))
    in_bias = scatter_about(arg_keys[18], (FF,), 0.5, 3.0, ((0, 4),), jnp.float32)
    w_out = scatter_about(arg_keys[19], (D, FF), (FF // 2) ** -0.5, 0.3125, ((0, 8), (1, 4)))
    out_bias = scatter_about(arg_keys[20], (D,), 0.5, 3.0, (), jnp.float32)
    cotangent = scatter_about(arg_keys[21], (TOKENS, D), 1.0, 6.0, ((0, 32),), jnp.float32)
    return {"layer_in": layer_in, "node_counts": node_counts, "spatial_ids": spatial_ids, "path_ids": path_ids, "ln1_gain": ln1_gain, "ln1_bias": ln1_bias, "w_q": w_q, "w_k": w_k, "w_v": w_v, "q_bias": q_bias, "v_bias": v_bias, "spatial_table": spatial_table, "edge_table": edge_table, "w_o": w_o, "o_bias": o_bias, "ln2_gain": ln2_gain, "ln2_bias": ln2_bias, "w_in": w_in, "in_bias": in_bias, "w_out": w_out, "out_bias": out_bias, "cotangent": cotangent}


highest = lax.Precision.HIGHEST

@jax.custom_vjp
def low(v):
    return lax.optimization_barrier(v.astype(jnp.bfloat16)).astype(jnp.float32)

@jax.custom_vjp
def low_back(v):
    return v

def low_keep(v):
    return (low(v), None)

def low_pass(kept, grad):
    return (grad,)

def back_keep(v):
    return (v, None)

def back_low(kept, grad):
    return (low(grad),)
low.defvjp(low_keep, low_pass)
low_back.defvjp(back_keep, back_low)

def layer_norm(values, gain, shift):
    centred = values - lax.optimization_barrier(jnp.mean(values, axis=-1, keepdims=True))
    normed = centred * lax.rsqrt(lax.optimization_barrier(jnp.mean(centred * centred, axis=-1, keepdims=True)) + 1e-05)
    return normed * gain + shift

def graph_attention(query, keys, values, spatial_g, path_g, count, table_spatial, table_edge):
    slots = query.shape[0]
    places = jnp.arange(slots, dtype=jnp.int32)
    virtual = (places[:, None] == 0) | (places[None, :] == 0)
    bucket = jnp.where(virtual, SPATIAL - 1, spatial_g).astype(jnp.int32)
    bias = jnp.take(table_spatial, bucket, axis=0) + lax.optimization_barrier(jnp.mean(jnp.take(table_edge, path_g, axis=0), axis=0))
    bias = jnp.transpose(bias, (2, 0, 1))
    scores = jnp.einsum('qhd,khd->hqk', query, keys, precision=highest) * HDIM ** (-0.5)
    scores = low_back(scores + bias)
    valid = places[None, None, :] <= count
    scores = jnp.where(valid, scores, -1e+30)
    top = lax.optimization_barrier(jnp.max(scores, axis=-1, keepdims=True))
    weights = jnp.exp(scores - top)
    probs = low(weights / lax.optimization_barrier(jnp.sum(weights, axis=-1, keepdims=True)))
    attended = jnp.einsum('hqk,khd->qhd', probs, values, precision=highest)
    return low(low_back(attended)).reshape(slots, HEADS * HDIM)

def reference(layer_in, node_counts, spatial_ids, path_ids, ln1_gain, ln1_bias, w_q, w_k, w_v, q_bias, v_bias, spatial_table, edge_table, w_o, o_bias, ln2_gain, ln2_bias, w_in, in_bias, w_out, out_bias, cotangent):
    split_shape = (GRAPHS, SLOT, HEADS, HDIM)
    per_graph = jax.checkpoint(graph_attention)

    def forward(inputs, first_gain, first_shift, weight_q, weight_k, weight_v, bias_q, bias_v, table_spatial, table_edge, weight_o, bias_o, second_gain, second_shift, weight_in, bias_in, weight_out, bias_out):
        h1 = low(layer_norm(inputs, first_gain, first_shift))
        query = low(low_back(jnp.dot(h1, weight_q, precision=highest) + bias_q))
        keys = low(low_back(jnp.dot(h1, weight_k, precision=highest)))
        values = low(low_back(jnp.dot(h1, weight_v, precision=highest) + bias_v))

        def one_graph(item):
            return per_graph(item[0], item[1], item[2], item[3], item[4], item[5], table_spatial, table_edge)
        attended = lax.map(one_graph, (query.reshape(split_shape), keys.reshape(split_shape), values.reshape(split_shape), spatial_ids, path_ids, node_counts))
        attended = attended.reshape(TOKENS, D)
        branch = low_back(jnp.dot(attended, weight_o.T, precision=highest))
        mid = inputs + branch + bias_o
        h2 = low(layer_norm(mid, second_gain, second_shift))
        pre = low_back(jnp.dot(h2, weight_in, precision=highest) + bias_in)
        hidden = low(jax.nn.gelu(pre, approximate=False))
        return mid + low_back(jnp.dot(hidden, weight_out.T, precision=highest)) + bias_out
    layer_out, pull = jax.vjp(forward, layer_in, ln1_gain, ln1_bias, w_q.astype(jnp.float32), w_k.astype(jnp.float32), w_v.astype(jnp.float32), q_bias, v_bias, spatial_table.astype(jnp.float32), edge_table.astype(jnp.float32), w_o.astype(jnp.float32), o_bias, ln2_gain, ln2_bias, w_in.astype(jnp.float32), in_bias, w_out.astype(jnp.float32), out_bias)
    grads = pull(cotangent)
    return (layer_out, grads[0], grads[1], grads[2], grads[3], grads[4], grads[5], grads[6], grads[7], grads[8], grads[9], grads[10], grads[11], grads[12], grads[13], grads[14], grads[15], grads[16], grads[17])
```

```python
import functools

import jax
import jax.numpy as jnp
from jax import lax
from jax.experimental import pallas as pl
from jax.experimental.pallas import tpu as pltpu
from jax.sharding import PartitionSpec as P

epsilon = 1e-05
masked_score = -1e30
edge_unit = 1638.0
spatial_unit = 4096.0
bf16 = jnp.bfloat16
f32 = jnp.float32
i32 = jnp.int32
vmem = pl.BlockSpec(memory_space=pltpu.VMEM)
smem = pl.BlockSpec(memory_space=pltpu.SMEM)
params = pltpu.CompilerParams(vmem_limit_bytes=48 << 20)


def normalize(values):
    centred = values - jnp.mean(values, axis=-1, keepdims=True)
    scale = lax.rsqrt(jnp.mean(centred * centred, axis=-1, keepdims=True) + epsilon)
    return (centred * scale, scale)


def normalize_back(grad_normed, normed, scale):
    inner = grad_normed - jnp.mean(grad_normed, axis=-1, keepdims=True)
    inner = inner - normed * jnp.mean(grad_normed * normed, axis=-1, keepdims=True)
    return inner * scale


def dot_nn(left, right):
    return lax.dot_general(
        left, right, (((1,), (0,)), ((), ())), preferred_element_type=f32
    )


def dot_nt(left, right):
    return lax.dot_general(
        left, right, (((1,), (1,)), ((), ())), preferred_element_type=f32
    )


def column_sum(values):
    return jnp.sum(values, axis=0, keepdims=True)


def shape(dims, kind):
    return jax.ShapeDtypeStruct(dims, kind)


def relative(place, side, which, step):
    z, x, y = place[0], place[1], place[2]
    flip_x = (0, 1 - side, side, 1)[which]
    flip_y = (0, side, 1 - side, 1)[which]
    row = (z ^ step) * 2 + (x ^ flip_x)
    column = (y ^ flip_y) * 2 + side
    return row, column


def pack_kernel(wq, wk, wv, wo, wi, wu, edge, first, second, table):
    first[...] = jnp.concatenate([wq[...], wk[...], wv[...], wo[...]], 1)
    second[...] = jnp.concatenate([wi[...], wu[...]], 1)
    table[...] = edge[...].astype(f32).T.astype(bf16)


def pack(wq, wk, wv, wo, wi, wu, edge):
    rows, width = wq.shape
    return pl.pallas_call(
        pack_kernel,
        out_shape=(
            shape((rows, 4 * width), bf16),
            shape((rows, 2 * width), bf16),
            shape((edge.shape[1], edge.shape[0]), bf16),
        ),
        in_specs=[vmem] * 7,
        out_specs=[vmem] * 3,
        compiler_params=params,
        name="pack",
    )(wq, wk, wv, wo, wi, wu, edge)


def prepare_kernel(virtual, place, spatial, path, layer_in, gain, bias, ids, buckets, h1, h1_t):
    slots = spatial.shape[1]
    for hop in range(path.shape[1]):
        ids[hop] = path[0, hop].T
    rows = lax.broadcasted_iota(i32, (slots, slots), 0)
    columns = lax.broadcasted_iota(i32, (slots, slots), 1)
    buckets[...] = jnp.where((rows == 0) | (columns == 0), virtual, spatial[0].T)
    normed, scale = normalize(layer_in[...])
    out = normed * gain[...] + bias[...]
    h1[...] = out.astype(bf16)
    h1_t[...] = out.T.astype(bf16)


def prepare(place, spatial, path, layer_in, gain, bias, virtual):
    hops, slots = path.shape[1], path.shape[2]
    rows, width = layer_in.shape
    whole = lambda dims: pl.BlockSpec(dims, lambda i, s: (0,) * len(dims))
    return pl.pallas_call(
        functools.partial(prepare_kernel, virtual),
        grid_spec=pltpu.PrefetchScalarGridSpec(
            num_scalar_prefetch=1,
            grid=(1,),
            in_specs=[
                pl.BlockSpec((1, slots, slots), lambda i, s: (s[4], 0, 0)),
                pl.BlockSpec((1, hops, slots, slots), lambda i, s: (s[4], 0, 0, 0)),
                whole((rows, width)),
                whole((1, width)),
                whole((1, width)),
            ],
            out_specs=[
                whole((hops, slots, slots)),
                whole((slots, slots)),
                whole((rows, width)),
                whole((width, rows)),
            ],
        ),
        out_shape=(
            shape((hops, slots, slots), i32),
            shape((slots, slots), i32),
            shape((rows, width), bf16),
            shape((width, rows), bf16),
        ),
        compiler_params=params,
        name="prepare",
    )(place, spatial, path, layer_in, gain, bias)


def quantize(table, unit):
    held = jnp.round(table.astype(f32) * unit).astype(i32)
    partner = jnp.concatenate([held[4:], held[:4]], 0)
    return held + partner * 65536


def lanes_gather(table, places):
    return jnp.take_along_axis(table, places, axis=1, mode="promise_in_bounds")


def lookup_kernel(first, step, share, place, chunk, ids, *refs):
    if first:
        total, table = refs
        previous = None
    else:
        previous, total, table = refs
    hops, slots = ids.shape[0], ids.shape[1]
    pairs = total.shape[0]
    heads = 2 * pairs
    rows = chunk.shape[1]
    packed = jnp.concatenate(
        [quantize(chunk[i * heads : (i + 1) * heads, :], edge_unit) for i in range(share // rows)], 1
    )
    blocks = share // 128
    for pair in range(pairs):
        head = (pair // 4) * 8 + pair % 4
        for block in range(blocks):
            table[pair, block] = jnp.broadcast_to(
                packed[head : head + 1, block * 128 : (block + 1) * 128], (8, 128)
            )
    base = (place[0] ^ step) * share

    def body(i, carry):
        offset = pl.multiple_of(i * 8, 8)
        sums = [None] * pairs
        if not first:
            sums = [previous[pair, pl.ds(offset, 8), :] for pair in range(pairs)]
        for hop in range(hops):
            relative_id = ids[hop, pl.ds(offset, 8), :] - base
            low = relative_id & 127
            high = relative_id >> 7
            masks = [high == block for block in range(blocks)]
            for pair in range(pairs):
                value = jnp.zeros((8, 128), i32)
                for block in range(blocks):
                    value = jnp.where(masks[block], lanes_gather(table[pair, block], low), value)
                sums[pair] = value if sums[pair] is None else sums[pair] + value
        for pair in range(pairs):
            total[pair, pl.ds(offset, 8), :] = sums[pair]
        return carry

    lax.fori_loop(0, slots // 8, body, 0)


def lookup(place, chunk, ids, previous, step, share):
    heads = chunk.shape[0] // (share // chunk.shape[1])
    pairs = heads // 2
    slots = ids.shape[1]
    first = previous is None
    out = shape((pairs, slots, slots), i32)
    return pl.pallas_call(
        functools.partial(lookup_kernel, first, step, share),
        out_shape=out,
        in_specs=[smem] + [vmem] * (2 if first else 3),
        out_specs=vmem,
        scratch_shapes=[pltpu.VMEM((pairs, share // 128, 8, 128), i32)],
        input_output_aliases={} if first else {3: 0},
        compiler_params=params,
        name="lookup",
    )(place, chunk, ids, *(() if first else (previous,)))


def assemble(place, parts, whole):
    if len(parts) == 1:
        whole[...] = parts[0][...]
        return
    core = place[3]
    rows = parts[0].shape[1]
    for other in range(2):
        for which in range(4):
            for step in range(4):
                row, column = relative(place, core ^ other, which, step)
                start = pl.multiple_of(row * rows, rows)
                whole[column, pl.ds(start, rows), :] = parts[other * 4 + which][step]


def head_masks(width, offset, depth):
    lanes = lax.broadcasted_iota(i32, (1, width), 1)
    out = []
    for head in range(8):
        start = offset + head * depth
        out.append(((lanes >= start) & (lanes < start + depth)).astype(f32).astype(bf16))
    return out


def attend_kernel(
    n_parts, place, counts, h1, biases, edge_sums, buckets, spatial_table, layer_in, o_bias, gain, bias, *refs
):
    parts = refs[:n_parts]
    weights, transposed, value_win, probs_out, att_low, att_high, mid, h2 = refs[n_parts:]
    assemble(place, parts, weights)
    slots = h1.shape[0]
    width = biases.shape[2]
    depth = width // 8
    pad = 256 - width
    hops = 5
    count = counts[place[4]]
    packed = quantize(spatial_table[...].astype(f32).T, spatial_unit)
    packed = jnp.concatenate([packed, jnp.zeros((packed.shape[0], 128 - packed.shape[1]), i32)], 1)
    rows_of = lax.broadcasted_iota(i32, (slots, slots), 0)
    hidden_key = rows_of > count
    bucket = buckets[...]
    key_masks = head_masks(256, pad, depth)
    mid[...] = layer_in[...] + o_bias[...]
    groups = biases.shape[0]
    for group in range(groups):
        natural = dot_nn(h1[...], weights[group, :, : 3 * width + pad])
        row_bias = jnp.concatenate(
            [
                biases[group, 0:1, :],
                jnp.zeros((1, width), f32),
                biases[group, 1:2, :],
                jnp.zeros((1, pad), f32),
            ],
            1,
        )
        natural = natural + row_bias
        natural_t = natural.T
        transposed[group] = natural_t[: 3 * width].astype(bf16)
        natural = natural.astype(bf16)
        value_win[group] = natural[:, 2 * width : 2 * width + 256]
        keys = natural[:, width - pad : 2 * width]
        stack = jnp.concatenate([keys * mask for mask in key_masks], 0)
        query = jnp.concatenate([jnp.zeros((pad, slots), f32), natural_t[:width]], 0).astype(bf16)
        scores = dot_nn(stack, query) * depth ** (-0.5)
        out = []
        for pair in range(4):
            word = edge_sums[group * 4 + pair]
            head = group * 8 + pair
            spatial_word = lanes_gather(
                jnp.broadcast_to(packed[head : head + 1], (slots, 128)), bucket
            )
            low = (word << 16) >> 16
            spatial_low = (spatial_word << 16) >> 16
            high = (word - low) >> 16
            spatial_high = (spatial_word - spatial_low) >> 16
            for part, spatial_part, place_in in ((low, spatial_low, pair), (high, spatial_high, pair + 4)):
                pair_bias = part.astype(f32) * (1.0 / (edge_unit * hops))
                pair_bias = pair_bias + spatial_part.astype(f32) * (1.0 / spatial_unit)
                score = scores[place_in * slots : (place_in + 1) * slots] + pair_bias
                score = jnp.where(hidden_key, masked_score, score)
                weight = jnp.exp(score - jnp.max(score, axis=0, keepdims=True))
                probs = weight * (1.0 / column_sum(weight))
                probs_out[group * 8 + place_in] = probs
                values = natural_t[2 * width + place_in * depth : 2 * width + (place_in + 1) * depth]
                out.append((place_in, dot_nn(values.astype(bf16), probs.astype(bf16))))
        out = [item[1] for item in sorted(out, key=lambda item: item[0])]
        gap = jnp.zeros((pad, slots), f32)
        att_low[group] = jnp.concatenate(out + [gap], 0).T.astype(bf16)
        high_form = jnp.concatenate([gap] + out, 0).T.astype(bf16)
        att_high[group] = high_form
        mid[...] += dot_nt(high_form, weights[group, :, 3 * width - pad : 4 * width])
    normed, scale = normalize(mid[...])
    h2[...] = (normed * gain[...] + bias[...]).astype(bf16)


def attend(place, counts, h1, biases, edge_sums, buckets, spatial_table, layer_in, o_bias, gain, bias, parts):
    slots, features = h1.shape
    groups, width = biases.shape[0], biases.shape[2]
    heads = groups * 8
    return pl.pallas_call(
        functools.partial(attend_kernel, len(parts)),
        out_shape=(
            shape((groups, features, 4 * width), bf16),
            shape((groups, 3 * width, slots), bf16),
            shape((groups, slots, 256), bf16),
            shape((heads, slots, slots), f32),
            shape((groups, slots, 256), bf16),
            shape((groups, slots, 256), bf16),
            shape((slots, features), f32),
            shape((slots, features), bf16),
        ),
        in_specs=[smem, smem] + [vmem] * (9 + len(parts)),
        out_specs=[vmem] * 8,
        compiler_params=params,
        name="attend",
    )(place, counts, h1, biases, edge_sums, buckets, spatial_table, layer_in, o_bias, gain, bias, *parts)


def feed_kernel(
    n_parts, place, mid, h2, weights_a, biases, out_bias, gain, cotangent, att_low, *refs
):
    parts = refs[:n_parts]
    layer_out, grad_mid, grad_att_t, columns, rows_t, sums, weights = refs[n_parts:]
    assemble(place, parts, weights)
    slots, features = mid.shape
    groups, width = biases.shape[0], biases.shape[2]
    pad = 256 - width
    lanes = lax.broadcasted_iota(i32, (1, 256), 1)
    cot = cotangent[...]
    grad_ffn = cot.astype(bf16)
    h2_value = h2[...]
    layer_out[...] = mid[...] + out_bias[...]
    grad_h2 = jnp.zeros((slots, features), f32)
    sums[...] = jnp.zeros_like(sums)
    for group in range(groups):
        in_bias = jnp.concatenate([biases[group, 2:3, :], jnp.zeros((1, pad), f32)], 1)
        pre = dot_nn(h2_value, weights[group, :, :256]) + in_bias
        cdf = 0.5 * (1.0 + lax.erf(pre * (0.5**0.5)))
        slope = cdf + pre * jnp.exp(-0.5 * pre * pre) * 0.3989422804014327
        hidden = pltpu.roll(pre * cdf, pad, 1)
        hidden = jnp.where(lanes >= pad, hidden, 0.0).astype(bf16)
        layer_out[...] += dot_nt(hidden, weights[group, :, width - pad : 2 * width])
        grad_hidden = dot_nn(grad_ffn, weights[group, :, width - pad : 2 * width])
        grad_hidden = pltpu.roll(grad_hidden, width, 1)
        grad_pre = jnp.where(lanes < width, grad_hidden * slope, 0.0).astype(bf16)
        grad_h2 = grad_h2 + dot_nt(grad_pre, weights[group, :, :256])
        columns[group, :, 0:256] = grad_pre
        columns[group, :, 256:512] = hidden
        columns[group, :, 512:768] = att_low[group]
        sums[12 + group : 13 + group, 0:256] = column_sum(grad_pre.astype(f32))
    normed, scale = normalize(mid[...])
    grad = cot + normalize_back(grad_h2 * gain[...], normed, scale)
    grad_mid[...] = grad
    branch = grad.astype(bf16)
    sums[2:3, :] = column_sum(grad)
    sums[3:4, :] = column_sum(grad_h2 * normed)
    sums[4:5, :] = column_sum(grad_h2)
    sums[5:6, :] = column_sum(cot)
    rows_t[0] = h2_value.astype(f32).T.astype(bf16)
    rows_t[1] = cot.T.astype(bf16)
    rows_t[2] = grad.T.astype(bf16)
    for group in range(groups):
        grad_att = dot_nn(branch, weights_a[group]).T
        grad_att = jnp.concatenate([grad_att[pad:], jnp.zeros((pad, slots), f32)], 0)
        grad_att_t[group] = grad_att.astype(bf16)


def feed(place, mid, h2, weights_a, biases, out_bias, gain, cotangent, att_low, parts):
    slots, features = mid.shape
    groups, width = biases.shape[0], biases.shape[2]
    whole = lambda dims: pl.BlockSpec(dims, lambda i: (0,) * len(dims))
    return pl.pallas_call(
        functools.partial(feed_kernel, len(parts)),
        grid=(1,),
        out_shape=(
            shape((slots, features), f32),
            shape((slots, features), f32),
            shape((groups, 256, slots), bf16),
            shape((groups, slots, 768), bf16),
            shape((3, features, slots), bf16),
            shape((16, features), f32),
        ),
        in_specs=[
            smem,
            whole(mid.shape),
            whole(h2.shape),
            pl.BlockSpec((groups, features, 256), lambda i: (0, 0, 2)),
            whole(biases.shape),
            whole(out_bias.shape),
            whole(gain.shape),
            whole(cotangent.shape),
            whole(att_low.shape),
        ]
        + [whole(part.shape) for part in parts],
        out_specs=[
            whole((slots, features)),
            whole((slots, features)),
            whole((groups, 256, slots)),
            whole((groups, slots, 768)),
            whole((3, features, slots)),
            whole((16, features)),
        ],
        scratch_shapes=[pltpu.VMEM((groups, features, 2 * width), bf16)],
        compiler_params=params,
        name="feed",
    )(place, mid, h2, weights_a, biases, out_bias, gain, cotangent, att_low, *parts)


def attend_back_kernel(
    probs_in, value_win, transposed, grad_att_t, weights, layer_in, gain, grad_mid, sums_in,
    score_grads, columns, grad_in, sums,
):
    slots, features = layer_in.shape
    groups = transposed.shape[0]
    width = transposed.shape[1] // 3
    depth = width // 8
    pad = 256 - width
    value_masks = head_masks(256, 0, depth)
    grad_h1 = jnp.zeros((slots, features), f32)
    sums[...] = sums_in[...]
    scale = depth ** (-0.5)
    for group in range(groups):
        values = value_win[group]
        stack = jnp.concatenate([values * mask for mask in value_masks], 0)
        grad_att = grad_att_t[group]
        grad_probs = dot_nn(stack, grad_att)
        grad_att = grad_att.astype(f32)
        held = transposed[group].astype(f32)
        query_out, key_out, value_out, score_out = [], [], [], []
        for head in range(8):
            probs = probs_in[group * 8 + head]
            part = probs * grad_probs[head * slots : (head + 1) * slots]
            grads = (part - probs * column_sum(part)).astype(bf16)
            score_out.append(grads)
            cut = slice(head * depth, (head + 1) * depth)
            value_out.append(dot_nt(grad_att[cut].astype(bf16), probs.astype(bf16)))
            key_rows = held[width + head * depth : width + (head + 1) * depth]
            query_out.append(dot_nn(key_rows.astype(bf16), grads) * scale)
            key_out.append(dot_nt(held[cut].astype(bf16), grads) * scale)
        score_grads[:, group * 8 : (group + 1) * 8, :] = jnp.swapaxes(
            jnp.stack([g.astype(f32) for g in score_out]), 0, 1
        ).astype(bf16)
        gap = jnp.zeros((pad, slots), f32)
        natural = jnp.concatenate(query_out + key_out + value_out + [gap], 0).T.astype(bf16)
        columns[group] = natural
        grad_h1 = grad_h1 + dot_nt(natural, weights[group, :, : 3 * width + pad])
        sums[8 + group : 9 + group, 0 : 3 * width + pad] = column_sum(natural.astype(f32))
    normed, inverse = normalize(layer_in[...])
    grad_in[...] = grad_mid[...] + normalize_back(grad_h1 * gain[...], normed, inverse)
    sums[0:1, :] = column_sum(grad_h1 * normed)
    sums[1:2, :] = column_sum(grad_h1)


def attend_back(probs, value_win, transposed, grad_att_t, weights, layer_in, gain, grad_mid, sums):
    slots, features = layer_in.shape
    groups = transposed.shape[0]
    width = transposed.shape[1] // 3
    return pl.pallas_call(
        attend_back_kernel,
        out_shape=(
            shape((slots, groups * 8, slots), bf16),
            shape((groups, slots, 2 * width + 256), bf16),
            shape((slots, features), f32),
            shape(sums.shape, f32),
        ),
        in_specs=[vmem] * 9,
        out_specs=[vmem] * 4,
        compiler_params=params,
        name="attend_back",
    )(probs, value_win, transposed, grad_att_t, weights, layer_in, gain, grad_mid, sums)


def weight_grads_kernel(plan, place, rows_own, rows_other, columns_own, columns_other, own, across, over, both, rows_t):
    kinds = rows_own.shape[0]
    slots = rows_own.shape[2]
    for kind in range(kinds):
        rows_t[kind, :, 0:slots] = rows_own[kind]
        rows_t[kind, :, slots : 2 * slots] = rows_other[kind]
    core = place[3]
    height = own.shape[1]
    for which, out in ((3, both), (2, over), (1, across), (0, own)):
        column = relative(place, core, which, 0)[1]
        right = jnp.concatenate([columns_own[column], columns_other[column]], 0)
        for step in range(4):
            row = relative(place, core, which, step)[0]
            start = pl.multiple_of(row * height, height)
            out[step] = plan(lambda kind: rows_t[kind, pl.ds(start, height), :], right).astype(bf16)


def plan_first(rows_of, right):
    return dot_nn(rows_of(0), right)


def plan_second(rows_of, right):
    grad_in = dot_nn(rows_of(0), right[:, 0:256])
    grad_out = dot_nn(rows_of(1), right[:, 256:512])
    grad_o = dot_nn(rows_of(2), right[:, 512:768])
    return jnp.concatenate(
        [grad_in[:, :128], grad_in[:, 128:] + grad_out[:, :128], grad_out[:, 128:], grad_o], 1
    )


def weight_grads(plan, place, rows_own, rows_other, columns_own, columns_other, height):
    kinds, features, slots = rows_own.shape
    out = shape((4, height, 640), bf16)
    return pl.pallas_call(
        functools.partial(weight_grads_kernel, plan),
        out_shape=(out,) * 4,
        in_specs=[smem] + [vmem] * 4,
        out_specs=[vmem] * 4,
        scratch_shapes=[pltpu.VMEM((kinds, features, 2 * slots), bf16)],
        compiler_params=params,
        name="weight_grads",
    )(place, rows_own, rows_other, columns_own, columns_other)


def table_kernel(digit, staged, span, place, grads, ids, buckets, *refs):
    if staged:
        mine, partner, spatial, total = refs
    else:
        total, spatial = refs
    hops = ids.shape[0]
    heads = grads.shape[1]
    high_count = total.shape[0] // heads
    total[...] = jnp.zeros_like(total)
    spatial[...] = jnp.zeros_like(spatial)
    digits = lax.broadcasted_iota(i32, (digit, 128), 0).astype(f32).astype(bf16)
    kinds = lax.broadcasted_iota(i32, (heads, 128), 0).astype(f32).astype(bf16)
    one = jnp.ones((), bf16)
    zero = jnp.zeros((), bf16)

    def body(i, carry):
        lefts, rights, plain, kind_rights = [], [], [], []
        for j in range(span):
            row = i * span + j
            piece = grads[row]
            bucket = buckets[pl.ds(row, 1), :].astype(f32).astype(bf16)
            plain.append(piece)
            kind_rights.append(jnp.where(jnp.broadcast_to(bucket, (heads, 128)) == kinds, one, zero))
            for hop in range(hops):
                value = ids[hop, pl.ds(row, 1), :].astype(f32)
                high = jnp.floor((value + 0.5) * (1.0 / digit))
                low = value - high * digit
                low = jnp.broadcast_to(low.astype(bf16), (digit, 128))
                high = jnp.broadcast_to(high.astype(bf16), (heads, 128))
                rights.append(jnp.where(low == digits, one, zero))
                lefts.append(
                    jnp.concatenate(
                        [jnp.where(high == jnp.full((), k, bf16), piece, zero) for k in range(high_count)], 0
                    )
                )
        total[...] += dot_nt(jnp.concatenate(lefts, 1), jnp.concatenate(rights, 1))
        spatial[...] += dot_nt(jnp.concatenate(plain, 1), jnp.concatenate(kind_rights, 1))
        return carry

    lax.fori_loop(0, grads.shape[0] // span, body, 0)
    if staged:
        core = place[3]
        for other, out in ((0, mine), (1, partner)):
            for which in range(4):
                for step in range(4):
                    row, column = relative(place, core ^ other, which, step)
                    start = pl.multiple_of(row * heads + column * 8, 8)
                    out[which, step] = total[pl.ds(start, 8), :] * (1.0 / hops)


def table_grads(place, grads, ids, buckets, digit, edges, staged):
    heads = grads.shape[1]
    high_count = edges // digit
    total = (high_count * heads, digit)
    block = shape((4, 4, 8, digit), f32)
    spatial = shape((heads, heads), f32)
    return pl.pallas_call(
        functools.partial(table_kernel, digit, staged, 8),
        out_shape=(block, block, spatial) if staged else (shape(total, f32), spatial),
        in_specs=[smem] + [vmem] * 3,
        out_specs=[vmem] * (3 if staged else 2),
        scratch_shapes=[pltpu.VMEM(total, f32)] if staged else [],
        compiler_params=params,
        name="table_grads",
    )(place, grads, ids, buckets)


class Links:
    def __init__(self):
        self.core = self.hop(lambda z, x, y, c: (z, x, y, 1 - c))
        self.first = self.hop(lambda z, x, y, c: (z, x, 1 - y, c) if c else (z, 1 - x, y, c))
        self.second = self.hop(lambda z, x, y, c: (z, 1 - x, y, c) if c else (z, x, 1 - y, c))
        self.along_x = self.hop(lambda z, x, y, c: (z, 1 - x, y, c))
        self.along_z = [self.hop(lambda z, x, y, c, k=k: (z ^ k, x, y, c)) for k in (1, 2, 3)]

    def hop(self, move):
        index = lambda z, x, y, c: (z * 2 + x) * 4 + y * 2 + c
        spots = [(z, x, y, c) for z in range(4) for x in range(2) for y in range(2) for c in range(2)]
        return [(index(*spot), index(*move(*spot))) for spot in spots]


def send(values, hop):
    return lax.ppermute(values, ("dp", "mp"), hop)


def gather_staged(links, own):
    stack = jnp.stack([own] + [send(own, hop) for hop in links.along_z])
    across = send(stack, links.first)
    over = send(stack, links.second)
    both = send(across, links.second)
    mine = (stack, across, over, both)
    return mine + tuple(send(part, links.core) for part in mine)


def add_rounded(*terms):
    total = terms[0].astype(f32)
    for term in terms[1:]:
        total = total + term.astype(f32)
    return total.astype(bf16)


def reduce_staged(links, own, across, over, both):
    across = add_rounded(across, send(both, links.second))
    own = add_rounded(own, send(over, links.second), send(across, links.first))
    total = own[0].astype(f32)
    for step, hop in enumerate(links.along_z):
        total = total + send(own[step + 1], hop).astype(f32)
    return total


def local(
    layer_in,
    node_counts,
    spatial_ids,
    path_ids,
    ln1_gain,
    ln1_bias,
    w_q,
    w_k,
    w_v,
    q_bias,
    v_bias,
    spatial_table,
    edge_table,
    w_o,
    o_bias,
    ln2_gain,
    ln2_bias,
    w_in,
    in_bias,
    w_out,
    out_bias,
    cotangent,
):
    dp_size, mp_size = lax.axis_size("dp"), lax.axis_size("mp")
    dp_index, mp_index = lax.axis_index("dp"), lax.axis_index("mp")
    staged = dp_size == 8 and mp_size == 4
    features = layer_in.shape[1]
    width = w_q.shape[1]
    height = w_q.shape[0]
    edges = edge_table.shape[0] * dp_size
    heads = spatial_table.shape[1]
    kinds = spatial_table.shape[0]
    hops = path_ids.shape[1]
    share = edges // 4
    digit = edges // 8
    place = jnp.stack([dp_index // 2, dp_index % 2, mp_index // 2, mp_index % 2, mp_index]).astype(i32)
    row = lambda v: v.reshape(1, features)

    biases = lax.all_gather(jnp.stack([q_bias, v_bias, in_bias]), "mp", axis=0, tiled=False)
    ids, buckets, h1, h1_t = prepare(
        place, spatial_ids, path_ids, layer_in, row(ln1_gain), row(ln1_bias), kinds - 1
    )
    if staged:
        links = Links()
        first, second, table_t = pack(w_q, w_k, w_v, w_o, w_in, w_out, edge_table)
        neighbour = send(table_t, links.along_x)
        even = dp_index % 2 == 0
        pair = jnp.concatenate(
            [jnp.where(even, table_t, neighbour), jnp.where(even, neighbour, table_t)], 0
        )
        chunks = [pair] + [send(pair, hop) for hop in links.along_z]
        parts_a = gather_staged(links, first)
        parts_b = gather_staged(links, second)
        lookup_place = place
    else:
        gathered = [
            lax.all_gather(lax.all_gather(w, "dp", axis=0, tiled=True), "mp", axis=0)
            for w in (w_q, w_k, w_v, w_o, w_in, w_out)
        ]
        parts_a = (jnp.concatenate(gathered[:4], 2),)
        parts_b = (jnp.concatenate(gathered[4:], 2),)
        table_t = lax.all_gather(edge_table, "dp", axis=0, tiled=True).T
        chunks = [table_t[:, i * share : (i + 1) * share] for i in range(4)]
        lookup_place = jnp.zeros((5,), i32)
    edge_sums = None
    for step in range(4):
        edge_sums = lookup(lookup_place, chunks[step], ids, edge_sums, step, share)

    weights, transposed, value_win, probs, att_low, att_high, mid, h2 = attend(
        place, node_counts, h1, biases, edge_sums, buckets, spatial_table,
        layer_in, row(o_bias), row(ln2_gain), row(ln2_bias), parts_a,
    )
    layer_out, grad_mid, grad_att_t, columns_b, rows_b, sums = feed(
        place, mid, h2, weights, biases, row(out_bias), row(ln2_gain), cotangent, att_low, parts_b
    )
    rows_a = h1_t.reshape(1, *h1_t.shape)
    if staged:
        other_rows_b = send(rows_b, links.core)
        other_columns_b = send(columns_b, links.core)
        other_rows_a = send(rows_a, links.core)
        pieces_b = weight_grads(
            plan_second, place, rows_b, other_rows_b, columns_b, other_columns_b, height
        )
        grads_b = reduce_staged(links, *pieces_b)
    score_grads, columns_a, grad_layer_in, sums = attend_back(
        probs, value_win, transposed, grad_att_t, weights, layer_in, row(ln1_gain), grad_mid, sums
    )
    if staged:
        other_columns_a = send(columns_a, links.core)
        pieces_a = weight_grads(
            plan_first, place, rows_a, other_rows_a, columns_a, other_columns_a, height
        )
        grads_a = reduce_staged(links, *pieces_a)
        mine, partner, spatial = table_grads(place, score_grads, ids, buckets, digit, edges, True)
        small = jnp.concatenate(
            [
                sums.reshape(-1, digit),
                jnp.pad(spatial, ((0, 0), (0, digit - heads))),
            ],
            0,
        )
        n_small = small.shape[0]
        flat = lambda a: a.reshape(-1, digit)
        got = send(jnp.concatenate([flat(partner), small], 0), links.core)
        table = mine + got[:-n_small].reshape(mine.shape)
        small = small + got[-n_small:]
        got = send(jnp.concatenate([flat(table[2:4]), small], 0), links.second)
        blocks = got[:-n_small].reshape(2, *mine.shape[1:])
        across = table[1] + blocks[1]
        small = small + got[-n_small:]
        got = send(jnp.concatenate([flat(across), small], 0), links.first)
        own = table[0] + blocks[0] + got[:-n_small].reshape(mine.shape[1:])
        small = small + got[-n_small:]
        grad_edge, total = own[0], small
        for step, hop in enumerate(links.along_z):
            got = send(jnp.concatenate([own[step + 1], small], 0), hop)
            grad_edge = grad_edge + got[: own.shape[1]]
            total = total + got[own.shape[1] :]
        grad_edge = grad_edge.T
        spatial = total[-heads:, :kinds]
        totals = total[:-heads].reshape(sums.shape)
        grad_w_q, grad_w_k, grad_w_v = (grads_a[:, i * width : (i + 1) * width] for i in range(3))
        grad_w_in, grad_w_out, grad_w_o = (grads_b[:, i * width : (i + 1) * width] for i in range(3))
    else:
        contract = lambda a, b: lax.dot_general(
            a, b, (((1,), (1,)), ((), ())), preferred_element_type=f32
        )

        def scatter(rows_t, columns):
            grads = contract(rows_t, columns)
            grads = jnp.transpose(grads, (1, 0, 2))
            grads = lax.psum_scatter(grads, "mp", scatter_dimension=0, tiled=False)
            return lax.psum_scatter(grads, "dp", scatter_dimension=0, tiled=True)

        grad_w_q, grad_w_k, grad_w_v = (
            scatter(h1_t, columns_a[:, :, i * width : (i + 1) * width]) for i in range(3)
        )
        grad_w_in = scatter(rows_b[0], columns_b[:, :, :width])
        grad_w_out = scatter(rows_b[1], columns_b[:, :, 512 - width : 512])
        grad_w_o = scatter(rows_b[2], columns_b[:, :, 512 : 512 + width])
        table, spatial = table_grads(place, score_grads, ids, buckets, digit, edges, False)
        table = table.reshape(-1, heads, digit).transpose(0, 2, 1).reshape(edges, heads) / hops
        table = lax.psum_scatter(table, "dp", scatter_dimension=0, tiled=True)
        table = lax.psum(table, "mp")
        grad_edge = lax.dynamic_slice_in_dim(table, mp_index * 8, 8, 1)
        totals, spatial = lax.psum((sums, spatial), ("dp", "mp"))
        spatial = spatial[:, :kinds]
    grad_spatial = lax.dynamic_slice_in_dim(spatial, mp_index * 8, 8, 0).T
    head_sums = lax.dynamic_slice_in_dim(totals, 8 + mp_index, 1, 0)[0]
    hidden_sums = lax.dynamic_slice_in_dim(totals, 12 + mp_index, 1, 0)[0]
    return (
        layer_out,
        grad_layer_in,
        totals[0],
        totals[1],
        grad_w_q,
        grad_w_k,
        grad_w_v,
        head_sums[:width],
        head_sums[2 * width : 3 * width],
        grad_spatial,
        grad_edge,
        grad_w_o,
        totals[2],
        totals[3],
        totals[4],
        grad_w_in,
        hidden_sums[:width],
        grad_w_out,
        totals[5],
    )


def solution(mesh):
    return jax.shard_map(
        local,
        mesh=mesh,
        in_specs=(
            P(("dp", "mp"), None),
            P("dp"),
            P("dp", None, None),
            P("dp", None, None, None),
            P(),
            P(),
            P("dp", "mp"),
            P("dp", "mp"),
            P("dp", "mp"),
            P("mp"),
            P("mp"),
            P(),
            P("dp", None),
            P("dp", "mp"),
            P(),
            P(),
            P(),
            P("dp", "mp"),
            P("mp"),
            P("dp", "mp"),
            P(),
            P(("dp", "mp"), None),
        ),
        out_specs=(
            P(("dp", "mp"), None),
            P(("dp", "mp"), None),
            P(),
            P(),
            P("dp", "mp"),
            P("dp", "mp"),
            P("dp", "mp"),
            P("mp"),
            P("mp"),
            P(None, "mp"),
            P("dp", "mp"),
            P("dp", "mp"),
            P(),
            P(),
            P(),
            P("dp", "mp"),
            P("mp"),
            P("dp", "mp"),
            P(),
        ),
        check_vma=False,
    )
```

```python
import functools

import jax
import jax.numpy as jnp
from jax import lax
from jax.experimental import pallas as pl
from jax.experimental.pallas import tpu as pltpu
from jax.sharding import PartitionSpec as P

epsilon = 1e-05
masked_score = -1e30
edge_unit = 1638.0
spatial_unit = 4096.0
bf16 = jnp.bfloat16
f32 = jnp.float32
i32 = jnp.int32
vmem = pl.BlockSpec(memory_space=pltpu.VMEM)
smem = pl.BlockSpec(memory_space=pltpu.SMEM)
hbm = pl.BlockSpec(memory_space=pltpu.HBM)
untouched = pl.BlockSpec(memory_space=pl.ANY)


def params(mebibytes):
    return pltpu.CompilerParams(vmem_limit_bytes=mebibytes << 20)


def normalize(values):
    centred = values - jnp.mean(values, axis=-1, keepdims=True)
    scale = lax.rsqrt(jnp.mean(centred * centred, axis=-1, keepdims=True) + epsilon)
    return (centred * scale, scale)


def normalize_back(grad_normed, normed, scale):
    inner = grad_normed - jnp.mean(grad_normed, axis=-1, keepdims=True)
    inner = inner - normed * jnp.mean(grad_normed * normed, axis=-1, keepdims=True)
    return inner * scale


def dot_nn(left, right):
    return lax.dot_general(
        left, right, (((1,), (0,)), ((), ())), preferred_element_type=f32
    )


def dot_nt(left, right):
    return lax.dot_general(
        left, right, (((1,), (1,)), ((), ())), preferred_element_type=f32
    )


def column_sum(values):
    return jnp.sum(values, axis=0, keepdims=True)


def cost(microseconds):
    return pl.CostEstimate(flops=int(microseconds * 1.15e9), bytes_accessed=1024, transcendentals=0)


def as_row(ref):
    return ref[...].reshape(1, -1)


def shape(dims, kind):
    return jax.ShapeDtypeStruct(dims, kind)


def relative(place, side, which, step):
    z, x, y = place[0], place[1], place[2]
    flip_x = (0, 1 - side, side, 1)[which]
    flip_y = (0, side, 1 - side, 1)[which]
    row = (z ^ step) * 2 + (x ^ flip_x)
    column = (y ^ flip_y) * 2 + side
    return row, column


def pack_kernel(wq, wk, wv, wo, wi, wu, bq, bv, bi, first, second, biases, held, sems):
    copies = [
        pltpu.make_async_copy(source, held.at[i], sems.at[i])
        for i, source in enumerate((wq, wk, wv, wo, wi, wu))
    ]
    for copy in copies:
        copy.start()
    for i, bias in enumerate((bq, bv, bi)):
        biases[i : i + 1, :] = as_row(bias)
    for copy in copies:
        copy.wait()
    first[...] = jnp.concatenate([held[i] for i in range(4)], 1)
    second[...] = jnp.concatenate([held[4], held[5]], 1)


def pack(wq, wk, wv, wo, wi, wu, bq, bv, bi):
    rows, width = wq.shape
    return pl.pallas_call(
        pack_kernel,
        out_shape=(
            shape((rows, 4 * width), bf16),
            shape((rows, 2 * width), bf16),
            shape((3, width), f32),
        ),
        in_specs=[hbm] * 6 + [vmem] * 3,
        out_specs=[vmem] * 3,
        scratch_shapes=[pltpu.VMEM((6, rows, width), bf16), pltpu.SemaphoreType.DMA((6,))],
        compiler_params=params(4),
        cost_estimate=cost(1),
        name="pack",
    )(wq, wk, wv, wo, wi, wu, bq, bv, bi)


def prepare_kernel(virtual, place, spatial, path, layer_in, gain, bias, cotangent, ids, buckets, h1, rows_t):
    slots = spatial.shape[1]
    for hop in range(path.shape[1]):
        ids[hop] = path[0, hop].T
    rows = lax.broadcasted_iota(i32, (slots, slots), 0)
    columns = lax.broadcasted_iota(i32, (slots, slots), 1)
    buckets[...] = jnp.where((rows == 0) | (columns == 0), virtual, spatial[0].T)
    normed, scale = normalize(layer_in[...])
    out = normed * as_row(gain) + as_row(bias)
    h1[...] = out.astype(bf16)
    rows_t[0] = out.T.astype(bf16)
    rows_t[1] = cotangent[...].T.astype(bf16)


def prepare(place, spatial, path, layer_in, gain, bias, cotangent, virtual):
    hops, slots = path.shape[1], path.shape[2]
    rows, width = layer_in.shape
    whole = lambda dims: pl.BlockSpec(dims, lambda i, s: (0,) * len(dims))
    return pl.pallas_call(
        functools.partial(prepare_kernel, virtual),
        grid_spec=pltpu.PrefetchScalarGridSpec(
            num_scalar_prefetch=1,
            grid=(1,),
            in_specs=[
                pl.BlockSpec((1, slots, slots), lambda i, s: (s[4], 0, 0)),
                pl.BlockSpec((1, hops, slots, slots), lambda i, s: (s[4], 0, 0, 0)),
                whole((rows, width)),
                whole((width,)),
                whole((width,)),
                whole((rows, width)),
            ],
            out_specs=[
                whole((hops, slots, slots)),
                whole((slots, slots)),
                whole((rows, width)),
                whole((2, width, rows)),
            ],
        ),
        out_shape=(
            shape((hops, slots, slots), i32),
            shape((slots, slots), i32),
            shape((rows, width), bf16),
            shape((2, width, rows), bf16),
        ),
        compiler_params=params(8),
        cost_estimate=cost(1),
        name="prepare",
    )(place, spatial, path, layer_in, gain, bias, cotangent)


def quantize(table, unit):
    held = jnp.round(table.astype(f32) * unit).astype(i32)
    partner = jnp.concatenate([held[4:], held[:4]], 0)
    return held + partner * 65536


def lanes_gather(table, places):
    return jnp.take_along_axis(table, places, axis=1, mode="promise_in_bounds")


def lookup_kernel(first, step, share, place, chunk, ids, *refs):
    if first:
        total, table = refs
        previous = None
    else:
        previous, total, table = refs
    hops, slots = ids.shape[0], ids.shape[1]
    pairs = total.shape[0]
    heads = 2 * pairs
    rows = chunk.shape[1]
    packed = jnp.concatenate(
        [quantize(chunk[i * heads : (i + 1) * heads, :], edge_unit) for i in range(share // rows)], 1
    )
    blocks = share // 128
    for pair in range(pairs):
        head = (pair // 4) * 8 + pair % 4
        for block in range(blocks):
            table[pair, block] = jnp.broadcast_to(
                packed[head : head + 1, block * 128 : (block + 1) * 128], (8, 128)
            )
    base = (place[0] ^ step) * share

    def body(i, carry):
        offset = pl.multiple_of(i * 8, 8)
        sums = [None] * pairs
        if not first:
            sums = [previous[pair, pl.ds(offset, 8), :] for pair in range(pairs)]
        for hop in range(hops):
            relative_id = ids[hop, pl.ds(offset, 8), :] - base
            low = relative_id & 127
            high = relative_id >> 7
            masks = [high == block for block in range(blocks)]
            for pair in range(pairs):
                value = jnp.zeros((8, 128), i32)
                for block in range(blocks):
                    value = jnp.where(masks[block], lanes_gather(table[pair, block], low), value)
                sums[pair] = value if sums[pair] is None else sums[pair] + value
        for pair in range(pairs):
            total[pair, pl.ds(offset, 8), :] = sums[pair]
        return carry

    lax.fori_loop(0, slots // 8, body, 0)


def lookup(place, chunk, ids, previous, step, share):
    heads = chunk.shape[0] // (share // chunk.shape[1])
    pairs = heads // 2
    slots = ids.shape[1]
    first = previous is None
    out = shape((pairs, slots, slots), i32)
    return pl.pallas_call(
        functools.partial(lookup_kernel, first, step, share),
        out_shape=out,
        in_specs=[smem] + [vmem] * (2 if first else 3),
        out_specs=vmem,
        scratch_shapes=[pltpu.VMEM((pairs, share // 128, 8, 128), i32)],
        input_output_aliases={} if first else {3: 0},
        compiler_params=params(8),
        cost_estimate=cost(6),
        name="lookup",
    )(place, chunk, ids, *(() if first else (previous,)))


def assemble(place, parts, whole):
    if len(parts) == 1:
        whole[...] = parts[0][...]
        return
    core = place[3]
    rows = parts[0].shape[1]
    for other in range(2):
        for which in range(4):
            for step in range(4):
                row, column = relative(place, core ^ other, which, step)
                start = pl.multiple_of(row * rows, rows)
                whole[column, pl.ds(start, rows), :] = parts[other * 4 + which][step]


def collect_biases(place, parts, whole):
    if len(parts) == 1:
        whole[...] = parts[0][...]
        return
    for i, part in enumerate(parts):
        whole[(place[2] ^ (i % 2)) * 2 + (place[3] ^ (i // 2))] = part[...]


def head_masks(width, offset, depth):
    lanes = lax.broadcasted_iota(i32, (1, width), 1)
    out = []
    for head in range(8):
        start = offset + head * depth
        out.append(((lanes >= start) & (lanes < start + depth)).astype(f32).astype(bf16))
    return out


def attend_kernel(
    n_parts, n_biases, place, counts, h1, edge_sums, buckets, spatial_table, layer_in, o_bias, gain, bias, *refs
):
    parts, bias_parts, refs = refs[:n_parts], refs[n_parts : n_parts + n_biases], refs[n_parts + n_biases :]
    weights, biases, transposed, value_win, probs_out, att_low, mid, h2 = refs
    assemble(place, parts, weights)
    collect_biases(place, bias_parts, biases)
    slots = h1.shape[0]
    groups, width = biases.shape[0], biases.shape[2]
    depth = width // 8
    pad = 256 - width
    hops = 5
    count = counts[place[4]]
    packed = quantize(spatial_table[...].astype(f32).T, spatial_unit)
    packed = jnp.concatenate([packed, jnp.zeros((packed.shape[0], 128 - packed.shape[1]), i32)], 1)
    hidden_key = lax.broadcasted_iota(i32, (slots, slots), 0) > count
    bucket = buckets[...]
    key_masks = head_masks(256, pad, depth)
    mid[...] = layer_in[...] + as_row(o_bias)
    for group in range(groups):
        natural = dot_nn(h1[...], weights[group, :, : 3 * width + pad])
        row_bias = jnp.concatenate(
            [
                biases[group, 0:1, :],
                jnp.zeros((1, width), f32),
                biases[group, 1:2, :],
                jnp.zeros((1, pad), f32),
            ],
            1,
        )
        natural = natural + row_bias
        natural_t = natural.T
        transposed[group] = natural_t[: 2 * width].astype(bf16)
        natural = natural.astype(bf16)
        value_win[group] = natural[:, 2 * width : 2 * width + 256]
        keys = natural[:, width - pad : 2 * width]
        stack = jnp.concatenate([keys * mask for mask in key_masks], 0)
        query = jnp.concatenate([jnp.zeros((pad, slots), f32), natural_t[:width]], 0).astype(bf16)
        scores = dot_nn(stack, query) * depth ** (-0.5)
        out = [None] * 8
        for pair in range(4):
            word = edge_sums[group * 4 + pair]
            head = group * 8 + pair
            spatial_word = lanes_gather(
                jnp.broadcast_to(packed[head : head + 1], (slots, 128)), bucket
            )
            low = (word << 16) >> 16
            spatial_low = (spatial_word << 16) >> 16
            high = (word - low) >> 16
            spatial_high = (spatial_word - spatial_low) >> 16
            for part, spatial_part, spot in ((low, spatial_low, pair), (high, spatial_high, pair + 4)):
                pair_bias = part.astype(f32) * (1.0 / (edge_unit * hops))
                pair_bias = pair_bias + spatial_part.astype(f32) * (1.0 / spatial_unit)
                score = scores[spot * slots : (spot + 1) * slots] + pair_bias
                score = jnp.where(hidden_key, masked_score, score)
                weight = jnp.exp(score - jnp.max(score, axis=0, keepdims=True))
                probs = weight * (1.0 / column_sum(weight))
                probs_out[group * 8 + spot] = probs
                values = natural_t[2 * width + spot * depth : 2 * width + (spot + 1) * depth]
                out[spot] = dot_nn(values.astype(bf16), probs.astype(bf16))
        gap = jnp.zeros((pad, slots), f32)
        att_low[group] = jnp.concatenate(out + [gap], 0).T.astype(bf16)
        high_form = jnp.concatenate([gap] + out, 0).T.astype(bf16)
        mid[...] += dot_nt(high_form, weights[group, :, 3 * width - pad : 4 * width])
    normed, scale = normalize(mid[...])
    h2[...] = (normed * as_row(gain) + as_row(bias)).astype(bf16)


def attend(place, counts, h1, edge_sums, buckets, spatial_table, layer_in, o_bias, gain, bias, parts, bias_parts):
    slots, features = h1.shape
    width = bias_parts[0].shape[-1]
    heads = spatial_table.shape[1]
    groups = heads // 8
    return pl.pallas_call(
        functools.partial(attend_kernel, len(parts), len(bias_parts)),
        out_shape=(
            shape((groups, features, 4 * width), bf16),
            shape((groups, 3, width), f32),
            shape((groups, 2 * width, slots), bf16),
            shape((groups, slots, 256), bf16),
            shape((heads, slots, slots), f32),
            shape((groups, slots, 256), bf16),
            shape((slots, features), f32),
            shape((slots, features), bf16),
        ),
        in_specs=[smem, smem] + [vmem] * (8 + len(parts) + len(bias_parts)),
        out_specs=[vmem] * 8,
        cost_estimate=cost(7),
        compiler_params=params(28),
        name="attend",
    )(
        place, counts, h1, edge_sums, buckets, spatial_table, layer_in, o_bias, gain, bias,
        *parts, *bias_parts,
    )


def group_order(place):
    return [
        (theirs, y, y * 2 + (place[3] ^ theirs)) for theirs in (1, 0) for y in (0, 1)
    ]


def feed_kernel(
    n_parts, place, mid, h2, weights_a, biases, out_bias, gain, cotangent, att_low, probs_in, *refs
):
    parts = refs[:n_parts]
    layer_out, grad_mid, grad_att_t, grad_values, mine, theirs, rows_t, sums, weights = refs[n_parts:]
    assemble(place, parts, weights)
    slots, features = mid.shape
    width = biases.shape[2]
    depth = width // 8
    pad = 256 - width
    lanes = lax.broadcasted_iota(i32, (1, 256), 1)
    cot = cotangent[...]
    grad_ffn = cot.astype(bf16)
    h2_value = h2[...]
    layer_out[...] = mid[...] + as_row(out_bias)
    grad_h2 = jnp.zeros((slots, features), f32)
    sums[...] = jnp.zeros_like(sums)
    order = group_order(place)
    for side, y, group in order:
        columns = theirs if side else mine
        in_bias = jnp.concatenate([biases[group, 2:3, :], jnp.zeros((1, pad), f32)], 1)
        pre = dot_nn(h2_value, weights[group, :, :256]) + in_bias
        cdf = 0.5 * (1.0 + lax.erf(pre * (0.5**0.5)))
        slope = cdf + pre * jnp.exp(-0.5 * pre * pre) * 0.3989422804014327
        hidden = pltpu.roll(pre * cdf, pad, 1)
        hidden = jnp.where(lanes >= pad, hidden, 0.0).astype(bf16)
        layer_out[...] += dot_nt(hidden, weights[group, :, width - pad : 2 * width])
        grad_hidden = dot_nn(grad_ffn, weights[group, :, width - pad : 2 * width])
        grad_hidden = pltpu.roll(grad_hidden, width, 1)
        grad_pre = jnp.where(lanes < width, grad_hidden * slope, 0.0).astype(bf16)
        grad_h2 = grad_h2 + dot_nt(grad_pre, weights[group, :, :256])
        columns[y, :, 0:256] = grad_pre
        columns[y, :, 256:512] = hidden
        columns[y, :, 512:768] = att_low[group]
        sums[pl.ds(12 + group, 1), 0:256] = column_sum(grad_pre.astype(f32))
    normed, scale = normalize(mid[...])
    grad = cot + normalize_back(grad_h2 * as_row(gain), normed, scale)
    grad_mid[...] = grad
    branch = grad.astype(bf16)
    sums[2:3, :] = column_sum(grad)
    sums[3:4, :] = column_sum(grad_h2 * normed)
    sums[4:5, :] = column_sum(grad_h2)
    sums[5:6, :] = column_sum(cot)
    rows_t[0] = h2_value.astype(f32).T.astype(bf16)
    rows_t[1] = grad.T.astype(bf16)
    gap = jnp.zeros((pad, slots), f32)
    for side, y, group in order:
        columns = theirs if side else mine
        grad_att = dot_nn(branch, weights_a[group]).T[pad:]
        grad_att_t[group] = jnp.concatenate([grad_att, gap], 0).astype(bf16)
        out = []
        for head in range(8):
            out.append(
                dot_nt(
                    grad_att[head * depth : (head + 1) * depth].astype(bf16),
                    probs_in[group * 8 + head].astype(bf16),
                )
            )
        low_form = jnp.concatenate(out + [gap], 0).T.astype(bf16)
        grad_values[group] = low_form
        columns[y, :, 768:1024] = jnp.concatenate([gap] + out, 0).T.astype(bf16)
        sums[pl.ds(8 + group, 1), 512:768] = column_sum(low_form.astype(f32))


def feed(place, mid, h2, weights_a, biases, out_bias, gain, cotangent, att_low, probs, parts):
    slots, features = mid.shape
    groups, width = biases.shape[0], biases.shape[2]
    whole = lambda array: pl.BlockSpec(array.shape, lambda i: (0,) * len(array.shape))
    outs = (
        shape((slots, features), f32),
        shape((slots, features), f32),
        shape((groups, 256, slots), bf16),
        shape((groups, slots, 256), bf16),
        shape((2, slots, 1024), bf16),
        shape((2, slots, 1024), bf16),
        shape((2, features, slots), bf16),
        shape((16, features), f32),
    )
    rest = (biases, out_bias, gain, cotangent, att_low, probs)
    return pl.pallas_call(
        functools.partial(feed_kernel, len(parts)),
        grid=(1,),
        out_shape=outs,
        in_specs=[
            smem,
            whole(mid),
            whole(h2),
            pl.BlockSpec((groups, features, 256), lambda i: (0, 0, 2)),
        ]
        + [whole(a) for a in rest + tuple(parts)],
        out_specs=[whole(out) for out in outs],
        scratch_shapes=[pltpu.VMEM((groups, features, 2 * width), bf16)],
        cost_estimate=cost(7),
        compiler_params=params(32),
        name="feed",
    )(place, mid, h2, weights_a, *rest, *parts)


def attend_back_kernel(
    place, probs_in, value_win, transposed, grad_att_t, grad_values, weights, layer_in, gain, grad_mid,
    sums_in, after, score_grads, mine, theirs, grad_in, sums,
):
    slots, features = layer_in.shape
    width = transposed.shape[1] // 2
    depth = width // 8
    value_masks = head_masks(256, 0, depth)
    grad_h1 = jnp.zeros((slots, features), f32)
    sums[...] = sums_in[...]
    scale = depth ** (-0.5)
    for side, y, group in group_order(place):
        columns = theirs if side else mine
        values = value_win[group]
        stack = jnp.concatenate([values * mask for mask in value_masks], 0)
        grad_probs = dot_nn(stack, grad_att_t[group])
        held = transposed[group].astype(f32)
        query_out, key_out, score_out = [], [], []
        for head in range(8):
            probs = probs_in[group * 8 + head]
            part = probs * grad_probs[head * slots : (head + 1) * slots]
            exact = part - probs * column_sum(part)
            grads = exact.astype(bf16)
            score_out.append(exact)
            key_rows = held[width + head * depth : width + (head + 1) * depth]
            query_out.append(dot_nn(key_rows.astype(bf16), grads) * scale)
            query_rows = held[head * depth : (head + 1) * depth]
            key_out.append(dot_nt(query_rows.astype(bf16), grads) * scale)
        score_grads[group] = jnp.swapaxes(jnp.stack(score_out), 0, 1)
        natural = jnp.concatenate(query_out + key_out, 0).T.astype(bf16)
        columns[y] = natural
        grad_h1 = grad_h1 + dot_nt(natural, weights[group, :, : 2 * width])
        grad_h1 = grad_h1 + dot_nt(grad_values[group], weights[group, :, 2 * width : 2 * width + 256])
        sums[pl.ds(8 + group, 1), 0 : 2 * width] = column_sum(natural.astype(f32))
    normed, inverse = normalize(layer_in[...])
    grad_in[...] = grad_mid[...] + normalize_back(grad_h1 * as_row(gain), normed, inverse)
    sums[0:1, :] = column_sum(grad_h1 * normed)
    sums[1:2, :] = column_sum(grad_h1)


def attend_back(
    place, probs, value_win, transposed, grad_att_t, grad_values, weights, layer_in, gain, grad_mid, sums, after
):
    slots, features = layer_in.shape
    groups = transposed.shape[0]
    width = transposed.shape[1] // 2
    return pl.pallas_call(
        attend_back_kernel,
        out_shape=(
            shape((groups, slots, 8, slots), f32),
            shape((2, slots, 2 * width), bf16),
            shape((2, slots, 2 * width), bf16),
            shape((slots, features), f32),
            shape(sums.shape, f32),
        ),
        in_specs=[smem] + [vmem] * 10 + [untouched],
        out_specs=[vmem] * 5,
        cost_estimate=cost(7),
        compiler_params=params(24),
        name="attend_back",
    )(
        place, probs, value_win, transposed, grad_att_t, grad_values, weights, layer_in, gain, grad_mid,
        sums, after,
    )


def weight_grads_kernel(plan, n_rows, place, columns_own, columns_other, *refs):
    own_rows, other_rows = refs[:n_rows], refs[n_rows : 2 * n_rows]
    own, across, over, both, rows_t = refs[2 * n_rows :]
    kind = 0
    for mine, other in zip(own_rows, other_rows):
        slots = mine.shape[2]
        for i in range(mine.shape[0]):
            rows_t[kind, :, 0:slots] = mine[i]
            rows_t[kind, :, slots : 2 * slots] = other[i]
            kind += 1
    core = place[3]
    height = own.shape[1]
    for which, out in ((3, both), (2, over), (1, across), (0, own)):
        y = relative(place, core, which, 0)[1] >> 1
        right = jnp.concatenate([columns_own[y], columns_other[y]], 0)
        for step in range(4):
            row = relative(place, core, which, step)[0]
            start = pl.multiple_of(row * height, height)
            out[step] = plan(lambda kind: rows_t[kind, pl.ds(start, height), :], right).astype(bf16)


def plan_first(rows_of, right):
    return dot_nn(rows_of(0), right)


def plan_second(rows_of, right):
    grad_in = dot_nn(rows_of(2), right[:, 0:256])
    grad_out = dot_nn(rows_of(1), right[:, 256:512])
    grad_o = dot_nn(rows_of(3), right[:, 512:768])
    grad_v = dot_nn(rows_of(0), right[:, 768:1024])
    return jnp.concatenate(
        [
            grad_in[:, :128],
            grad_in[:, 128:] + grad_out[:, :128],
            grad_out[:, 128:],
            grad_o[:, :128],
            grad_o[:, 128:] + grad_v[:, :128],
            grad_v[:, 128:],
        ],
        1,
    )


def weight_grads(plan, place, columns_own, columns_other, own_rows, other_rows, height, lanes, microseconds):
    features, slots = own_rows[0].shape[1:]
    kinds = sum(rows.shape[0] for rows in own_rows)
    out = shape((4, height, lanes), bf16)
    return pl.pallas_call(
        functools.partial(weight_grads_kernel, plan, len(own_rows)),
        out_shape=(out,) * 4,
        in_specs=[smem] + [vmem] * (2 + 2 * len(own_rows)),
        out_specs=[vmem] * 4,
        scratch_shapes=[pltpu.VMEM((kinds, features, 2 * slots), bf16)],
        cost_estimate=cost(microseconds),
        compiler_params=params(20),
        name="weight_grads",
    )(place, columns_own, columns_other, *own_rows, *other_rows)


def table_kernel(digit, staged, span, place, grads, ids, buckets, sums, after, *refs):
    if staged:
        mine, theirs, small, total, spatial = refs
    else:
        total, spatial = refs
    hops = ids.shape[0]
    groups = grads.shape[0]
    heads = groups * 8
    high_count = total.shape[0] // heads
    total[...] = jnp.zeros_like(total)
    spatial[...] = jnp.zeros_like(spatial)
    digits = lax.broadcasted_iota(i32, (digit, 128), 0).astype(f32).astype(bf16)
    kinds = lax.broadcasted_iota(i32, (heads, 128), 0).astype(f32).astype(bf16)
    one = jnp.ones((), bf16)
    zero = jnp.zeros((), bf16)

    def body(i, carry):
        lefts, rights, plain, kind_rights = [], [], [], []
        for j in range(span):
            row = i * span + j
            piece = jnp.concatenate([grads[group, row] for group in range(groups)], 0).astype(bf16)
            bucket = buckets[pl.ds(row, 1), :].astype(f32).astype(bf16)
            plain.append(piece)
            kind_rights.append(jnp.where(jnp.broadcast_to(bucket, (heads, 128)) == kinds, one, zero))
            for hop in range(hops):
                value = ids[hop, pl.ds(row, 1), :].astype(f32)
                high = jnp.floor((value + 0.5) * (1.0 / digit))
                low = value - high * digit
                low = jnp.broadcast_to(low.astype(bf16), (digit, 128))
                high = jnp.broadcast_to(high.astype(bf16), (heads, 128))
                rights.append(jnp.where(low == digits, one, zero))
                lefts.append(
                    jnp.concatenate(
                        [jnp.where(high == jnp.full((), k, bf16), piece, zero) for k in range(high_count)], 0
                    )
                )
        total[...] += dot_nt(jnp.concatenate(lefts, 1), jnp.concatenate(rights, 1))
        spatial[...] += dot_nt(jnp.concatenate(plain, 1), jnp.concatenate(kind_rights, 1))
        return carry

    lax.fori_loop(0, grads.shape[1] // span, body, 0)
    if staged:
        core = place[3]
        for other, out in ((0, mine), (1, theirs)):
            for which in range(4):
                pieces = []
                for step in range(4):
                    row, column = relative(place, core ^ other, which, step)
                    start = pl.multiple_of(row * heads + column * 8, 8)
                    pieces.append(total[pl.ds(start, 8), :] * (1.0 / hops))
                out[which * 8 : (which + 1) * 8, :] = jnp.concatenate(pieces, 1)
        spread = []
        for group in range(4):
            spread += [spatial[group * 8 : (group + 1) * 8, :], jnp.zeros((8, 128 - heads), f32)]
        lanes = sums.shape[1]
        spread.append(jnp.zeros((8, lanes - 512), f32))
        spread = jnp.concatenate(spread, 1)
        small[0:16, :] = sums[...]
        small[16:24, :] = spread
        theirs[32:48, :] = sums[...]
        theirs[48:56, :] = spread


def table_grads(place, grads, ids, buckets, sums, after, digit, edges, staged):
    heads = grads.shape[0] * 8
    total = (edges // digit * heads, digit)
    lanes = sums.shape[1]
    outs = (shape((32, lanes), f32), shape((56, lanes), f32), shape((24, lanes), f32))
    inner = (shape(total, f32), shape((heads, heads), f32))
    return pl.pallas_call(
        functools.partial(table_kernel, digit, staged, 8),
        out_shape=outs if staged else inner,
        in_specs=[smem] + [vmem] * 4 + [untouched],
        out_specs=[vmem] * (3 if staged else 2),
        scratch_shapes=[pltpu.VMEM(a.shape, f32) for a in inner] if staged else [],
        cost_estimate=cost(15),
        compiler_params=params(12),
        name="table_grads",
    )(place, grads, ids, buckets, sums, after)


def meet_core_kernel(mine, small, got, out, keep):
    keep[...] = mine[0:16, :] + got[0:16, :]
    out[0:8, :] = mine[24:32, :] + got[24:32, :]
    out[8:16, :] = mine[16:24, :] + got[16:24, :]
    out[16:40, :] = small[...] + got[32:56, :]


def meet_second_kernel(keep, sent, got, out, kept):
    out[0:8, :] = keep[8:16, :] + got[0:8, :]
    out[8:32, :] = sent[16:40, :] + got[16:40, :]
    kept[...] = keep[0:8, :] + got[8:16, :]


def meet_first_kernel(kept, sent, got, *outs):
    own = kept[...] + got[0:8, :]
    small = sent[8:32, :] + got[8:32, :]
    digit = own.shape[1] // 4
    for step, out in enumerate(outs):
        out[0:8, 0:digit] = own[:, step * digit : (step + 1) * digit]
        out[0:8, digit:] = jnp.zeros((8, 3 * digit), f32)
        out[8:32, :] = small


def finish_kernel(place, own, first, second, third, edge, spatial, *outs):
    total = own[...] + first[...] + second[...] + third[...]
    digit = edge.shape[1]
    edge[...] = total[0:8, 0:digit]
    group = place[4]
    for i, out in enumerate(outs[:6]):
        out[...] = total[8 + i : 9 + i, :].reshape(out.shape)
    width = outs[6].shape[0]
    heads = total[16:17]
    hidden = total[20:21]
    kinds = total[24:32, 0:128]
    for other in range(1, 4):
        heads = jnp.where(group == other, total[16 + other : 17 + other], heads)
        hidden = jnp.where(group == other, total[20 + other : 21 + other], hidden)
        kinds = jnp.where(group == other, total[24:32, other * 128 : (other + 1) * 128], kinds)
    outs[6][...] = heads[:, :width].reshape(outs[6].shape)
    outs[7][...] = heads[:, 512 : 512 + width].reshape(outs[7].shape)
    outs[8][...] = hidden[:, :width].reshape(outs[8].shape)
    spatial[...] = kinds[:, : spatial.shape[1]]


def small_call(kernel, name, outs, *args):
    return pl.pallas_call(
        kernel,
        out_shape=outs,
        in_specs=[smem if args[i].ndim == 1 else vmem for i in range(len(args))],
        out_specs=[vmem] * len(outs),
        cost_estimate=cost(0.7),
        compiler_params=params(4),
        name=name,
    )(*args)


class Links:
    def __init__(self):
        self.core = self.hop(lambda z, x, y, c: (z, x, y, 1 - c))
        self.first = self.hop(lambda z, x, y, c: (z, x, 1 - y, c) if c else (z, 1 - x, y, c))
        self.second = self.hop(lambda z, x, y, c: (z, 1 - x, y, c) if c else (z, x, 1 - y, c))
        self.along_x = self.hop(lambda z, x, y, c: (z, 1 - x, y, c))
        self.along_y = self.hop(lambda z, x, y, c: (z, x, 1 - y, c))
        self.along_z = [self.hop(lambda z, x, y, c, k=k: (z ^ k, x, y, c)) for k in (1, 2, 3)]

    def hop(self, move):
        index = lambda z, x, y, c: (z * 2 + x) * 4 + y * 2 + c
        spots = [(z, x, y, c) for z in range(4) for x in range(2) for y in range(2) for c in range(2)]
        return [(index(*spot), index(*move(*spot))) for spot in spots]


def send(values, hop):
    return lax.ppermute(values, ("dp", "mp"), hop)


def gather_staged(links, own):
    stack = jnp.stack([own] + [send(own, hop) for hop in links.along_z])
    across = send(stack, links.first)
    over = send(stack, links.second)
    both = send(across, links.second)
    mine = (stack, across, over, both)
    return mine + tuple(send(part, links.core) for part in mine)


def add_rounded(*terms):
    total = terms[0].astype(f32)
    for term in terms[1:]:
        total = total + term.astype(f32)
    return total.astype(bf16)


def reduce_staged(links, own, across, over, both):
    across = add_rounded(across, send(both, links.second))
    own = add_rounded(own, send(over, links.second), send(across, links.first))
    total = own[0].astype(f32)
    for step, hop in enumerate(links.along_z):
        total = total + send(own[step + 1], hop).astype(f32)
    return total


def local(
    layer_in,
    node_counts,
    spatial_ids,
    path_ids,
    ln1_gain,
    ln1_bias,
    w_q,
    w_k,
    w_v,
    q_bias,
    v_bias,
    spatial_table,
    edge_table,
    w_o,
    o_bias,
    ln2_gain,
    ln2_bias,
    w_in,
    in_bias,
    w_out,
    out_bias,
    cotangent,
):
    dp_size, mp_size = lax.axis_size("dp"), lax.axis_size("mp")
    dp_index, mp_index = lax.axis_index("dp"), lax.axis_index("mp")
    staged = dp_size == 8 and mp_size == 4
    height, width = w_q.shape
    features = layer_in.shape[1]
    edges = edge_table.shape[0] * dp_size
    heads = spatial_table.shape[1]
    kinds = spatial_table.shape[0]
    hops = path_ids.shape[1]
    share = edges // 4
    digit = edges // 8
    place = jnp.stack([dp_index // 2, dp_index % 2, mp_index // 2, mp_index % 2, mp_index]).astype(i32)
    ids, buckets, h1, rows_early = prepare(
        place, spatial_ids, path_ids, layer_in, ln1_gain, ln1_bias, cotangent, kinds - 1
    )
    if staged:
        links = Links()
        first, second, own_biases = pack(w_q, w_k, w_v, w_o, w_in, w_out, q_bias, v_bias, in_bias)
        table_t = edge_table.T
        neighbour = send(table_t, links.along_x)
        even = dp_index % 2 == 0
        pair = jnp.concatenate(
            [jnp.where(even, table_t, neighbour), jnp.where(even, neighbour, table_t)], 0
        )
        chunks = [pair] + [send(pair, hop) for hop in links.along_z]
        parts_a = gather_staged(links, first)
        parts_b = gather_staged(links, second)
        y_biases = send(own_biases, links.along_y)
        bias_parts = (own_biases, y_biases, send(own_biases, links.core), send(y_biases, links.core))
        lookup_place = place
    else:
        gathered = [
            lax.all_gather(lax.all_gather(w, "dp", axis=0, tiled=True), "mp", axis=0)
            for w in (w_q, w_k, w_v, w_o, w_in, w_out)
        ]
        parts_a = (jnp.concatenate(gathered[:4], 2),)
        parts_b = (jnp.concatenate(gathered[4:], 2),)
        bias_parts = (lax.all_gather(jnp.stack([q_bias, v_bias, in_bias]), "mp", axis=0, tiled=False),)
        table_t = lax.all_gather(edge_table, "dp", axis=0, tiled=True).T
        chunks = [table_t[:, i * share : (i + 1) * share] for i in range(4)]
        lookup_place = jnp.zeros((5,), i32)
    edge_sums = None
    for step in range(4):
        edge_sums = lookup(lookup_place, chunks[step], ids, edge_sums, step, share)

    weights, biases, transposed, value_win, probs, att_low, mid, h2 = attend(
        place, node_counts, h1, edge_sums, buckets, spatial_table,
        layer_in, o_bias, ln2_gain, ln2_bias, parts_a, bias_parts,
    )
    layer_out, grad_mid, grad_att_t, grad_values, mine_b, theirs_b, rows_late, sums = feed(
        place, mid, h2, weights, biases, out_bias, ln2_gain, cotangent, att_low, probs, parts_b
    )
    after = sums
    if staged:
        rows_b = (rows_early, rows_late)
        other_rows_b = tuple(send(rows, links.core) for rows in rows_b)
        pieces_b = weight_grads(
            plan_second, place, mine_b, send(theirs_b, links.core), rows_b, other_rows_b, height, 4 * width, 4
        )
        grads_b = reduce_staged(links, *pieces_b)
        after = pieces_b[0]
    score_grads, mine_a, theirs_a, grad_layer_in, sums = attend_back(
        place, probs, value_win, transposed, grad_att_t, grad_values, weights,
        layer_in, ln1_gain, grad_mid, sums, after,
    )
    if staged:
        pieces_a = weight_grads(
            plan_first, place, mine_a, send(theirs_a, links.core),
            (rows_early[0:1],), (other_rows_b[0][0:1],), height, 2 * width, 2,
        )
        grads_a = reduce_staged(links, *pieces_a)
        mine, theirs, small = table_grads(
            place, score_grads, ids, buckets, sums, pieces_a[0], digit, edges, True
        )
        sent, keep = small_call(
            meet_core_kernel, "meet_core", (shape((40, features), f32), shape((16, features), f32)),
            mine, small, send(theirs, links.core),
        )
        sent, keep = small_call(
            meet_second_kernel, "meet_second", (shape((32, features), f32), shape((8, features), f32)),
            keep, sent, send(sent, links.second),
        )
        outs = small_call(
            meet_first_kernel, "meet_first", (shape((32, features), f32),) * 4,
            keep, sent, send(sent, links.first),
        )
        got = [send(out, hop) for out, hop in zip(outs[1:], links.along_z)]
        grad_edge, grad_spatial, *rows = small_call(
            finish_kernel, "finish",
            (shape((8, digit), f32), shape((8, kinds), f32))
            + (shape((features,), f32),) * 6
            + (shape((width,), f32),) * 3,
            place, outs[0], *got,
        )
        grad_edge = grad_edge.T
        grad_spatial = grad_spatial.T
        grad_w_q, grad_w_k = (grads_a[:, i * width : (i + 1) * width] for i in range(2))
        grad_w_in, grad_w_out, grad_w_o, grad_w_v = (
            grads_b[:, i * width : (i + 1) * width] for i in range(4)
        )
    else:
        contract = lambda a, b: lax.dot_general(
            a, b, (((1,), (1,)), ((), ())), preferred_element_type=f32
        )

        def unmix(mine, theirs):
            even = mp_index % 2 == 0
            cores = jnp.where(even, jnp.stack([mine, theirs], 1), jnp.stack([theirs, mine], 1))
            return cores.reshape(4, *mine.shape[1:])

        def scatter(rows_t, columns):
            grads = contract(rows_t, columns)
            grads = jnp.transpose(grads, (1, 0, 2))
            grads = lax.psum_scatter(grads, "mp", scatter_dimension=0, tiled=False)
            return lax.psum_scatter(grads, "dp", scatter_dimension=0, tiled=True)

        columns_a, columns_b = unmix(mine_a, theirs_a), unmix(mine_b, theirs_b)
        grad_w_q, grad_w_k = (
            scatter(rows_early[0], columns_a[:, :, i * width : (i + 1) * width]) for i in range(2)
        )
        grad_w_v = scatter(rows_early[0], columns_b[:, :, 1024 - width :])
        grad_w_in = scatter(rows_late[0], columns_b[:, :, :width])
        grad_w_out = scatter(rows_early[1], columns_b[:, :, 512 - width : 512])
        grad_w_o = scatter(rows_late[1], columns_b[:, :, 512 : 512 + width])
        table, spatial = table_grads(place, score_grads, ids, buckets, sums, sums, digit, edges, False)
        table = table.reshape(-1, heads, digit).transpose(0, 2, 1).reshape(edges, heads) / hops
        table = lax.psum_scatter(table, "dp", scatter_dimension=0, tiled=True)
        table = lax.psum(table, "mp")
        grad_edge = lax.dynamic_slice_in_dim(table, mp_index * 8, 8, 1)
        totals, spatial = lax.psum((sums, spatial), ("dp", "mp"))
        grad_spatial = lax.dynamic_slice_in_dim(spatial[:, :kinds], mp_index * 8, 8, 0).T
        head_sums = lax.dynamic_slice_in_dim(totals, 8 + mp_index, 1, 0)[0]
        hidden_sums = lax.dynamic_slice_in_dim(totals, 12 + mp_index, 1, 0)[0]
        rows = [totals[i] for i in range(6)]
        rows += [head_sums[:width], head_sums[512 : 512 + width], hidden_sums[:width]]
    return (
        layer_out,
        grad_layer_in,
        rows[0],
        rows[1],
        grad_w_q,
        grad_w_k,
        grad_w_v,
        rows[6],
        rows[7],
        grad_spatial,
        grad_edge,
        grad_w_o,
        rows[2],
        rows[3],
        rows[4],
        grad_w_in,
        rows[8],
        grad_w_out,
        rows[5],
    )


def solution(mesh):
    return jax.shard_map(
        local,
        mesh=mesh,
        in_specs=(
            P(("dp", "mp"), None),
            P("dp"),
            P("dp", None, None),
            P("dp", None, None, None),
            P(),
            P(),
            P("dp", "mp"),
            P("dp", "mp"),
            P("dp", "mp"),
            P("mp"),
            P("mp"),
            P(),
            P("dp", None),
            P("dp", "mp"),
            P(),
            P(),
            P(),
            P("dp", "mp"),
            P("mp"),
            P("dp", "mp"),
            P(),
            P(("dp", "mp"), None),
        ),
        out_specs=(
            P(("dp", "mp"), None),
            P(("dp", "mp"), None),
            P(),
            P(),
            P("dp", "mp"),
            P("dp", "mp"),
            P("dp", "mp"),
            P("mp"),
            P("mp"),
            P(None, "mp"),
            P("dp", "mp"),
            P("dp", "mp"),
            P(),
            P(),
            P(),
            P("dp", "mp"),
            P("mp"),
            P("dp", "mp"),
            P(),
        ),
        check_vma=False,
    )
```

```python
import functools

import jax
import jax.numpy as jnp
from jax import lax
from jax.experimental import pallas as pl
from jax.experimental.pallas import tpu as pltpu
from jax.sharding import PartitionSpec as P

epsilon = 1e-05
masked_score = -1e30
edge_unit = 1638.0
spatial_unit = 4096.0
bf16 = jnp.bfloat16
f32 = jnp.float32
i32 = jnp.int32
vmem = pl.BlockSpec(memory_space=pltpu.VMEM)
smem = pl.BlockSpec(memory_space=pltpu.SMEM)
hbm = pl.BlockSpec(memory_space=pltpu.HBM)
untouched = pl.BlockSpec(memory_space=pl.ANY)


def params(mebibytes):
    return pltpu.CompilerParams(vmem_limit_bytes=mebibytes << 20)


def normalize(values):
    centred = values - jnp.mean(values, axis=-1, keepdims=True)
    scale = lax.rsqrt(jnp.mean(centred * centred, axis=-1, keepdims=True) + epsilon)
    return (centred * scale, scale)


def normalize_back(grad_normed, normed, scale):
    inner = grad_normed - jnp.mean(grad_normed, axis=-1, keepdims=True)
    inner = inner - normed * jnp.mean(grad_normed * normed, axis=-1, keepdims=True)
    return inner * scale


def dot_nn(left, right):
    return lax.dot_general(
        left, right, (((1,), (0,)), ((), ())), preferred_element_type=f32
    )


def dot_nt(left, right):
    return lax.dot_general(
        left, right, (((1,), (1,)), ((), ())), preferred_element_type=f32
    )


def column_sum(values):
    return jnp.sum(values, axis=0, keepdims=True)


def cost(microseconds):
    return pl.CostEstimate(flops=int(microseconds * 1.15e9), bytes_accessed=1024, transcendentals=0)


def as_row(ref):
    return ref[...].reshape(1, -1)


def shape(dims, kind):
    return jax.ShapeDtypeStruct(dims, kind)


def relative(place, side, which, step):
    z, x, y = place[0], place[1], place[2]
    flip_x = (0, 1 - side, side, 1)[which]
    flip_y = (0, side, 1 - side, 1)[which]
    row = (z ^ step) * 2 + (x ^ flip_x)
    column = (y ^ flip_y) * 2 + side
    return row, column


def three_terms(values):
    terms = []
    for _ in range(3):
        term = values.astype(bf16)
        terms.append(term)
        values = values - term.astype(f32)
    return terms


def pack_first_kernel(wq, wk, wv, wo, bq, bv, bi, weights, biases, held, sems):
    copies = [
        pltpu.make_async_copy(source, held.at[i], sems.at[i]) for i, source in enumerate((wq, wk, wv, wo))
    ]
    for copy in copies:
        copy.start()
    row = jnp.concatenate([as_row(bq), as_row(bv), as_row(bi)], 1)
    lanes = weights.shape[1]
    row = jnp.concatenate([row, jnp.zeros((1, lanes - row.shape[1]), f32)], 1)
    terms = [term.astype(f32) for term in three_terms(row)]
    biases[...] = jnp.concatenate(terms + [jnp.zeros((13, lanes), f32)], 0).astype(bf16)
    for copy in copies:
        copy.wait()
    weights[...] = jnp.concatenate([held[i] for i in range(4)], 1)


def pack_first(wq, wk, wv, wo, bq, bv, bi):
    rows, width = wq.shape
    return pl.pallas_call(
        pack_first_kernel,
        out_shape=(shape((rows, 4 * width), bf16), shape((16, 4 * width), bf16)),
        in_specs=[hbm] * 4 + [vmem] * 3,
        out_specs=[vmem] * 2,
        scratch_shapes=[pltpu.VMEM((4, rows, width), bf16), pltpu.SemaphoreType.DMA((4,))],
        cost_estimate=cost(1),
        compiler_params=params(62),
        name="pack_first",
    )(wq, wk, wv, wo, bq, bv, bi)


def pack_second_kernel(place, wi, wu, edge, neighbour, out):
    rows = wi.shape[0]
    out[0:rows, :] = jnp.concatenate([wi[...], wu[...]], 1)
    even = place[1] == 0
    mine, other = edge[...].astype(f32), neighbour[...].astype(f32)
    low, high = jnp.where(even, mine, other), jnp.where(even, other, mine)
    out[rows:, :] = jnp.concatenate([low, high], 1).astype(bf16)


def pack_second(place, wi, wu, edge, neighbour):
    rows, width = wi.shape
    return pl.pallas_call(
        pack_second_kernel,
        out_shape=shape((rows + edge.shape[0], 2 * width), bf16),
        in_specs=[smem] + [vmem] * 4,
        out_specs=vmem,
        cost_estimate=cost(1),
        compiler_params=params(4),
        name="pack_second",
    )(place, wi, wu, edge, neighbour)


def prepare_kernel(virtual, place, spatial, path, layer_in, gain, bias, cotangent, ids, buckets, h1, rows_t):
    slots = spatial.shape[1]
    for hop in range(path.shape[1]):
        ids[hop] = path[0, hop].T
    rows = lax.broadcasted_iota(i32, (slots, slots), 0)
    columns = lax.broadcasted_iota(i32, (slots, slots), 1)
    buckets[...] = jnp.where((rows == 0) | (columns == 0), virtual, spatial[0].T)
    normed, scale = normalize(layer_in[...])
    out = normed * as_row(gain) + as_row(bias)
    h1[...] = out.astype(bf16)
    rows_t[0] = out.T.astype(bf16)
    rows_t[1] = cotangent[...].T.astype(bf16)


def prepare(place, spatial, path, layer_in, gain, bias, cotangent, virtual):
    hops, slots = path.shape[1], path.shape[2]
    rows, width = layer_in.shape
    whole = lambda dims: pl.BlockSpec(dims, lambda i, s: (0,) * len(dims))
    return pl.pallas_call(
        functools.partial(prepare_kernel, virtual),
        grid_spec=pltpu.PrefetchScalarGridSpec(
            num_scalar_prefetch=1,
            grid=(1,),
            in_specs=[
                pl.BlockSpec((1, slots, slots), lambda i, s: (s[4], 0, 0)),
                pl.BlockSpec((1, hops, slots, slots), lambda i, s: (s[4], 0, 0, 0)),
                whole((rows, width)),
                whole((width,)),
                whole((width,)),
                whole((rows, width)),
            ],
            out_specs=[
                whole((hops, slots, slots)),
                whole((slots, slots)),
                whole((rows, width)),
                whole((2, width, rows)),
            ],
        ),
        out_shape=(
            shape((hops, slots, slots), i32),
            shape((slots, slots), i32),
            shape((rows, width), bf16),
            shape((2, width, rows), bf16),
        ),
        compiler_params=params(8),
        cost_estimate=cost(1),
        name="prepare",
    )(place, spatial, path, layer_in, gain, bias, cotangent)


def quantize(table, unit):
    held = jnp.round(table.astype(f32) * unit).astype(i32)
    partner = jnp.concatenate([held[4:], held[:4]], 0)
    return held + partner * 65536


def lanes_gather(table, places):
    return jnp.take_along_axis(table, places, axis=1, mode="promise_in_bounds")


def lookup_kernel(first, step, share, place, chunk, ids, *refs):
    if first:
        total, table = refs
        previous = None
    else:
        previous, total, table = refs
    hops, slots = ids.shape[0], ids.shape[1]
    pairs = total.shape[0]
    packed = quantize(chunk[chunk.shape[0] - 2 * pairs :, :], edge_unit)
    blocks = share // 128
    for pair in range(pairs):
        head = (pair // 4) * 8 + pair % 4
        for block in range(blocks):
            table[pair, block] = jnp.broadcast_to(
                packed[head : head + 1, block * 128 : (block + 1) * 128], (8, 128)
            )
    base = (place[0] ^ step) * share

    def body(i, carry):
        offset = pl.multiple_of(i * 8, 8)
        sums = [None] * pairs
        if not first:
            sums = [previous[pair, pl.ds(offset, 8), :] for pair in range(pairs)]
        for hop in range(hops):
            relative_id = ids[hop, pl.ds(offset, 8), :] - base
            low = relative_id & 127
            high = relative_id >> 7
            masks = [high == block for block in range(blocks)]
            for pair in range(pairs):
                value = jnp.zeros((8, 128), i32)
                for block in range(blocks):
                    value = jnp.where(masks[block], lanes_gather(table[pair, block], low), value)
                sums[pair] = value if sums[pair] is None else sums[pair] + value
        for pair in range(pairs):
            total[pair, pl.ds(offset, 8), :] = sums[pair]
        return carry

    lax.fori_loop(0, slots // 8, body, 0)


def lookup(place, chunk, ids, previous, step, heads):
    share = chunk.shape[1]
    pairs = heads // 2
    slots = ids.shape[1]
    first = previous is None
    out = shape((pairs, slots, slots), i32)
    return pl.pallas_call(
        functools.partial(lookup_kernel, first, step, share),
        out_shape=out,
        in_specs=[smem] + [vmem] * (2 if first else 3),
        out_specs=vmem,
        scratch_shapes=[pltpu.VMEM((pairs, share // 128, 8, 128), i32)],
        input_output_aliases={} if first else {3: 0},
        compiler_params=params(8),
        cost_estimate=cost(6),
        name="lookup",
    )(place, chunk, ids, *(() if first else (previous,)))


def assemble(place, parts, whole, biases=None):
    if len(parts) == 1:
        whole[...] = parts[0][...]
        return
    core = place[3]
    rows = whole.shape[1] // 8
    for other in range(2):
        for which in range(4):
            part = parts[other * 4 + which]
            for step in range(4):
                row, column = relative(place, core ^ other, which, step)
                start = pl.multiple_of(row * rows, rows)
                whole[column, pl.ds(start, rows), :] = part[step * rows : (step + 1) * rows, :]
            if biases is not None:
                terms = part[4 * rows : 4 * rows + 16, :].astype(f32)
                biases[column] = terms[0:1] + terms[1:2] + terms[2:3]


def head_masks(width, offset, depth):
    lanes = lax.broadcasted_iota(i32, (1, width), 1)
    out = []
    for head in range(8):
        start = offset + head * depth
        out.append(((lanes >= start) & (lanes < start + depth)).astype(f32).astype(bf16))
    return out


def attend_kernel(
    n_parts, place, counts, h1, edge_sums, buckets, spatial_table, layer_in, o_bias, gain, bias, *refs
):
    parts, refs = refs[:n_parts], refs[n_parts:]
    weights, biases, transposed, value_win, probs_out, att_low, mid, h2 = refs
    if n_parts == 2:
        assemble(place, parts[:1], weights)
        biases[...] = parts[1][...]
    else:
        assemble(place, parts, weights, biases)
    slots = h1.shape[0]
    groups, width = biases.shape[0], biases.shape[2] // 4
    depth = width // 8
    pad = 256 - width
    hops = 5
    count = counts[place[4]]
    packed = quantize(spatial_table[...].astype(f32).T, spatial_unit)
    packed = jnp.concatenate([packed, jnp.zeros((packed.shape[0], 128 - packed.shape[1]), i32)], 1)
    hidden_key = lax.broadcasted_iota(i32, (slots, slots), 0) > count
    bucket = buckets[...]
    key_masks = head_masks(256, pad, depth)
    mid[...] = layer_in[...] + as_row(o_bias)
    for group in range(groups):
        natural = dot_nn(h1[...], weights[group, :, : 3 * width + pad])
        row_bias = jnp.concatenate(
            [
                biases[group, 0:1, :width],
                jnp.zeros((1, width), f32),
                biases[group, 0:1, width : 2 * width],
                jnp.zeros((1, pad), f32),
            ],
            1,
        )
        natural = natural + row_bias
        natural_t = natural.T
        transposed[group] = natural_t[: 2 * width].astype(bf16)
        natural = natural.astype(bf16)
        value_win[group] = natural[:, 2 * width : 2 * width + 256]
        keys = natural[:, width - pad : 2 * width]
        stack = jnp.concatenate([keys * mask for mask in key_masks], 0)
        query = jnp.concatenate([jnp.zeros((pad, slots), f32), natural_t[:width]], 0).astype(bf16)
        scores = dot_nn(stack, query) * depth ** (-0.5)
        out = [None] * 8
        for pair in range(4):
            word = edge_sums[group * 4 + pair]
            head = group * 8 + pair
            spatial_word = lanes_gather(
                jnp.broadcast_to(packed[head : head + 1], (slots, 128)), bucket
            )
            low = (word << 16) >> 16
            spatial_low = (spatial_word << 16) >> 16
            high = (word - low) >> 16
            spatial_high = (spatial_word - spatial_low) >> 16
            for part, spatial_part, spot in ((low, spatial_low, pair), (high, spatial_high, pair + 4)):
                pair_bias = part.astype(f32) * (1.0 / (edge_unit * hops))
                pair_bias = pair_bias + spatial_part.astype(f32) * (1.0 / spatial_unit)
                score = scores[spot * slots : (spot + 1) * slots] + pair_bias
                score = jnp.where(hidden_key, masked_score, score)
                weight = jnp.exp(score - jnp.max(score, axis=0, keepdims=True))
                probs = weight * (1.0 / column_sum(weight))
                probs_out[group * 8 + spot] = probs
                values = natural_t[2 * width + spot * depth : 2 * width + (spot + 1) * depth]
                out[spot] = dot_nn(values.astype(bf16), probs.astype(bf16))
        gap = jnp.zeros((pad, slots), f32)
        att_low[group] = jnp.concatenate(out + [gap], 0).T.astype(bf16)
        high_form = jnp.concatenate([gap] + out, 0).T.astype(bf16)
        mid[...] += dot_nt(high_form, weights[group, :, 3 * width - pad : 4 * width])
    normed, scale = normalize(mid[...])
    h2[...] = (normed * as_row(gain) + as_row(bias)).astype(bf16)


def attend(place, counts, h1, edge_sums, buckets, spatial_table, layer_in, o_bias, gain, bias, parts):
    slots, features = h1.shape
    width = parts[0].shape[-1] // 4
    heads = spatial_table.shape[1]
    groups = heads // 8
    return pl.pallas_call(
        functools.partial(attend_kernel, len(parts)),
        out_shape=(
            shape((groups, features, 4 * width), bf16),
            shape((groups, 1, 4 * width), f32),
            shape((groups, 2 * width, slots), bf16),
            shape((groups, slots, 256), bf16),
            shape((heads, slots, slots), f32),
            shape((groups, slots, 256), bf16),
            shape((slots, features), f32),
            shape((slots, features), bf16),
        ),
        in_specs=[smem, smem] + [vmem] * (8 + len(parts)),
        out_specs=[vmem] * 8,
        cost_estimate=cost(7),
        compiler_params=params(28),
        name="attend",
    )(
        place, counts, h1, edge_sums, buckets, spatial_table, layer_in, o_bias, gain, bias,
        *parts,
    )


def group_order(place):
    return [
        (theirs, y, y * 2 + (place[3] ^ theirs)) for theirs in (1, 0) for y in (0, 1)
    ]


def feed_kernel(
    n_parts, place, mid, h2, weights_a, biases, out_bias, gain, cotangent, att_low, probs_in, *refs
):
    parts = refs[:n_parts]
    layer_out, grad_mid, grad_att_t, grad_values, mine, theirs, rows_t, sums, weights = refs[n_parts:]
    assemble(place, parts, weights)
    slots, features = mid.shape
    width = biases.shape[2] // 4
    depth = width // 8
    pad = 256 - width
    lanes = lax.broadcasted_iota(i32, (1, 256), 1)
    cot = cotangent[...]
    grad_ffn = cot.astype(bf16)
    h2_value = h2[...]
    layer_out[...] = mid[...] + as_row(out_bias)
    grad_h2 = jnp.zeros((slots, features), f32)
    sums[...] = jnp.zeros_like(sums)
    order = group_order(place)
    for side, y, group in order:
        columns = theirs if side else mine
        in_bias = jnp.concatenate(
            [biases[group, 0:1, 2 * width : 3 * width], jnp.zeros((1, pad), f32)], 1
        )
        pre = dot_nn(h2_value, weights[group, :, :256]) + in_bias
        cdf = 0.5 * (1.0 + lax.erf(pre * (0.5**0.5)))
        slope = cdf + pre * jnp.exp(-0.5 * pre * pre) * 0.3989422804014327
        hidden = pltpu.roll(pre * cdf, pad, 1)
        hidden = jnp.where(lanes >= pad, hidden, 0.0).astype(bf16)
        layer_out[...] += dot_nt(hidden, weights[group, :, width - pad : 2 * width])
        grad_hidden = dot_nn(grad_ffn, weights[group, :, width - pad : 2 * width])
        grad_hidden = pltpu.roll(grad_hidden, width, 1)
        grad_pre = jnp.where(lanes < width, grad_hidden * slope, 0.0).astype(bf16)
        grad_h2 = grad_h2 + dot_nt(grad_pre, weights[group, :, :256])
        columns[y, :, 0:256] = grad_pre
        columns[y, :, 256:512] = hidden
        columns[y, :, 512:768] = att_low[group]
        sums[pl.ds(12 + group, 1), 0:256] = column_sum(grad_pre.astype(f32))
    normed, scale = normalize(mid[...])
    grad = cot + normalize_back(grad_h2 * as_row(gain), normed, scale)
    grad_mid[...] = grad
    branch = grad.astype(bf16)
    sums[2:3, :] = column_sum(grad)
    sums[3:4, :] = column_sum(grad_h2 * normed)
    sums[4:5, :] = column_sum(grad_h2)
    sums[5:6, :] = column_sum(cot)
    rows_t[0] = h2_value.astype(f32).T.astype(bf16)
    rows_t[1] = grad.T.astype(bf16)
    gap = jnp.zeros((pad, slots), f32)
    for side, y, group in order:
        columns = theirs if side else mine
        grad_att = dot_nn(branch, weights_a[group]).T[pad:]
        grad_att_t[group] = jnp.concatenate([grad_att, gap], 0).astype(bf16)
        out = []
        for head in range(8):
            out.append(
                dot_nt(
                    grad_att[head * depth : (head + 1) * depth].astype(bf16),
                    probs_in[group * 8 + head].astype(bf16),
                )
            )
        low_form = jnp.concatenate(out + [gap], 0).T.astype(bf16)
        grad_values[group] = low_form
        columns[y, :, 768:1024] = jnp.concatenate([gap] + out, 0).T.astype(bf16)
        sums[pl.ds(8 + group, 1), 512:768] = column_sum(low_form.astype(f32))


def feed(place, mid, h2, weights_a, biases, out_bias, gain, cotangent, att_low, probs, parts):
    slots, features = mid.shape
    groups, width = biases.shape[0], biases.shape[2] // 4
    whole = lambda array: pl.BlockSpec(array.shape, lambda i: (0,) * len(array.shape))
    outs = (
        shape((slots, features), f32),
        shape((slots, features), f32),
        shape((groups, 256, slots), bf16),
        shape((groups, slots, 256), bf16),
        shape((2, slots, 1024), bf16),
        shape((2, slots, 1024), bf16),
        shape((2, features, slots), bf16),
        shape((16, features), f32),
    )
    rest = (biases, out_bias, gain, cotangent, att_low, probs)
    return pl.pallas_call(
        functools.partial(feed_kernel, len(parts)),
        grid=(1,),
        out_shape=outs,
        in_specs=[
            smem,
            whole(mid),
            whole(h2),
            pl.BlockSpec((groups, features, 256), lambda i: (0, 0, 2)),
        ]
        + [whole(a) for a in rest + tuple(parts)],
        out_specs=[whole(out) for out in outs],
        scratch_shapes=[pltpu.VMEM((groups, features, 2 * width), bf16)],
        cost_estimate=cost(7),
        compiler_params=params(32),
        name="feed",
    )(place, mid, h2, weights_a, *rest, *parts)


def attend_back_kernel(
    place, probs_in, value_win, transposed, grad_att_t, grad_values, weights, layer_in, gain, grad_mid,
    sums_in, after, score_grads, mine, theirs, grad_in, sums,
):
    slots, features = layer_in.shape
    width = transposed.shape[1] // 2
    depth = width // 8
    value_masks = head_masks(256, 0, depth)
    grad_h1 = jnp.zeros((slots, features), f32)
    sums[...] = sums_in[...]
    scale = depth ** (-0.5)
    for side, y, group in group_order(place):
        columns = theirs if side else mine
        values = value_win[group]
        stack = jnp.concatenate([values * mask for mask in value_masks], 0)
        grad_probs = dot_nn(stack, grad_att_t[group])
        held = transposed[group].astype(f32)
        query_out, key_out, score_out = [], [], []
        for head in range(8):
            probs = probs_in[group * 8 + head]
            part = probs * grad_probs[head * slots : (head + 1) * slots]
            exact = part - probs * column_sum(part)
            grads = exact.astype(bf16)
            score_out.append(exact)
            key_rows = held[width + head * depth : width + (head + 1) * depth]
            query_out.append(dot_nn(key_rows.astype(bf16), grads) * scale)
            query_rows = held[head * depth : (head + 1) * depth]
            key_out.append(dot_nt(query_rows.astype(bf16), grads) * scale)
        score_grads[group] = jnp.swapaxes(jnp.stack(score_out), 0, 1)
        natural = jnp.concatenate(query_out + key_out, 0).T.astype(bf16)
        columns[y] = natural
        grad_h1 = grad_h1 + dot_nt(natural, weights[group, :, : 2 * width])
        grad_h1 = grad_h1 + dot_nt(grad_values[group], weights[group, :, 2 * width : 2 * width + 256])
        sums[pl.ds(8 + group, 1), 0 : 2 * width] = column_sum(natural.astype(f32))
    normed, inverse = normalize(layer_in[...])
    grad_in[...] = grad_mid[...] + normalize_back(grad_h1 * as_row(gain), normed, inverse)
    sums[0:1, :] = column_sum(grad_h1 * normed)
    sums[1:2, :] = column_sum(grad_h1)


def attend_back(
    place, probs, value_win, transposed, grad_att_t, grad_values, weights, layer_in, gain, grad_mid, sums, after
):
    slots, features = layer_in.shape
    groups = transposed.shape[0]
    width = transposed.shape[1] // 2
    return pl.pallas_call(
        attend_back_kernel,
        out_shape=(
            shape((groups, slots, 8, slots), f32),
            shape((2, slots, 2 * width), bf16),
            shape((2, slots, 2 * width), bf16),
            shape((slots, features), f32),
            shape(sums.shape, f32),
        ),
        in_specs=[smem] + [vmem] * 10 + [untouched],
        out_specs=[vmem] * 5,
        cost_estimate=cost(7),
        compiler_params=params(24),
        name="attend_back",
    )(
        place, probs, value_win, transposed, grad_att_t, grad_values, weights, layer_in, gain, grad_mid,
        sums, after,
    )


def weight_grads_kernel(plan, n_rows, place, columns_own, columns_other, *refs):
    own_rows, other_rows = refs[:n_rows], refs[n_rows : 2 * n_rows]
    own, across, over, both, rows_t = refs[2 * n_rows :]
    kind = 0
    for mine, other in zip(own_rows, other_rows):
        slots = mine.shape[2]
        for i in range(mine.shape[0]):
            rows_t[kind, :, 0:slots] = mine[i]
            rows_t[kind, :, slots : 2 * slots] = other[i]
            kind += 1
    core = place[3]
    height = own.shape[1]
    for which, out in ((3, both), (2, over), (1, across), (0, own)):
        y = relative(place, core, which, 0)[1] >> 1
        right = jnp.concatenate([columns_own[y], columns_other[y]], 0)
        for step in range(4):
            row = relative(place, core, which, step)[0]
            start = pl.multiple_of(row * height, height)
            out[step] = plan(lambda kind: rows_t[kind, pl.ds(start, height), :], right).astype(bf16)


def plan_first(rows_of, right):
    return dot_nn(rows_of(0), right)


def plan_second(rows_of, right):
    grad_in = dot_nn(rows_of(2), right[:, 0:256])
    grad_out = dot_nn(rows_of(1), right[:, 256:512])
    grad_o = dot_nn(rows_of(3), right[:, 512:768])
    grad_v = dot_nn(rows_of(0), right[:, 768:1024])
    return jnp.concatenate(
        [
            grad_in[:, :128],
            grad_in[:, 128:] + grad_out[:, :128],
            grad_out[:, 128:],
            grad_o[:, :128],
            grad_o[:, 128:] + grad_v[:, :128],
            grad_v[:, 128:],
        ],
        1,
    )


def weight_grads(plan, place, columns_own, columns_other, own_rows, other_rows, height, lanes, microseconds):
    features, slots = own_rows[0].shape[1:]
    kinds = sum(rows.shape[0] for rows in own_rows)
    out = shape((4, height, lanes), bf16)
    return pl.pallas_call(
        functools.partial(weight_grads_kernel, plan, len(own_rows)),
        out_shape=(out,) * 4,
        in_specs=[smem] + [vmem] * (2 + 2 * len(own_rows)),
        out_specs=[vmem] * 4,
        scratch_shapes=[pltpu.VMEM((kinds, features, 2 * slots), bf16)],
        cost_estimate=cost(microseconds),
        compiler_params=params(20),
        name="weight_grads",
    )(place, columns_own, columns_other, *own_rows, *other_rows)


def table_kernel(digit, staged, span, place, grads, ids, buckets, sums, after, *refs):
    if staged:
        mine, theirs, small, total, spatial = refs
    else:
        total, spatial = refs
    hops = ids.shape[0]
    groups = grads.shape[0]
    heads = groups * 8
    high_count = total.shape[0] // heads
    total[...] = jnp.zeros_like(total)
    spatial[...] = jnp.zeros_like(spatial)
    digits = lax.broadcasted_iota(i32, (digit, 128), 0).astype(f32).astype(bf16)
    kinds = lax.broadcasted_iota(i32, (heads, 128), 0).astype(f32).astype(bf16)
    one = jnp.ones((), bf16)
    zero = jnp.zeros((), bf16)

    def body(i, carry):
        lefts, rights, plain, kind_rights = [], [], [], []
        for j in range(span):
            row = i * span + j
            piece = jnp.concatenate([grads[group, row] for group in range(groups)], 0).astype(bf16)
            bucket = buckets[pl.ds(row, 1), :].astype(f32).astype(bf16)
            plain.append(piece)
            kind_rights.append(jnp.where(jnp.broadcast_to(bucket, (heads, 128)) == kinds, one, zero))
            for hop in range(hops):
                value = ids[hop, pl.ds(row, 1), :].astype(f32)
                high = jnp.floor((value + 0.5) * (1.0 / digit))
                low = value - high * digit
                low = jnp.broadcast_to(low.astype(bf16), (digit, 128))
                high = jnp.broadcast_to(high.astype(bf16), (heads, 128))
                rights.append(jnp.where(low == digits, one, zero))
                lefts.append(
                    jnp.concatenate(
                        [jnp.where(high == jnp.full((), k, bf16), piece, zero) for k in range(high_count)], 0
                    )
                )
        total[...] += dot_nt(jnp.concatenate(lefts, 1), jnp.concatenate(rights, 1))
        spatial[...] += dot_nt(jnp.concatenate(plain, 1), jnp.concatenate(kind_rights, 1))
        return carry

    lax.fori_loop(0, grads.shape[1] // span, body, 0)
    if staged:
        core = place[3]
        for other, out in ((0, mine), (1, theirs)):
            for which in range(4):
                pieces = []
                for step in range(4):
                    row, column = relative(place, core ^ other, which, step)
                    start = pl.multiple_of(row * heads + column * 8, 8)
                    pieces.append(total[pl.ds(start, 8), :] * (1.0 / hops))
                out[which * 8 : (which + 1) * 8, :] = jnp.concatenate(pieces, 1)
        spread = []
        for group in range(4):
            spread += [spatial[group * 8 : (group + 1) * 8, :], jnp.zeros((8, 128 - heads), f32)]
        lanes = sums.shape[1]
        spread.append(jnp.zeros((8, lanes - 512), f32))
        spread = jnp.concatenate(spread, 1)
        small[0:16, :] = sums[...]
        small[16:24, :] = spread
        theirs[32:48, :] = sums[...]
        theirs[48:56, :] = spread


def table_grads(place, grads, ids, buckets, sums, after, digit, edges, staged):
    heads = grads.shape[0] * 8
    total = (edges // digit * heads, digit)
    lanes = sums.shape[1]
    outs = (shape((32, lanes), f32), shape((56, lanes), f32), shape((24, lanes), f32))
    inner = (shape(total, f32), shape((heads, heads), f32))
    return pl.pallas_call(
        functools.partial(table_kernel, digit, staged, 8),
        out_shape=outs if staged else inner,
        in_specs=[smem] + [vmem] * 4 + [untouched],
        out_specs=[vmem] * (3 if staged else 2),
        scratch_shapes=[pltpu.VMEM(a.shape, f32) for a in inner] if staged else [],
        cost_estimate=cost(15),
        compiler_params=params(12),
        name="table_grads",
    )(place, grads, ids, buckets, sums, after)


def meet_core_kernel(mine, small, got, out, keep):
    keep[...] = mine[0:16, :] + got[0:16, :]
    out[0:8, :] = mine[24:32, :] + got[24:32, :]
    out[8:16, :] = mine[16:24, :] + got[16:24, :]
    out[16:40, :] = small[...] + got[32:56, :]


def meet_second_kernel(keep, sent, got, out, kept):
    out[0:8, :] = keep[8:16, :] + got[0:8, :]
    out[8:32, :] = sent[16:40, :] + got[16:40, :]
    kept[...] = keep[0:8, :] + got[8:16, :]


def meet_first_kernel(kept, sent, got, *outs):
    own = kept[...] + got[0:8, :]
    small = sent[8:32, :] + got[8:32, :]
    digit = own.shape[1] // 4
    for step, out in enumerate(outs):
        out[0:8, 0:digit] = own[:, step * digit : (step + 1) * digit]
        out[0:8, digit:] = jnp.zeros((8, 3 * digit), f32)
        out[8:32, :] = small


def finish_kernel(place, own, first, second, third, edge, spatial, *outs):
    total = own[...] + first[...] + second[...] + third[...]
    digit = edge.shape[1]
    edge[...] = total[0:8, 0:digit]
    group = place[4]
    for i, out in enumerate(outs[:6]):
        out[...] = total[8 + i : 9 + i, :].reshape(out.shape)
    width = outs[6].shape[0]
    heads = total[16:17]
    hidden = total[20:21]
    kinds = total[24:32, 0:128]
    for other in range(1, 4):
        heads = jnp.where(group == other, total[16 + other : 17 + other], heads)
        hidden = jnp.where(group == other, total[20 + other : 21 + other], hidden)
        kinds = jnp.where(group == other, total[24:32, other * 128 : (other + 1) * 128], kinds)
    outs[6][...] = heads[:, :width].reshape(outs[6].shape)
    outs[7][...] = heads[:, 512 : 512 + width].reshape(outs[7].shape)
    outs[8][...] = hidden[:, :width].reshape(outs[8].shape)
    spatial[...] = kinds[:, : spatial.shape[1]]


def small_call(kernel, name, outs, *args):
    return pl.pallas_call(
        kernel,
        out_shape=outs,
        in_specs=[smem if args[i].ndim == 1 else vmem for i in range(len(args))],
        out_specs=[vmem] * len(outs),
        cost_estimate=cost(0.7),
        compiler_params=params(4),
        name=name,
    )(*args)


class Links:
    def __init__(self):
        self.core = self.hop(lambda z, x, y, c: (z, x, y, 1 - c))
        self.first = self.hop(lambda z, x, y, c: (z, x, 1 - y, c) if c else (z, 1 - x, y, c))
        self.second = self.hop(lambda z, x, y, c: (z, 1 - x, y, c) if c else (z, x, 1 - y, c))
        self.along_x = self.hop(lambda z, x, y, c: (z, 1 - x, y, c))
        self.along_y = self.hop(lambda z, x, y, c: (z, x, 1 - y, c))
        self.along_z = [self.hop(lambda z, x, y, c, k=k: (z ^ k, x, y, c)) for k in (1, 2, 3)]

    def hop(self, move):
        index = lambda z, x, y, c: (z * 2 + x) * 4 + y * 2 + c
        spots = [(z, x, y, c) for z in range(4) for x in range(2) for y in range(2) for c in range(2)]
        return [(index(*spot), index(*move(*spot))) for spot in spots]


def send(values, hop):
    return lax.ppermute(values, ("dp", "mp"), hop)


def around(links, own):
    return [own] + [send(own, hop) for hop in links.along_z]


def spread(links, stack):
    across = send(stack, links.first)
    over = send(stack, links.second)
    both = send(across, links.second)
    mine = (stack, across, over, both)
    return mine + tuple(send(part, links.core) for part in mine)


def add_rounded(*terms):
    total = terms[0].astype(f32)
    for term in terms[1:]:
        total = total + term.astype(f32)
    return total.astype(bf16)


def reduce_staged(links, own, across, over, both):
    across = add_rounded(across, send(both, links.second))
    own = add_rounded(own, send(over, links.second), send(across, links.first))
    total = own[0].astype(f32)
    for step, hop in enumerate(links.along_z):
        total = total + send(own[step + 1], hop).astype(f32)
    return total


def local(
    layer_in,
    node_counts,
    spatial_ids,
    path_ids,
    ln1_gain,
    ln1_bias,
    w_q,
    w_k,
    w_v,
    q_bias,
    v_bias,
    spatial_table,
    edge_table,
    w_o,
    o_bias,
    ln2_gain,
    ln2_bias,
    w_in,
    in_bias,
    w_out,
    out_bias,
    cotangent,
):
    dp_size, mp_size = lax.axis_size("dp"), lax.axis_size("mp")
    dp_index, mp_index = lax.axis_index("dp"), lax.axis_index("mp")
    staged = dp_size == 8 and mp_size == 4
    height, width = w_q.shape
    features = layer_in.shape[1]
    edges = edge_table.shape[0] * dp_size
    heads = spatial_table.shape[1]
    kinds = spatial_table.shape[0]
    hops = path_ids.shape[1]
    share = edges // 4
    digit = edges // 8
    place = jnp.stack([dp_index // 2, dp_index % 2, mp_index // 2, mp_index % 2, mp_index]).astype(i32)
    ids, buckets, h1, rows_early = prepare(
        place, spatial_ids, path_ids, layer_in, ln1_gain, ln1_bias, cotangent, kinds - 1
    )
    if staged:
        links = Links()
        first, own_biases = pack_first(w_q, w_k, w_v, w_o, q_bias, v_bias, in_bias)
        table_t = edge_table.T
        second = pack_second(place, w_in, w_out, table_t, send(table_t, links.along_x))
        parts_a = spread(links, jnp.concatenate(around(links, first) + [own_biases], 0))
        chunks = around(links, second)
        parts_b = spread(links, jnp.concatenate([chunk[:height] for chunk in chunks], 0))
        lookup_place = place
    else:
        gathered = [
            lax.all_gather(lax.all_gather(w, "dp", axis=0, tiled=True), "mp", axis=0)
            for w in (w_q, w_k, w_v, w_o, w_in, w_out)
        ]
        bias_row = jnp.concatenate([q_bias, v_bias, in_bias, jnp.zeros((width,), f32)])
        bias_row = lax.all_gather(bias_row[None], "mp", axis=0)
        parts_a = (jnp.concatenate(gathered[:4], 2), bias_row)
        parts_b = (jnp.concatenate(gathered[4:], 2),)
        table_t = lax.all_gather(edge_table, "dp", axis=0, tiled=True).T
        chunks = [table_t[:, i * share : (i + 1) * share] for i in range(4)]
        lookup_place = jnp.zeros((5,), i32)
    edge_sums = None
    for step in range(4):
        edge_sums = lookup(lookup_place, chunks[step], ids, edge_sums, step, heads)

    weights, biases, transposed, value_win, probs, att_low, mid, h2 = attend(
        place, node_counts, h1, edge_sums, buckets, spatial_table,
        layer_in, o_bias, ln2_gain, ln2_bias, parts_a,
    )
    layer_out, grad_mid, grad_att_t, grad_values, mine_b, theirs_b, rows_late, sums = feed(
        place, mid, h2, weights, biases, out_bias, ln2_gain, cotangent, att_low, probs, parts_b
    )
    after = sums
    if staged:
        rows_b = (rows_early, rows_late)
        other_rows_b = tuple(send(rows, links.core) for rows in rows_b)
        pieces_b = weight_grads(
            plan_second, place, mine_b, send(theirs_b, links.core), rows_b, other_rows_b, height, 4 * width, 4
        )
        grads_b = reduce_staged(links, *pieces_b)
        after = pieces_b[0]
    score_grads, mine_a, theirs_a, grad_layer_in, sums = attend_back(
        place, probs, value_win, transposed, grad_att_t, grad_values, weights,
        layer_in, ln1_gain, grad_mid, sums, after,
    )
    if staged:
        pieces_a = weight_grads(
            plan_first, place, mine_a, send(theirs_a, links.core),
            (rows_early[0:1],), (other_rows_b[0][0:1],), height, 2 * width, 2,
        )
        grads_a = reduce_staged(links, *pieces_a)
        mine, theirs, small = table_grads(
            place, score_grads, ids, buckets, sums, pieces_a[0], digit, edges, True
        )
        sent, keep = small_call(
            meet_core_kernel, "meet_core", (shape((40, features), f32), shape((16, features), f32)),
            mine, small, send(theirs, links.core),
        )
        sent, keep = small_call(
            meet_second_kernel, "meet_second", (shape((32, features), f32), shape((8, features), f32)),
            keep, sent, send(sent, links.second),
        )
        outs = small_call(
            meet_first_kernel, "meet_first", (shape((32, features), f32),) * 4,
            keep, sent, send(sent, links.first),
        )
        got = [send(out, hop) for out, hop in zip(outs[1:], links.along_z)]
        grad_edge, grad_spatial, *rows = small_call(
            finish_kernel, "finish",
            (shape((8, digit), f32), shape((8, kinds), f32))
            + (shape((features,), f32),) * 6
            + (shape((width,), f32),) * 3,
            place, outs[0], *got,
        )
        grad_edge = grad_edge.T
        grad_spatial = grad_spatial.T
        grad_w_q, grad_w_k = (grads_a[:, i * width : (i + 1) * width] for i in range(2))
        grad_w_in, grad_w_out, grad_w_o, grad_w_v = (
            grads_b[:, i * width : (i + 1) * width] for i in range(4)
        )
    else:
        contract = lambda a, b: lax.dot_general(
            a, b, (((1,), (1,)), ((), ())), preferred_element_type=f32
        )

        def unmix(mine, theirs):
            even = mp_index % 2 == 0
            cores = jnp.where(even, jnp.stack([mine, theirs], 1), jnp.stack([theirs, mine], 1))
            return cores.reshape(4, *mine.shape[1:])

        def scatter(rows_t, columns):
            grads = contract(rows_t, columns)
            grads = jnp.transpose(grads, (1, 0, 2))
            grads = lax.psum_scatter(grads, "mp", scatter_dimension=0, tiled=False)
            return lax.psum_scatter(grads, "dp", scatter_dimension=0, tiled=True)

        columns_a, columns_b = unmix(mine_a, theirs_a), unmix(mine_b, theirs_b)
        grad_w_q, grad_w_k = (
            scatter(rows_early[0], columns_a[:, :, i * width : (i + 1) * width]) for i in range(2)
        )
        grad_w_v = scatter(rows_early[0], columns_b[:, :, 1024 - width :])
        grad_w_in = scatter(rows_late[0], columns_b[:, :, :width])
        grad_w_out = scatter(rows_early[1], columns_b[:, :, 512 - width : 512])
        grad_w_o = scatter(rows_late[1], columns_b[:, :, 512 : 512 + width])
        table, spatial = table_grads(place, score_grads, ids, buckets, sums, sums, digit, edges, False)
        table = table.reshape(-1, heads, digit).transpose(0, 2, 1).reshape(edges, heads) / hops
        table = lax.psum_scatter(table, "dp", scatter_dimension=0, tiled=True)
        table = lax.psum(table, "mp")
        grad_edge = lax.dynamic_slice_in_dim(table, mp_index * 8, 8, 1)
        totals, spatial = lax.psum((sums, spatial), ("dp", "mp"))
        grad_spatial = lax.dynamic_slice_in_dim(spatial[:, :kinds], mp_index * 8, 8, 0).T
        head_sums = lax.dynamic_slice_in_dim(totals, 8 + mp_index, 1, 0)[0]
        hidden_sums = lax.dynamic_slice_in_dim(totals, 12 + mp_index, 1, 0)[0]
        rows = [totals[i] for i in range(6)]
        rows += [head_sums[:width], head_sums[512 : 512 + width], hidden_sums[:width]]
    return (
        layer_out,
        grad_layer_in,
        rows[0],
        rows[1],
        grad_w_q,
        grad_w_k,
        grad_w_v,
        rows[6],
        rows[7],
        grad_spatial,
        grad_edge,
        grad_w_o,
        rows[2],
        rows[3],
        rows[4],
        grad_w_in,
        rows[8],
        grad_w_out,
        rows[5],
    )


def solution(mesh):
    return jax.shard_map(
        local,
        mesh=mesh,
        in_specs=(
            P(("dp", "mp"), None),
            P("dp"),
            P("dp", None, None),
            P("dp", None, None, None),
            P(),
            P(),
            P("dp", "mp"),
            P("dp", "mp"),
            P("dp", "mp"),
            P("mp"),
            P("mp"),
            P(),
            P("dp", None),
            P("dp", "mp"),
            P(),
            P(),
            P(),
            P("dp", "mp"),
            P("mp"),
            P("dp", "mp"),
            P(),
            P(("dp", "mp"), None),
        ),
        out_specs=(
            P(("dp", "mp"), None),
            P(("dp", "mp"), None),
            P(),
            P(),
            P("dp", "mp"),
            P("dp", "mp"),
            P("dp", "mp"),
            P("mp"),
            P("mp"),
            P(None, "mp"),
            P("dp", "mp"),
            P("dp", "mp"),
            P(),
            P(),
            P(),
            P("dp", "mp"),
            P("mp"),
            P("dp", "mp"),
            P(),
        ),
        check_vma=False,
    )
```

```python
import functools

import jax
import jax.numpy as jnp
from jax import lax
from jax.experimental import pallas as pl
from jax.experimental.pallas import tpu as pltpu
from jax.sharding import PartitionSpec as P

epsilon = 1e-05
masked_score = -1e30
edge_unit = 1638.0
spatial_unit = 4096.0
hurry = 0.1
bf16 = jnp.bfloat16
f32 = jnp.float32
i32 = jnp.int32
vmem = pl.BlockSpec(memory_space=pltpu.VMEM)
smem = pl.BlockSpec(memory_space=pltpu.SMEM)
hbm = pl.BlockSpec(memory_space=pltpu.HBM)
untouched = pl.BlockSpec(memory_space=pl.ANY)


def params(mebibytes):
    return pltpu.CompilerParams(vmem_limit_bytes=mebibytes << 20)


def normalize(values):
    centred = values - jnp.mean(values, axis=-1, keepdims=True)
    scale = lax.rsqrt(jnp.mean(centred * centred, axis=-1, keepdims=True) + epsilon)
    return (centred * scale, scale)


def normalize_back(grad_normed, normed, scale):
    inner = grad_normed - jnp.mean(grad_normed, axis=-1, keepdims=True)
    inner = inner - normed * jnp.mean(grad_normed * normed, axis=-1, keepdims=True)
    return inner * scale


def dot_nn(left, right):
    return lax.dot_general(
        left, right, (((1,), (0,)), ((), ())), preferred_element_type=f32
    )


def dot_nt(left, right):
    return lax.dot_general(
        left, right, (((1,), (1,)), ((), ())), preferred_element_type=f32
    )


def column_sum(values):
    return jnp.sum(values, axis=0, keepdims=True)


def cost(microseconds):
    return pl.CostEstimate(flops=int(microseconds * hurry * 1.15e9), bytes_accessed=1024, transcendentals=0)


def as_row(ref):
    return ref[...].reshape(1, -1)


def shape(dims, kind):
    return jax.ShapeDtypeStruct(dims, kind)


def relative(place, side, which, step):
    z, x, y = place[0], place[1], place[2]
    flip_x = (0, 1 - side, side, 1)[which]
    flip_y = (0, side, 1 - side, 1)[which]
    row = (z ^ step) * 2 + (x ^ flip_x)
    column = (y ^ flip_y) * 2 + side
    return row, column


def three_terms(values):
    terms = []
    for _ in range(3):
        term = values.astype(bf16)
        terms.append(term)
        values = values - term.astype(f32)
    return terms


def pack_first_kernel(place, wq, wk, wv, wo, bq, bv, bi, edge, neighbour, after, weights, biases, held, sems):
    copies = [
        pltpu.make_async_copy(source, held.at[i], sems.at[i]) for i, source in enumerate((wq, wk, wv, wo))
    ]
    for copy in copies:
        copy.start()
    row = jnp.concatenate([as_row(bq), as_row(bv), as_row(bi)], 1)
    lanes = weights.shape[1]
    row = jnp.concatenate([row, jnp.zeros((1, lanes - row.shape[1]), f32)], 1)
    terms = [term.astype(f32) for term in three_terms(row)]
    biases[...] = jnp.concatenate(terms + [jnp.zeros((13, lanes), f32)], 0).astype(bf16)
    even = place[1] == 0
    mine, other = edge[...].astype(f32), neighbour[...].astype(f32)
    low, high = jnp.where(even, mine, other), jnp.where(even, other, mine)
    rows = held.shape[1]
    half = low.shape[0] // 2
    weights[rows:, :] = jnp.concatenate([low[:half], low[half:], high[:half], high[half:]], 1).astype(bf16)
    for copy in copies:
        copy.wait()
    weights[0:rows, :] = jnp.concatenate([held[i] for i in range(4)], 1)


def pack_first(place, wq, wk, wv, wo, bq, bv, bi, edge, neighbour, after):
    rows, width = wq.shape
    return pl.pallas_call(
        pack_first_kernel,
        out_shape=(shape((rows + 16, 4 * width), bf16), shape((16, 4 * width), bf16)),
        in_specs=[smem] + [hbm] * 4 + [vmem] * 5 + [untouched],
        out_specs=[vmem] * 2,
        scratch_shapes=[pltpu.VMEM((4, rows, width), bf16), pltpu.SemaphoreType.DMA((4,))],
        cost_estimate=cost(2),
        compiler_params=params(60),
        name="pack_first",
    )(place, wq, wk, wv, wo, bq, bv, bi, edge, neighbour, after)


def pack_second_kernel(wi, wu, out):
    out[...] = jnp.concatenate([wi[...], wu[...]], 1)


def pack_second(wi, wu):
    rows, width = wi.shape
    return pl.pallas_call(
        pack_second_kernel,
        out_shape=shape((rows, 2 * width), bf16),
        in_specs=[vmem] * 2,
        out_specs=vmem,
        cost_estimate=cost(1),
        compiler_params=params(60),
        name="pack_second",
    )(wi, wu)


def prepare_kernel(virtual, place, spatial, path, layer_in, gain, bias, cotangent, ids, buckets, h1, rows_t):
    slots = spatial.shape[1]
    for hop in range(path.shape[1]):
        ids[hop] = path[0, hop].T
    rows = lax.broadcasted_iota(i32, (slots, slots), 0)
    columns = lax.broadcasted_iota(i32, (slots, slots), 1)
    buckets[...] = jnp.where((rows == 0) | (columns == 0), virtual, spatial[0].T)
    normed, scale = normalize(layer_in[...])
    out = normed * as_row(gain) + as_row(bias)
    h1[...] = out.astype(bf16)
    rows_t[0] = out.T.astype(bf16)
    rows_t[1] = cotangent[...].T.astype(bf16)


def prepare(place, spatial, path, layer_in, gain, bias, cotangent, virtual):
    hops, slots = path.shape[1], path.shape[2]
    rows, width = layer_in.shape
    whole = lambda dims: pl.BlockSpec(dims, lambda i, s: (0,) * len(dims))
    return pl.pallas_call(
        functools.partial(prepare_kernel, virtual),
        grid_spec=pltpu.PrefetchScalarGridSpec(
            num_scalar_prefetch=1,
            grid=(1,),
            in_specs=[
                pl.BlockSpec((1, slots, slots), lambda i, s: (s[4], 0, 0)),
                pl.BlockSpec((1, hops, slots, slots), lambda i, s: (s[4], 0, 0, 0)),
                whole((rows, width)),
                whole((width,)),
                whole((width,)),
                whole((rows, width)),
            ],
            out_specs=[
                whole((hops, slots, slots)),
                whole((slots, slots)),
                whole((rows, width)),
                whole((2, width, rows)),
            ],
        ),
        out_shape=(
            shape((hops, slots, slots), i32),
            shape((slots, slots), i32),
            shape((rows, width), bf16),
            shape((2, width, rows), bf16),
        ),
        compiler_params=params(62),
        cost_estimate=cost(1),
        name="prepare",
    )(place, spatial, path, layer_in, gain, bias, cotangent)


def quantize(table, unit):
    held = jnp.round(table.astype(f32) * unit).astype(i32)
    partner = jnp.concatenate([held[4:], held[:4]], 0)
    return held + partner * 65536


def lanes_gather(table, places):
    return jnp.take_along_axis(table, places, axis=1, mode="promise_in_bounds")


def lookup_kernel(first, step, share, place, chunk, ids, *refs):
    total, table = refs[-2:]
    previous = None if first else refs[0]
    hops, slots = ids.shape[0], ids.shape[1]
    pairs = total.shape[0]
    below = chunk[chunk.shape[0] - 16 :, :]
    half = share // 2
    below = [below[:, i * half : (i + 1) * half] for i in range(4)]
    packed = quantize(
        jnp.concatenate(
            [jnp.concatenate([below[0], below[2]], 1), jnp.concatenate([below[1], below[3]], 1)], 0
        ),
        edge_unit,
    )
    blocks = share // 128
    for pair in range(pairs):
        head = (pair // 4) * 8 + pair % 4
        for block in range(blocks):
            table[pair, block] = jnp.broadcast_to(
                packed[head : head + 1, block * 128 : (block + 1) * 128], (8, 128)
            )
    base = (place[0] ^ step) * share

    def body(i, carry):
        offset = pl.multiple_of(i * 8, 8)
        sums = [None] * pairs
        if not first:
            sums = [previous[pair, pl.ds(offset, 8), :] for pair in range(pairs)]
        for hop in range(hops):
            relative_id = ids[hop, pl.ds(offset, 8), :] - base
            low = relative_id & 127
            high = relative_id >> 7
            masks = [high == block for block in range(blocks)]
            for pair in range(pairs):
                value = jnp.zeros((8, 128), i32)
                for block in range(blocks):
                    value = jnp.where(masks[block], lanes_gather(table[pair, block], low), value)
                sums[pair] = value if sums[pair] is None else sums[pair] + value
        for pair in range(pairs):
            total[pair, pl.ds(offset, 8), :] = sums[pair]
        return carry

    lax.fori_loop(0, slots // 8, body, 0)


def lookup(place, chunk, ids, previous, step, heads, after=()):
    share = chunk.shape[1] // 2
    pairs = heads // 2
    slots = ids.shape[1]
    first = previous is None
    out = shape((pairs, slots, slots), i32)
    return pl.pallas_call(
        functools.partial(lookup_kernel, first, step, share),
        out_shape=out,
        in_specs=[smem] + [vmem] * (2 if first else 3) + [untouched] * len(after),
        out_specs=vmem,
        scratch_shapes=[pltpu.VMEM((pairs, share // 128, 8, 128), i32)],
        input_output_aliases={} if first else {3: 0},
        compiler_params=params(8),
        cost_estimate=cost(6),
        name="lookup",
    )(place, chunk, ids, *(() if first else (previous,)), *after)


def assemble(place, parts, whole, biases=None):
    if len(parts) <= 2:
        whole[...] = parts[0][...]
        return
    core = place[3]
    rows = whole.shape[1] // 8
    each = len(parts) // 2
    for other in range(2):
        for which in range(4):
            for step in range(4):
                row, column = relative(place, core ^ other, which, step)
                start = pl.multiple_of(row * rows, rows)
                part = parts[other * each + which // (4 // each)]
                at = (step * (4 // each) + which % (4 // each)) * rows
                whole[column, pl.ds(start, rows), :] = part[at : at + rows, :]
            if biases is not None:
                terms = parts[other * each + which][4 * rows : 4 * rows + 16, :].astype(f32)
                biases[column] = terms[0:1] + terms[1:2] + terms[2:3]


def head_masks(width, offset, depth):
    lanes = lax.broadcasted_iota(i32, (1, width), 1)
    out = []
    for head in range(8):
        start = offset + head * depth
        out.append(((lanes >= start) & (lanes < start + depth)).astype(f32).astype(bf16))
    return out


def attend_kernel(
    n_parts, place, counts, h1, edge_sums, buckets, spatial_table, layer_in, o_bias, gain, bias, *refs
):
    parts, refs = refs[:n_parts], refs[n_parts:]
    weights, biases, transposed, value_win, probs_out, att_low, mid, h2 = refs
    assemble(place, parts, weights, biases)
    if n_parts == 2:
        biases[...] = parts[1][...]
    slots = h1.shape[0]
    groups, width = biases.shape[0], biases.shape[2] // 4
    depth = width // 8
    pad = 256 - width
    hops = 5
    count = counts[place[4]]
    packed = quantize(spatial_table[...].astype(f32).T, spatial_unit)
    packed = jnp.concatenate([packed, jnp.zeros((packed.shape[0], 128 - packed.shape[1]), i32)], 1)
    hidden_key = lax.broadcasted_iota(i32, (slots, slots), 0) > count
    bucket = buckets[...]
    key_masks = head_masks(256, pad, depth)
    mid[...] = layer_in[...] + as_row(o_bias)
    for group in range(groups):
        natural = dot_nn(h1[...], weights[group, :, : 3 * width + pad])
        row_bias = jnp.concatenate(
            [
                biases[group, 0:1, :width],
                jnp.zeros((1, width), f32),
                biases[group, 0:1, width : 2 * width],
                jnp.zeros((1, pad), f32),
            ],
            1,
        )
        natural = natural + row_bias
        natural_t = natural.T
        transposed[group] = natural_t[: 2 * width].astype(bf16)
        natural = natural.astype(bf16)
        value_win[group] = natural[:, 2 * width : 2 * width + 256]
        keys = natural[:, width - pad : 2 * width]
        stack = jnp.concatenate([keys * mask for mask in key_masks], 0)
        query = jnp.concatenate([jnp.zeros((pad, slots), f32), natural_t[:width]], 0).astype(bf16)
        scores = dot_nn(stack, query) * depth ** (-0.5)
        out = [None] * 8
        for pair in range(4):
            word = edge_sums[group * 4 + pair]
            head = group * 8 + pair
            spatial_word = lanes_gather(
                jnp.broadcast_to(packed[head : head + 1], (slots, 128)), bucket
            )
            low = (word << 16) >> 16
            spatial_low = (spatial_word << 16) >> 16
            high = (word - low) >> 16
            spatial_high = (spatial_word - spatial_low) >> 16
            for part, spatial_part, spot in ((low, spatial_low, pair), (high, spatial_high, pair + 4)):
                pair_bias = part.astype(f32) * (1.0 / (edge_unit * hops))
                pair_bias = pair_bias + spatial_part.astype(f32) * (1.0 / spatial_unit)
                score = scores[spot * slots : (spot + 1) * slots] + pair_bias
                score = jnp.where(hidden_key, masked_score, score)
                weight = jnp.exp(score - jnp.max(score, axis=0, keepdims=True))
                probs = weight * (1.0 / column_sum(weight))
                probs_out[group * 8 + spot] = probs
                values = natural_t[2 * width + spot * depth : 2 * width + (spot + 1) * depth]
                out[spot] = dot_nn(values.astype(bf16), probs.astype(bf16))
        gap = jnp.zeros((pad, slots), f32)
        att_low[group] = jnp.concatenate(out + [gap], 0).T.astype(bf16)
        high_form = jnp.concatenate([gap] + out, 0).T.astype(bf16)
        mid[...] += dot_nt(high_form, weights[group, :, 3 * width - pad : 4 * width])
    normed, scale = normalize(mid[...])
    h2[...] = (normed * as_row(gain) + as_row(bias)).astype(bf16)


def attend(place, counts, h1, edge_sums, buckets, spatial_table, layer_in, o_bias, gain, bias, parts):
    slots, features = h1.shape
    width = parts[0].shape[-1] // 4
    heads = spatial_table.shape[1]
    groups = heads // 8
    return pl.pallas_call(
        functools.partial(attend_kernel, len(parts)),
        out_shape=(
            shape((groups, features, 4 * width), bf16),
            shape((groups, 1, 4 * width), f32),
            shape((groups, 2 * width, slots), bf16),
            shape((groups, slots, 256), bf16),
            shape((heads, slots, slots), f32),
            shape((groups, slots, 256), bf16),
            shape((slots, features), f32),
            shape((slots, features), bf16),
        ),
        in_specs=[smem, smem] + [vmem] * (8 + len(parts)),
        out_specs=[vmem] * 8,
        cost_estimate=cost(7),
        compiler_params=params(28),
        name="attend",
    )(
        place, counts, h1, edge_sums, buckets, spatial_table, layer_in, o_bias, gain, bias,
        *parts,
    )


def group_order(place):
    return [
        (theirs, y, y * 2 + (place[3] ^ theirs)) for theirs in (1, 0) for y in (0, 1)
    ]


def feed_kernel(
    n_parts, place, mid, h2, weights_a, biases, out_bias, gain, cotangent, att_low, probs_in, *refs
):
    parts = refs[:n_parts]
    layer_out, grad_mid, grad_att_t, grad_values, mine, theirs, rows_t, sums, weights = refs[-9:]
    assemble(place, parts, weights)
    slots, features = mid.shape
    width = biases.shape[2] // 4
    depth = width // 8
    pad = 256 - width
    lanes = lax.broadcasted_iota(i32, (1, 256), 1)
    cot = cotangent[...]
    grad_ffn = cot.astype(bf16)
    h2_value = h2[...]
    layer_out[...] = mid[...] + as_row(out_bias)
    grad_h2 = jnp.zeros((slots, features), f32)
    sums[...] = jnp.zeros_like(sums)
    order = group_order(place)
    for side, y, group in order:
        columns = theirs if side else mine
        in_bias = jnp.concatenate(
            [biases[group, 0:1, 2 * width : 3 * width], jnp.zeros((1, pad), f32)], 1
        )
        pre = dot_nn(h2_value, weights[group, :, :256]) + in_bias
        cdf = 0.5 * (1.0 + lax.erf(pre * (0.5**0.5)))
        slope = cdf + pre * jnp.exp(-0.5 * pre * pre) * 0.3989422804014327
        hidden = pltpu.roll(pre * cdf, pad, 1)
        hidden = jnp.where(lanes >= pad, hidden, 0.0).astype(bf16)
        layer_out[...] += dot_nt(hidden, weights[group, :, width - pad : 2 * width])
        grad_hidden = dot_nn(grad_ffn, weights[group, :, width - pad : 2 * width])
        grad_hidden = pltpu.roll(grad_hidden, width, 1)
        grad_pre = jnp.where(lanes < width, grad_hidden * slope, 0.0).astype(bf16)
        grad_h2 = grad_h2 + dot_nt(grad_pre, weights[group, :, :256])
        columns[y, :, 0:256] = grad_pre
        columns[y, :, 256:512] = hidden
        columns[y, :, 512:768] = att_low[group]
        sums[pl.ds(12 + group, 1), 0:256] = column_sum(grad_pre.astype(f32))
    normed, scale = normalize(mid[...])
    grad = cot + normalize_back(grad_h2 * as_row(gain), normed, scale)
    grad_mid[...] = grad
    branch = grad.astype(bf16)
    sums[2:3, :] = column_sum(grad)
    sums[3:4, :] = column_sum(grad_h2 * normed)
    sums[4:5, :] = column_sum(grad_h2)
    sums[5:6, :] = column_sum(cot)
    rows_t[0] = h2_value.astype(f32).T.astype(bf16)
    rows_t[1] = grad.T.astype(bf16)
    gap = jnp.zeros((pad, slots), f32)
    for side, y, group in order:
        columns = theirs if side else mine
        grad_att = dot_nn(branch, weights_a[group]).T[pad:]
        grad_att_t[group] = jnp.concatenate([grad_att, gap], 0).astype(bf16)
        out = []
        for head in range(8):
            out.append(
                dot_nt(
                    grad_att[head * depth : (head + 1) * depth].astype(bf16),
                    probs_in[group * 8 + head].astype(bf16),
                )
            )
        low_form = jnp.concatenate(out + [gap], 0).T.astype(bf16)
        grad_values[group] = low_form
        columns[y, :, 768:1024] = jnp.concatenate([gap] + out, 0).T.astype(bf16)
        sums[pl.ds(8 + group, 1), 512:768] = column_sum(low_form.astype(f32))


def feed(place, mid, h2, weights_a, biases, out_bias, gain, cotangent, att_low, probs, parts, after=()):
    slots, features = mid.shape
    groups, width = biases.shape[0], biases.shape[2] // 4
    whole = lambda array: pl.BlockSpec(array.shape, lambda i: (0,) * len(array.shape))
    outs = (
        shape((slots, features), f32),
        shape((slots, features), f32),
        shape((groups, 256, slots), bf16),
        shape((groups, slots, 256), bf16),
        shape((2, slots, 1024), bf16),
        shape((2, slots, 1024), bf16),
        shape((2, features, slots), bf16),
        shape((16, features), f32),
    )
    rest = (biases, out_bias, gain, cotangent, att_low, probs)
    return pl.pallas_call(
        functools.partial(feed_kernel, len(parts)),
        grid=(1,),
        out_shape=outs,
        in_specs=[
            smem,
            whole(mid),
            whole(h2),
            pl.BlockSpec((groups, features, 256), lambda i: (0, 0, 2)),
        ]
        + [whole(a) for a in rest + tuple(parts)]
        + [untouched] * len(after),
        out_specs=[whole(out) for out in outs],
        scratch_shapes=[pltpu.VMEM((groups, features, 2 * width), bf16)],
        cost_estimate=cost(7),
        compiler_params=params(32),
        name="feed",
    )(place, mid, h2, weights_a, *rest, *parts, *after)


def attend_back_kernel(
    place, probs_in, value_win, transposed, grad_att_t, grad_values, weights, layer_in, gain, grad_mid,
    sums_in, after, score_grads, mine, theirs, grad_in, sums,
):
    slots, features = layer_in.shape
    width = transposed.shape[1] // 2
    depth = width // 8
    value_masks = head_masks(256, 0, depth)
    grad_h1 = jnp.zeros((slots, features), f32)
    sums[...] = sums_in[...]
    scale = depth ** (-0.5)
    for side, y, group in group_order(place):
        columns = theirs if side else mine
        values = value_win[group]
        stack = jnp.concatenate([values * mask for mask in value_masks], 0)
        grad_probs = dot_nn(stack, grad_att_t[group])
        held = transposed[group].astype(f32)
        query_out, key_out, score_out = [], [], []
        for head in range(8):
            probs = probs_in[group * 8 + head]
            part = probs * grad_probs[head * slots : (head + 1) * slots]
            exact = part - probs * column_sum(part)
            grads = exact.astype(bf16)
            score_out.append(exact)
            key_rows = held[width + head * depth : width + (head + 1) * depth]
            query_out.append(dot_nn(key_rows.astype(bf16), grads) * scale)
            query_rows = held[head * depth : (head + 1) * depth]
            key_out.append(dot_nt(query_rows.astype(bf16), grads) * scale)
        score_grads[group] = jnp.swapaxes(jnp.stack(score_out), 0, 1)
        natural = jnp.concatenate(query_out + key_out, 0).T.astype(bf16)
        columns[y] = natural
        grad_h1 = grad_h1 + dot_nt(natural, weights[group, :, : 2 * width])
        grad_h1 = grad_h1 + dot_nt(grad_values[group], weights[group, :, 2 * width : 2 * width + 256])
        sums[pl.ds(8 + group, 1), 0 : 2 * width] = column_sum(natural.astype(f32))
    normed, inverse = normalize(layer_in[...])
    grad_in[...] = grad_mid[...] + normalize_back(grad_h1 * as_row(gain), normed, inverse)
    sums[0:1, :] = column_sum(grad_h1 * normed)
    sums[1:2, :] = column_sum(grad_h1)


def attend_back(
    place, probs, value_win, transposed, grad_att_t, grad_values, weights, layer_in, gain, grad_mid, sums, after
):
    slots, features = layer_in.shape
    groups = transposed.shape[0]
    width = transposed.shape[1] // 2
    return pl.pallas_call(
        attend_back_kernel,
        out_shape=(
            shape((groups, slots, 8, slots), f32),
            shape((2, slots, 2 * width), bf16),
            shape((2, slots, 2 * width), bf16),
            shape((slots, features), f32),
            shape(sums.shape, f32),
        ),
        in_specs=[smem] + [vmem] * 10 + [untouched],
        out_specs=[vmem] * 5,
        cost_estimate=cost(7),
        compiler_params=params(24),
        name="attend_back",
    )(
        place, probs, value_win, transposed, grad_att_t, grad_values, weights, layer_in, gain, grad_mid,
        sums, after,
    )


def weight_grads_kernel(plan, n_rows, place, columns_own, columns_other, *refs):
    own_rows, other_rows = refs[:n_rows], refs[n_rows : 2 * n_rows]
    own, across, second, rows_t = refs[-4:]
    kind = 0
    for mine, other in zip(own_rows, other_rows):
        slots = mine.shape[2]
        for i in range(mine.shape[0]):
            rows_t[kind, :, 0:slots] = mine[i]
            rows_t[kind, :, slots : 2 * slots] = other[i]
            kind += 1
    core = place[3]
    height = own.shape[1]
    for which, out, at in ((3, second, 0), (2, second, 4), (1, across, 0), (0, own, 0)):
        y = relative(place, core, which, 0)[1] >> 1
        right = jnp.concatenate([columns_own[y], columns_other[y]], 0)
        for step in range(4):
            row = relative(place, core, which, step)[0]
            start = pl.multiple_of(row * height, height)
            out[at + step] = plan(lambda kind: rows_t[kind, pl.ds(start, height), :], right).astype(bf16)


def plan_first(rows_of, right):
    return dot_nn(rows_of(0), right)


def plan_second(rows_of, right):
    grad_in = dot_nn(rows_of(2), right[:, 0:256])
    grad_out = dot_nn(rows_of(1), right[:, 256:512])
    grad_o = dot_nn(rows_of(3), right[:, 512:768])
    grad_v = dot_nn(rows_of(0), right[:, 768:1024])
    return jnp.concatenate(
        [
            grad_in[:, :128],
            grad_in[:, 128:] + grad_out[:, :128],
            grad_out[:, 128:],
            grad_o[:, :128],
            grad_o[:, 128:] + grad_v[:, :128],
            grad_v[:, 128:],
        ],
        1,
    )


def weight_grads(
    plan, place, columns_own, columns_other, own_rows, other_rows, height, lanes, microseconds, after=()
):
    features, slots = own_rows[0].shape[1:]
    kinds = sum(rows.shape[0] for rows in own_rows)
    out = shape((4, height, lanes), bf16)
    return pl.pallas_call(
        functools.partial(weight_grads_kernel, plan, len(own_rows)),
        out_shape=(out, out, shape((8, height, lanes), bf16)),
        in_specs=[smem] + [vmem] * (2 + 2 * len(own_rows)) + [untouched] * len(after),
        out_specs=[vmem] * 3,
        scratch_shapes=[pltpu.VMEM((kinds, features, 2 * slots), bf16)],
        cost_estimate=cost(microseconds),
        compiler_params=params(20),
        name="weight_grads",
    )(place, columns_own, columns_other, *own_rows, *other_rows, *after)


def table_kernel(digit, start, stop, previous, last, place, grads, ids, buckets, *refs):
    hops = ids.shape[0]
    groups = grads.shape[0]
    heads = groups * 8
    span = 8
    if previous:
        total_in, spatial_in = refs[:2]
    if last:
        sums = refs[2]
        mine, theirs, small, total, spatial = refs[-5:]
    else:
        total, spatial = refs[-2:]
    total[...] = total_in[...] if previous else jnp.zeros_like(total)
    spatial[...] = spatial_in[...] if previous else jnp.zeros_like(spatial)
    high_count = total.shape[0] // heads
    digits = lax.broadcasted_iota(i32, (digit, 128), 0).astype(f32).astype(bf16)
    kinds = lax.broadcasted_iota(i32, (heads, 128), 0).astype(f32).astype(bf16)
    one = jnp.ones((), bf16)
    zero = jnp.zeros((), bf16)

    def body(i, carry):
        lefts, rights, plain, kind_rights = [], [], [], []
        for j in range(span):
            row = i * span + j
            piece = jnp.concatenate([grads[group, row] for group in range(groups)], 0).astype(bf16)
            bucket = buckets[pl.ds(row, 1), :].astype(f32).astype(bf16)
            plain.append(piece)
            kind_rights.append(jnp.where(jnp.broadcast_to(bucket, (heads, 128)) == kinds, one, zero))
            for hop in range(hops):
                value = ids[hop, pl.ds(row, 1), :].astype(f32)
                high = jnp.floor((value + 0.5) * (1.0 / digit))
                low = value - high * digit
                low = jnp.broadcast_to(low.astype(bf16), (digit, 128))
                high = jnp.broadcast_to(high.astype(bf16), (heads, 128))
                rights.append(jnp.where(low == digits, one, zero))
                lefts.append(
                    jnp.concatenate(
                        [jnp.where(high == jnp.full((), k, bf16), piece, zero) for k in range(high_count)], 0
                    )
                )
        total[...] += dot_nt(jnp.concatenate(lefts, 1), jnp.concatenate(rights, 1))
        spatial[...] += dot_nt(jnp.concatenate(plain, 1), jnp.concatenate(kind_rights, 1))
        return carry

    lax.fori_loop(start // span, stop // span, body, 0)
    if last:
        core = place[3]
        for other, out in ((0, mine), (1, theirs)):
            for which in range(4):
                pieces = []
                for step in range(4):
                    row, column = relative(place, core ^ other, which, step)
                    at = pl.multiple_of(row * heads + column * 8, 8)
                    pieces.append(total[pl.ds(at, 8), :] * (1.0 / hops))
                out[which * 16 : which * 16 + 8, :] = jnp.concatenate(pieces[:2], 1)
                out[which * 16 + 8 : which * 16 + 16, :] = jnp.concatenate(pieces[2:], 1)
        half = small.shape[1]
        held = sums[...]
        spread = [jnp.zeros((8, digit), f32)] + [spatial[group * 8 : (group + 1) * 8, :] for group in range(4)]
        spread.append(jnp.zeros((8, half - digit - 4 * heads), f32))
        packed = [jnp.concatenate(spread, 1), held[0:8, :half], held[0:8, half:]]
        packed.append(
            jnp.concatenate(
                [
                    jnp.concatenate([held[8:12, :digit], held[12:16, :digit]], 0),
                    jnp.concatenate([held[8:12, 512 : 512 + digit], jnp.zeros((4, digit), f32)], 0),
                ],
                1,
            )
        )
        packed = jnp.concatenate(packed, 0)
        small[...] = packed
        theirs[64:96, :] = packed


def table_grads(place, grads, ids, buckets, digit, edges, start, stop, previous=(), sums=None, after=()):
    heads = grads.shape[0] * 8
    last = sums is not None
    inner = (shape((edges // digit * heads, digit), f32), shape((heads, heads), f32))
    outs = inner
    if last:
        lanes = sums.shape[1] // 2
        outs = (shape((64, lanes), f32), shape((96, lanes), f32), shape((32, lanes), f32))
    inputs = tuple(previous) + ((sums,) if last else ())
    return pl.pallas_call(
        functools.partial(table_kernel, digit, start, stop, len(previous) > 0, last),
        out_shape=outs,
        in_specs=[smem] + [vmem] * (3 + len(inputs)) + [untouched] * len(after),
        out_specs=[vmem] * len(outs),
        scratch_shapes=[pltpu.VMEM(a.shape, f32) for a in inner] if last else [],
        cost_estimate=cost(15 * (stop - start) / grads.shape[1]),
        compiler_params=params(12),
        name="table_grads",
    )(place, grads, ids, buckets, *inputs, *after)


def meet_core_kernel(mine, small, got, after, out, keep):
    keep[0:16, :] = mine[0:16, :] + got[0:16, :]
    keep[16:32, :] = mine[32:48, :] + got[32:48, :]
    out[0:16, :] = mine[48:64, :] + got[48:64, :]
    out[16:32, :] = mine[16:32, :] + got[16:32, :]
    out[32:64, :] = small[...] + got[64:96, :]


def meet_near_kernel(keep, sent, got, out, kept):
    out[0:16, :] = keep[16:32, :] + got[0:16, :]
    out[16:48, :] = sent[32:64, :] + got[32:64, :]
    kept[...] = keep[0:16, :] + got[16:32, :]


def meet_far_kernel(kept, sent, got, own, first_hop, second_hop, *outs):
    table = kept[...] + got[0:16, :]
    small = sent[16:48, :] + got[16:48, :]
    digit = table.shape[1] // 2
    rows = own.shape[1]
    for step, out in enumerate(outs):
        total = own[step].astype(f32) + first_hop[step].astype(f32) + second_hop[step + 4].astype(f32)
        out[0:rows, :] = total.astype(bf16)
        block = table[(step // 2) * 8 : (step // 2) * 8 + 8, (step % 2) * digit : (step % 2 + 1) * digit]
        head = jnp.concatenate([block, small[0:8, digit:]], 1)
        out[rows:, :] = jnp.concatenate([head, small[8:32]], 0).astype(bf16)


def finish_kernel(place, own, first, second, third, after, *outs):
    total = own[...].astype(f32)
    for part in (first, second, third):
        total = total + part[...].astype(f32)
    query, key, edge, spatial = outs[:4]
    outs = outs[4:]
    rows, width = query.shape
    digit = edge.shape[1]
    query[...] = total[0:rows, 0:width]
    key[...] = total[0:rows, width : 2 * width]
    edge[...] = total[rows : rows + 8, 0:digit]
    group = place[4]
    at = rows + 8
    for i, out in enumerate(outs[:6]):
        row = jnp.concatenate([total[at + i : at + i + 1, :], total[at + 8 + i : at + 9 + i, :]], 1)
        out[...] = row.reshape(out.shape)
    at = rows + 24
    heads = total[at : at + 1]
    hidden = total[at + 4 : at + 5]
    kinds = total[rows : rows + 8, digit : digit + 32]
    for other in range(1, 4):
        heads = jnp.where(group == other, total[at + other : at + other + 1], heads)
        hidden = jnp.where(group == other, total[at + 4 + other : at + 5 + other], hidden)
        start = digit + other * 32
        kinds = jnp.where(group == other, total[rows : rows + 8, start : start + 32], kinds)
    outs[6][...] = heads[:, :width].reshape(outs[6].shape)
    outs[7][...] = heads[:, width : 2 * width].reshape(outs[7].shape)
    outs[8][...] = hidden[:, :width].reshape(outs[8].shape)
    spatial[...] = kinds[:, : spatial.shape[1]]


def small_call(kernel, name, outs, *args, waits=0, mebibytes=8):
    return pl.pallas_call(
        kernel,
        out_shape=outs,
        in_specs=[smem if args[i].ndim == 1 else vmem for i in range(len(args) - waits)]
        + [untouched] * waits,
        out_specs=[vmem] * len(outs),
        cost_estimate=cost(1),
        compiler_params=params(mebibytes),
        name=name,
    )(*args)


class Links:
    def __init__(self):
        self.core = self.hop(lambda z, x, y, c: (z, x, y, 1 - c))
        self.first = self.hop(lambda z, x, y, c: (z, x, 1 - y, c) if c else (z, 1 - x, y, c))
        self.second = self.hop(lambda z, x, y, c: (z, 1 - x, y, c) if c else (z, x, 1 - y, c))
        self.along_x = self.hop(lambda z, x, y, c: (z, 1 - x, y, c))
        self.along_y = self.hop(lambda z, x, y, c: (z, x, 1 - y, c))
        self.along_z = [self.hop(lambda z, x, y, c, k=k: (z ^ k, x, y, c)) for k in (1, 2, 3)]

    def hop(self, move):
        index = lambda z, x, y, c: (z * 2 + x) * 4 + y * 2 + c
        spots = [(z, x, y, c) for z in range(4) for x in range(2) for y in range(2) for c in range(2)]
        return [(index(*spot), index(*move(*spot))) for spot in spots]


def send(values, hop):
    return lax.ppermute(values, ("dp", "mp"), hop)


def around(links, own):
    return [own] + [send(own, hop) for hop in links.along_z]


def join_kernel(rows, count, *refs):
    out = refs[-1]
    for i in range(count):
        stop = min((i + 1) * rows, out.shape[0])
        out[i * rows : stop, :] = refs[i][0 : stop - i * rows, :]


def join(parts, rows, after=()):
    total = rows * (len(parts) - 1) + parts[-1].shape[0] if len(parts) == 5 else rows * len(parts)
    return small_call(
        functools.partial(join_kernel, rows, len(parts)), "join",
        (shape((total, parts[0].shape[1]), bf16),), *parts, *after, waits=len(after),
    )[0]


def join_pairs_kernel(rows, own, near, *refs):
    out = refs[-1]
    for i, (part, at) in enumerate(((own, 0), (near, 0), (own, rows), (near, rows))):
        out[i * rows : (i + 1) * rows, :] = part[at : at + rows, :]


def join_pairs(own, near, rows, after):
    return small_call(
        functools.partial(join_pairs_kernel, rows), "join_pairs",
        (shape((4 * rows, own.shape[1]), bf16),), own, near, *after, waits=len(after),
    )[0]


def add_kernel(count, *refs):
    for step in range(4):
        total = refs[0][step].astype(f32)
        for ref in refs[1:count]:
            total = total + ref[step].astype(f32)
        refs[-1][step] = total.astype(bf16)


def add_rounded(terms, after):
    return small_call(
        functools.partial(add_kernel, len(terms)), "add",
        (shape(terms[0].shape, bf16),), *terms, *after, waits=len(after),
    )[0]


def step_sum(refs, step):
    total = refs[0][step].astype(f32)
    for ref in refs[1:]:
        total = total + ref[step + ref.shape[0] - 4].astype(f32)
    return total.astype(bf16)


def add_pair_kernel(count, *refs):
    stay, go = refs[-2:]
    for i in range(2):
        stay[i] = step_sum(refs[:count], 2 * i)
        go[i] = step_sum(refs[:count], 2 * i + 1)


def add_pair(terms, after):
    out = shape((2,) + terms[0].shape[1:], bf16)
    return small_call(
        functools.partial(add_pair_kernel, len(terms)), "add_pair",
        (out,) * 2, *terms, *after, waits=len(after),
    )


def add_half_kernel(count, stay, got, *refs):
    for i, out in enumerate(refs[-2:]):
        out[...] = (stay[i].astype(f32) + got[i].astype(f32)).astype(bf16)


def add_half(stay, got, after):
    out = shape(stay.shape[1:], bf16)
    return small_call(
        functools.partial(add_half_kernel, 2), "add_half", (out,) * 2, stay, got, *after, waits=len(after)
    )


def settle_kernel(count, *refs):
    total = refs[0][...].astype(f32) + refs[1][...].astype(f32)
    outs = refs[len(refs) - count :]
    width = outs[0].shape[1]
    for i, out in enumerate(outs):
        out[...] = total[:, i * width : (i + 1) * width]


def settle(terms, width, after):
    rows, lanes = terms[0].shape
    count = lanes // width
    return small_call(
        functools.partial(settle_kernel, count), "settle",
        (shape((rows, width), f32),) * count, *terms, *after, waits=len(after), mebibytes=60,
    )


def held_until(values, *others):
    return lax.optimization_barrier((values, others))[0]


def local(
    layer_in,
    node_counts,
    spatial_ids,
    path_ids,
    ln1_gain,
    ln1_bias,
    w_q,
    w_k,
    w_v,
    q_bias,
    v_bias,
    spatial_table,
    edge_table,
    w_o,
    o_bias,
    ln2_gain,
    ln2_bias,
    w_in,
    in_bias,
    w_out,
    out_bias,
    cotangent,
):
    dp_size, mp_size = lax.axis_size("dp"), lax.axis_size("mp")
    dp_index, mp_index = lax.axis_index("dp"), lax.axis_index("mp")
    staged = dp_size == 8 and mp_size == 4
    height, width = w_q.shape
    features = layer_in.shape[1]
    edges = edge_table.shape[0] * dp_size
    heads = spatial_table.shape[1]
    kinds = spatial_table.shape[0]
    hops = path_ids.shape[1]
    share = edges // 4
    digit = edges // 8
    place = jnp.stack([dp_index // 2, dp_index % 2, mp_index // 2, mp_index % 2, mp_index]).astype(i32)
    ids, buckets, h1, rows_early = prepare(
        place, spatial_ids, path_ids, layer_in, ln1_gain, ln1_bias, cotangent, kinds - 1
    )
    if staged:
        links = Links()
        table_t = edge_table.T
        second = pack_second(w_in, w_out)
        first, own_biases = pack_first(
            place, w_q, w_k, w_v, w_o, q_bias, v_bias, in_bias, table_t, send(table_t, links.along_x), second
        )
        chunks = around(links, first)
        pair_b = join([second, send(second, links.first)], height)
        lookup_place = place
    else:
        gathered = [
            lax.all_gather(lax.all_gather(w, "dp", axis=0, tiled=True), "mp", axis=0)
            for w in (w_q, w_k, w_v, w_o, w_in, w_out)
        ]
        bias_row = jnp.concatenate([q_bias, v_bias, in_bias, jnp.zeros((width,), f32)])
        bias_row = lax.all_gather(bias_row[None], "mp", axis=0)
        parts_a = (jnp.concatenate(gathered[:4], 2), bias_row)
        parts_b = (jnp.concatenate(gathered[4:], 2),)
        table_t = lax.all_gather(edge_table, "dp", axis=0, tiled=True).T
        half = share // 2
        chunks = []
        for i in range(4):
            low, high = (table_t[:, i * share + n * half : i * share + (n + 1) * half] for n in range(2))
            chunks.append(
                jnp.concatenate([low[: heads // 2], low[heads // 2 :], high[: heads // 2], high[heads // 2 :]], 1)
            )
        lookup_place = jnp.zeros((5,), i32)
    edge_sums = None
    look = lambda step, after: lookup(lookup_place, chunks[step], ids, edge_sums, step, heads, after)
    if staged:
        edge_sums = look(0, (pair_b,))
        stack_a = join(chunks + [own_biases], height, (edge_sums,))
        across_a, over_a = send(stack_a, links.first), send(stack_a, links.second)
        pair_b = held_until(pair_b, stack_a)
        far_b = send(pair_b, links.along_z[1])
        edge_sums = look(1, (stack_a,))
        four_b = join([pair_b, far_b], 2 * height, (edge_sums,))
        near_b = send(four_b, links.along_z[0])
        edge_sums = look(2, (four_b,))
        across_a = held_until(across_a, edge_sums)
        both_a = send(across_a, links.second)
        eight_b = join_pairs(four_b, near_b, 2 * height, (edge_sums,))
        over_b = send(eight_b, links.second)
        edge_sums = look(3, (eight_b,))
        mine = (stack_a, across_a, over_a)
        theirs = tuple(send(held_until(part, eight_b), links.core) for part in mine)
        parts_a = mine + (both_a,) + theirs + (send(both_a, links.core),)
    else:
        for step in range(4):
            edge_sums = look(step, ())

    weights, biases, transposed, value_win, probs, att_low, mid, h2 = attend(
        place, node_counts, h1, edge_sums, buckets, spatial_table,
        layer_in, o_bias, ln2_gain, ln2_bias, parts_a,
    )
    if staged:
        parts_b = (
            eight_b, over_b, send(held_until(eight_b, edge_sums), links.core),
            send(held_until(over_b, mid), links.core),
        )
        other_rows_early = send(held_until(rows_early, mid), links.core)
        feed_after = (other_rows_early,)
    else:
        feed_after = ()
    layer_out, grad_mid, grad_att_t, grad_values, mine_b, theirs_b, rows_late, sums = feed(
        place, mid, h2, weights, biases, out_bias, ln2_gain, cotangent, att_low, probs, parts_b, feed_after
    )
    after = sums
    if staged:
        rows_b = (rows_early, rows_late)
        other_rows_b = (other_rows_early, send(rows_late, links.core))
        own_b, across_b, second_b = weight_grads(
            plan_second, place, mine_b, send(theirs_b, links.core), rows_b, other_rows_b, height, 4 * width, 4
        )
        got_second_b = send(second_b, links.second)
        after = own_b
    score_grads, mine_a, theirs_a, grad_layer_in, sums = attend_back(
        place, probs, value_win, transposed, grad_att_t, grad_values, weights,
        layer_in, ln1_gain, grad_mid, sums, after,
    )
    table = functools.partial(table_grads, place, score_grads, ids, buckets, digit, edges)
    slots = ids.shape[1]
    if staged:
        other_columns_a = send(theirs_a, links.core)
        partial = table(0, 64)
        across_b = add_rounded((across_b, got_second_b), (partial[0],))
        got_across_b = send(across_b, links.first)
        own_a, across_a, second_a = weight_grads(
            plan_first, place, mine_a, other_columns_a,
            (rows_early[0:1],), (other_rows_b[0][0:1],), height, 2 * width, 2, (partial[0],),
        )
        partial = table(64, 96, partial, after=(own_a, across_b))
        mine, theirs, small = table(96, slots, partial, sums)
        got_core = send(theirs, links.core)
        got_second_a = send(held_until(second_a, small), links.second)
        stay_b, go_b = add_pair((own_b, got_across_b, got_second_b), (small,))
        got_pair_b = send(go_b, links.along_z[0])
        half = features // 2
        sent, keep = small_call(
            meet_core_kernel, "meet_core", (shape((64, half), f32), shape((32, half), f32)),
            mine, small, got_core, stay_b, waits=1,
        )
        sent, keep = small_call(
            meet_near_kernel, "meet_near", (shape((48, half), f32), shape((16, half), f32)),
            keep, sent, send(sent, links.first),
        )
        got_last = send(sent, links.second)
        own_b, go_b = add_half(stay_b, got_pair_b, (sent,))
        got_b = send(go_b, links.along_z[1])
        across_a = add_rounded((across_a, got_second_a), (own_b,))
        got_across_a = send(across_a, links.first)
        own_a = small_call(
            meet_far_kernel, "meet_far", (shape((height + 32, half), bf16),) * 4,
            keep, sent, got_last, own_a, got_across_a, got_second_a,
        )
        got_a = [send(own_a[step + 1], hop) for step, hop in enumerate(links.along_z)]
        grad_w_in, grad_w_out, grad_w_o, grad_w_v = settle([own_b, got_b], width, (own_a[0],))
        grad_w_q, grad_w_k, grad_edge, grad_spatial, *rows = small_call(
            finish_kernel, "finish",
            (shape((height, width), f32),) * 2
            + (shape((8, digit), f32), shape((8, kinds), f32))
            + (shape((features,), f32),) * 6
            + (shape((width,), f32),) * 3,
            place, own_a[0], *got_a, grad_w_in, waits=1, mebibytes=60,
        )
        grad_edge = grad_edge.T
        grad_spatial = grad_spatial.T
    else:
        contract = lambda a, b: lax.dot_general(
            a, b, (((1,), (1,)), ((), ())), preferred_element_type=f32
        )

        def unmix(mine, theirs):
            even = mp_index % 2 == 0
            cores = jnp.where(even, jnp.stack([mine, theirs], 1), jnp.stack([theirs, mine], 1))
            return cores.reshape(4, *mine.shape[1:])

        def scatter(rows_t, columns):
            grads = contract(rows_t, columns)
            grads = jnp.transpose(grads, (1, 0, 2))
            grads = lax.psum_scatter(grads, "mp", scatter_dimension=0, tiled=False)
            return lax.psum_scatter(grads, "dp", scatter_dimension=0, tiled=True)

        columns_a, columns_b = unmix(mine_a, theirs_a), unmix(mine_b, theirs_b)
        grad_w_q, grad_w_k = (
            scatter(rows_early[0], columns_a[:, :, i * width : (i + 1) * width]) for i in range(2)
        )
        grad_w_v = scatter(rows_early[0], columns_b[:, :, 1024 - width :])
        grad_w_in = scatter(rows_late[0], columns_b[:, :, :width])
        grad_w_out = scatter(rows_early[1], columns_b[:, :, 512 - width : 512])
        grad_w_o = scatter(rows_late[1], columns_b[:, :, 512 : 512 + width])
        table, spatial = table(0, slots)
        table = table.reshape(-1, heads, digit).transpose(0, 2, 1).reshape(edges, heads) / hops
        table = lax.psum_scatter(table, "dp", scatter_dimension=0, tiled=True)
        table = lax.psum(table, "mp")
        grad_edge = lax.dynamic_slice_in_dim(table, mp_index * 8, 8, 1)
        totals, spatial = lax.psum((sums, spatial), ("dp", "mp"))
        grad_spatial = lax.dynamic_slice_in_dim(spatial[:, :kinds], mp_index * 8, 8, 0).T
        head_sums = lax.dynamic_slice_in_dim(totals, 8 + mp_index, 1, 0)[0]
        hidden_sums = lax.dynamic_slice_in_dim(totals, 12 + mp_index, 1, 0)[0]
        rows = [totals[i] for i in range(6)]
        rows += [head_sums[:width], head_sums[512 : 512 + width], hidden_sums[:width]]
    return (
        layer_out,
        grad_layer_in,
        rows[0],
        rows[1],
        grad_w_q,
        grad_w_k,
        grad_w_v,
        rows[6],
        rows[7],
        grad_spatial,
        grad_edge,
        grad_w_o,
        rows[2],
        rows[3],
        rows[4],
        grad_w_in,
        rows[8],
        grad_w_out,
        rows[5],
    )


def solution(mesh):
    return jax.shard_map(
        local,
        mesh=mesh,
        in_specs=(
            P(("dp", "mp"), None),
            P("dp"),
            P("dp", None, None),
            P("dp", None, None, None),
            P(),
            P(),
            P("dp", "mp"),
            P("dp", "mp"),
            P("dp", "mp"),
            P("mp"),
            P("mp"),
            P(),
            P("dp", None),
            P("dp", "mp"),
            P(),
            P(),
            P(),
            P("dp", "mp"),
            P("mp"),
            P("dp", "mp"),
            P(),
            P(("dp", "mp"), None),
        ),
        out_specs=(
            P(("dp", "mp"), None),
            P(("dp", "mp"), None),
            P(),
            P(),
            P("dp", "mp"),
            P("dp", "mp"),
            P("dp", "mp"),
            P("mp"),
            P("mp"),
            P(None, "mp"),
            P("dp", "mp"),
            P("dp", "mp"),
            P(),
            P(),
            P(),
            P("dp", "mp"),
            P("mp"),
            P("dp", "mp"),
            P(),
        ),
        check_vma=False,
    )
```

```python
import functools

import jax
import jax.numpy as jnp
from jax import lax
from jax.experimental import pallas as pl
from jax.experimental.pallas import tpu as pltpu
from jax.sharding import PartitionSpec as P

epsilon = 1e-05
masked_score = -1e30
edge_unit = 1638.0
spatial_unit = 4096.0
hurry = 0.02
bf16 = jnp.bfloat16
f32 = jnp.float32
i32 = jnp.int32
vmem = pl.BlockSpec(memory_space=pltpu.VMEM)
smem = pl.BlockSpec(memory_space=pltpu.SMEM)
hbm = pl.BlockSpec(memory_space=pltpu.HBM)
untouched = pl.BlockSpec(memory_space=pl.ANY)


def params(mebibytes):
    return pltpu.CompilerParams(vmem_limit_bytes=mebibytes << 20)


def normalize(values):
    centred = values - jnp.mean(values, axis=-1, keepdims=True)
    scale = lax.rsqrt(jnp.mean(centred * centred, axis=-1, keepdims=True) + epsilon)
    return (centred * scale, scale)


def normalize_back(grad_normed, normed, scale):
    inner = grad_normed - jnp.mean(grad_normed, axis=-1, keepdims=True)
    inner = inner - normed * jnp.mean(grad_normed * normed, axis=-1, keepdims=True)
    return inner * scale


def dot_nn(left, right):
    return lax.dot_general(
        left, right, (((1,), (0,)), ((), ())), preferred_element_type=f32
    )


def dot_nt(left, right):
    return lax.dot_general(
        left, right, (((1,), (1,)), ((), ())), preferred_element_type=f32
    )


def column_sum(values):
    return jnp.sum(values, axis=0, keepdims=True)


def cost(microseconds):
    return pl.CostEstimate(flops=int(microseconds * hurry * 1.15e9), bytes_accessed=1024, transcendentals=0)


def as_row(ref):
    return ref[...].reshape(1, -1)


def shape(dims, kind):
    return jax.ShapeDtypeStruct(dims, kind)


def relative(place, side, which, step):
    z, x, y = place[0], place[1], place[2]
    flip_x = (0, 1 - side, side, 1)[which]
    flip_y = (0, side, 1 - side, 1)[which]
    row = (z ^ step) * 2 + (x ^ flip_x)
    column = (y ^ flip_y) * 2 + side
    return row, column


def three_terms(values):
    terms = []
    for _ in range(3):
        term = values.astype(bf16)
        terms.append(term)
        values = values - term.astype(f32)
    return terms


def pack_first_kernel(place, wq, wk, wv, wo, bq, bv, bi, edge, neighbour, after, weights, biases, held, sems):
    copies = [
        pltpu.make_async_copy(source, held.at[i], sems.at[i]) for i, source in enumerate((wq, wk, wv, wo))
    ]
    for copy in copies:
        copy.start()
    row = jnp.concatenate([as_row(bq), as_row(bv), as_row(bi)], 1)
    lanes = weights.shape[1]
    row = jnp.concatenate([row, jnp.zeros((1, lanes - row.shape[1]), f32)], 1)
    terms = [term.astype(f32) for term in three_terms(row)]
    biases[...] = jnp.concatenate(terms + [jnp.zeros((13, lanes), f32)], 0).astype(bf16)
    even = place[1] == 0
    mine, other = edge[...].astype(f32), neighbour[...].astype(f32)
    low, high = jnp.where(even, mine, other), jnp.where(even, other, mine)
    rows = held.shape[1]
    half = low.shape[0] // 2
    weights[rows:, :] = jnp.concatenate([low[:half], low[half:], high[:half], high[half:]], 1).astype(bf16)
    for copy in copies:
        copy.wait()
    weights[0:rows, :] = jnp.concatenate([held[i] for i in range(4)], 1)


def pack_first(place, wq, wk, wv, wo, bq, bv, bi, edge, neighbour, after):
    rows, width = wq.shape
    return pl.pallas_call(
        pack_first_kernel,
        out_shape=(shape((rows + 16, 4 * width), bf16), shape((16, 4 * width), bf16)),
        in_specs=[smem] + [hbm] * 4 + [vmem] * 5 + [untouched],
        out_specs=[vmem] * 2,
        scratch_shapes=[pltpu.VMEM((4, rows, width), bf16), pltpu.SemaphoreType.DMA((4,))],
        cost_estimate=cost(2),
        compiler_params=params(60),
        name="pack_first",
    )(place, wq, wk, wv, wo, bq, bv, bi, edge, neighbour, after)


def pack_second_kernel(wi, wu, out):
    out[...] = jnp.concatenate([wi[...], wu[...]], 1)


def pack_second(wi, wu):
    rows, width = wi.shape
    return pl.pallas_call(
        pack_second_kernel,
        out_shape=shape((rows, 2 * width), bf16),
        in_specs=[vmem] * 2,
        out_specs=vmem,
        cost_estimate=cost(1),
        compiler_params=params(60),
        name="pack_second",
    )(wi, wu)


def prepare_kernel(
    virtual, place, spatial, path, layer_in, gain, bias, cotangent, after, ids, buckets, h1, rows_t
):
    slots = spatial.shape[1]
    for hop in range(path.shape[1]):
        ids[hop] = path[0, hop].T
    rows = lax.broadcasted_iota(i32, (slots, slots), 0)
    columns = lax.broadcasted_iota(i32, (slots, slots), 1)
    buckets[...] = jnp.where((rows == 0) | (columns == 0), virtual, spatial[0].T)
    normed, scale = normalize(layer_in[...])
    out = normed * as_row(gain) + as_row(bias)
    h1[...] = out.astype(bf16)
    rows_t[0] = out.T.astype(bf16)
    rows_t[1] = cotangent[...].T.astype(bf16)


def prepare(place, spatial, path, layer_in, gain, bias, cotangent, virtual, after):
    hops, slots = path.shape[1], path.shape[2]
    rows, width = layer_in.shape
    whole = lambda dims: pl.BlockSpec(dims, lambda i, s: (0,) * len(dims))
    return pl.pallas_call(
        functools.partial(prepare_kernel, virtual),
        grid_spec=pltpu.PrefetchScalarGridSpec(
            num_scalar_prefetch=1,
            grid=(1,),
            in_specs=[
                pl.BlockSpec((1, slots, slots), lambda i, s: (s[4], 0, 0)),
                pl.BlockSpec((1, hops, slots, slots), lambda i, s: (s[4], 0, 0, 0)),
                whole((rows, width)),
                whole((width,)),
                whole((width,)),
                whole((rows, width)),
                untouched,
            ],
            out_specs=[
                whole((hops, slots, slots)),
                whole((slots, slots)),
                whole((rows, width)),
                whole((2, width, rows)),
            ],
        ),
        out_shape=(
            shape((hops, slots, slots), i32),
            shape((slots, slots), i32),
            shape((rows, width), bf16),
            shape((2, width, rows), bf16),
        ),
        compiler_params=params(62),
        cost_estimate=cost(1),
        name="prepare",
    )(place, spatial, path, layer_in, gain, bias, cotangent, after)


def quantize(table, unit):
    held = jnp.round(table.astype(f32) * unit).astype(i32)
    partner = jnp.concatenate([held[4:], held[:4]], 0)
    return held + partner * 65536


def lanes_gather(table, places):
    return jnp.take_along_axis(table, places, axis=1, mode="promise_in_bounds")


def lookup_kernel(first, step, share, place, chunk, ids, *refs):
    total, table = refs[-2:]
    previous = None if first else refs[0]
    hops, slots = ids.shape[0], ids.shape[1]
    pairs = total.shape[0]
    below = chunk[chunk.shape[0] - 16 :, :]
    half = share // 2
    below = [below[:, i * half : (i + 1) * half] for i in range(4)]
    packed = quantize(
        jnp.concatenate(
            [jnp.concatenate([below[0], below[2]], 1), jnp.concatenate([below[1], below[3]], 1)], 0
        ),
        edge_unit,
    )
    blocks = share // 128
    for pair in range(pairs):
        head = (pair // 4) * 8 + pair % 4
        for block in range(blocks):
            table[pair, block] = jnp.broadcast_to(
                packed[head : head + 1, block * 128 : (block + 1) * 128], (8, 128)
            )
    base = (place[0] ^ step) * share

    def body(i, carry):
        offset = pl.multiple_of(i * 8, 8)
        sums = [None] * pairs
        if not first:
            sums = [previous[pair, pl.ds(offset, 8), :] for pair in range(pairs)]
        for hop in range(hops):
            relative_id = ids[hop, pl.ds(offset, 8), :] - base
            low = relative_id & 127
            high = relative_id >> 7
            masks = [high == block for block in range(blocks)]
            for pair in range(pairs):
                value = jnp.zeros((8, 128), i32)
                for block in range(blocks):
                    value = jnp.where(masks[block], lanes_gather(table[pair, block], low), value)
                sums[pair] = value if sums[pair] is None else sums[pair] + value
        for pair in range(pairs):
            total[pair, pl.ds(offset, 8), :] = sums[pair]
        return carry

    lax.fori_loop(0, slots // 8, body, 0)


def lookup(place, chunk, ids, previous, step, heads, after=()):
    share = chunk.shape[1] // 2
    pairs = heads // 2
    slots = ids.shape[1]
    first = previous is None
    out = shape((pairs, slots, slots), i32)
    return pl.pallas_call(
        functools.partial(lookup_kernel, first, step, share),
        out_shape=out,
        in_specs=[smem] + [vmem] * (2 if first else 3) + [untouched] * len(after),
        out_specs=vmem,
        scratch_shapes=[pltpu.VMEM((pairs, share // 128, 8, 128), i32)],
        input_output_aliases={} if first else {3: 0},
        compiler_params=params(8),
        cost_estimate=cost(6),
        name="lookup",
    )(place, chunk, ids, *(() if first else (previous,)), *after)


def assemble(place, parts, whole, biases=None):
    if len(parts) <= 2:
        whole[...] = parts[0][...]
        return
    core = place[3]
    rows = whole.shape[1] // 8
    each = len(parts) // 2
    for other in range(2):
        for which in range(4):
            for step in range(4):
                row, column = relative(place, core ^ other, which, step)
                start = pl.multiple_of(row * rows, rows)
                part = parts[other * each + which // (4 // each)]
                at = (step * (4 // each) + which % (4 // each)) * rows
                whole[column, pl.ds(start, rows), :] = part[at : at + rows, :]
            if biases is not None:
                terms = parts[other * each + which][4 * rows : 4 * rows + 16, :].astype(f32)
                biases[column] = terms[0:1] + terms[1:2] + terms[2:3]


def head_masks(width, offset, depth):
    lanes = lax.broadcasted_iota(i32, (1, width), 1)
    out = []
    for head in range(8):
        start = offset + head * depth
        out.append(((lanes >= start) & (lanes < start + depth)).astype(f32).astype(bf16))
    return out


def attend_kernel(
    n_parts, place, counts, h1, edge_sums, buckets, spatial_table, layer_in, o_bias, gain, bias, *refs
):
    parts, refs = refs[:n_parts], refs[n_parts:]
    weights, biases, transposed, value_win, probs_out, att_low, mid, h2 = refs
    assemble(place, parts, weights, biases)
    if n_parts == 2:
        biases[...] = parts[1][...]
    slots = h1.shape[0]
    groups, width = biases.shape[0], biases.shape[2] // 4
    depth = width // 8
    pad = 256 - width
    hops = 5
    count = counts[place[4]]
    packed = quantize(spatial_table[...].astype(f32).T, spatial_unit)
    packed = jnp.concatenate([packed, jnp.zeros((packed.shape[0], 128 - packed.shape[1]), i32)], 1)
    hidden_key = lax.broadcasted_iota(i32, (slots, slots), 0) > count
    bucket = buckets[...]
    key_masks = head_masks(256, pad, depth)
    mid[...] = layer_in[...] + as_row(o_bias)
    for group in range(groups):
        natural = dot_nn(h1[...], weights[group, :, : 3 * width + pad])
        row_bias = jnp.concatenate(
            [
                biases[group, 0:1, :width],
                jnp.zeros((1, width), f32),
                biases[group, 0:1, width : 2 * width],
                jnp.zeros((1, pad), f32),
            ],
            1,
        )
        natural = natural + row_bias
        natural_t = natural.T
        transposed[group] = natural_t[: 2 * width].astype(bf16)
        natural = natural.astype(bf16)
        value_win[group] = natural[:, 2 * width : 2 * width + 256]
        keys = natural[:, width - pad : 2 * width]
        stack = jnp.concatenate([keys * mask for mask in key_masks], 0)
        query = jnp.concatenate([jnp.zeros((pad, slots), f32), natural_t[:width]], 0).astype(bf16)
        scores = dot_nn(stack, query) * depth ** (-0.5)
        out = [None] * 8
        for pair in range(4):
            word = edge_sums[group * 4 + pair]
            head = group * 8 + pair
            spatial_word = lanes_gather(
                jnp.broadcast_to(packed[head : head + 1], (slots, 128)), bucket
            )
            low = (word << 16) >> 16
            spatial_low = (spatial_word << 16) >> 16
            high = (word - low) >> 16
            spatial_high = (spatial_word - spatial_low) >> 16
            for part, spatial_part, spot in ((low, spatial_low, pair), (high, spatial_high, pair + 4)):
                pair_bias = part.astype(f32) * (1.0 / (edge_unit * hops))
                pair_bias = pair_bias + spatial_part.astype(f32) * (1.0 / spatial_unit)
                score = scores[spot * slots : (spot + 1) * slots] + pair_bias
                score = jnp.where(hidden_key, masked_score, score)
                weight = jnp.exp(score - jnp.max(score, axis=0, keepdims=True))
                probs = weight * (1.0 / column_sum(weight))
                probs_out[group * 8 + spot] = probs
                values = natural_t[2 * width + spot * depth : 2 * width + (spot + 1) * depth]
                out[spot] = dot_nn(values.astype(bf16), probs.astype(bf16))
        gap = jnp.zeros((pad, slots), f32)
        att_low[group] = jnp.concatenate(out + [gap], 0).T.astype(bf16)
        high_form = jnp.concatenate([gap] + out, 0).T.astype(bf16)
        mid[...] += dot_nt(high_form, weights[group, :, 3 * width - pad : 4 * width])
    normed, scale = normalize(mid[...])
    h2[...] = (normed * as_row(gain) + as_row(bias)).astype(bf16)


def attend(place, counts, h1, edge_sums, buckets, spatial_table, layer_in, o_bias, gain, bias, parts):
    slots, features = h1.shape
    width = parts[0].shape[-1] // 4
    heads = spatial_table.shape[1]
    groups = heads // 8
    return pl.pallas_call(
        functools.partial(attend_kernel, len(parts)),
        out_shape=(
            shape((groups, features, 4 * width), bf16),
            shape((groups, 1, 4 * width), f32),
            shape((groups, 2 * width, slots), bf16),
            shape((groups, slots, 256), bf16),
            shape((heads, slots, slots), f32),
            shape((groups, slots, 256), bf16),
            shape((slots, features), f32),
            shape((slots, features), bf16),
        ),
        in_specs=[smem, smem] + [vmem] * (8 + len(parts)),
        out_specs=[vmem] * 8,
        cost_estimate=cost(7),
        compiler_params=params(28),
        name="attend",
    )(
        place, counts, h1, edge_sums, buckets, spatial_table, layer_in, o_bias, gain, bias,
        *parts,
    )


def group_order(place):
    return [
        (theirs, y, y * 2 + (place[3] ^ theirs)) for theirs in (1, 0) for y in (0, 1)
    ]


def feed_kernel(
    n_parts, place, mid, h2, weights_a, biases, out_bias, gain, cotangent, att_low, probs_in, *refs
):
    parts = refs[:n_parts]
    layer_out, grad_mid, grad_att_t, grad_values, mine, theirs, rows_t, sums, weights = refs[-9:]
    assemble(place, parts, weights)
    slots, features = mid.shape
    width = biases.shape[2] // 4
    depth = width // 8
    pad = 256 - width
    lanes = lax.broadcasted_iota(i32, (1, 256), 1)
    cot = cotangent[...]
    grad_ffn = cot.astype(bf16)
    h2_value = h2[...]
    layer_out[...] = mid[...] + as_row(out_bias)
    grad_h2 = jnp.zeros((slots, features), f32)
    sums[...] = jnp.zeros_like(sums)
    order = group_order(place)
    for side, y, group in order:
        columns = theirs if side else mine
        in_bias = jnp.concatenate(
            [biases[group, 0:1, 2 * width : 3 * width], jnp.zeros((1, pad), f32)], 1
        )
        pre = dot_nn(h2_value, weights[group, :, :256]) + in_bias
        cdf = 0.5 * (1.0 + lax.erf(pre * (0.5**0.5)))
        slope = cdf + pre * jnp.exp(-0.5 * pre * pre) * 0.3989422804014327
        hidden = pltpu.roll(pre * cdf, pad, 1)
        hidden = jnp.where(lanes >= pad, hidden, 0.0).astype(bf16)
        layer_out[...] += dot_nt(hidden, weights[group, :, width - pad : 2 * width])
        grad_hidden = dot_nn(grad_ffn, weights[group, :, width - pad : 2 * width])
        grad_hidden = pltpu.roll(grad_hidden, width, 1)
        grad_pre = jnp.where(lanes < width, grad_hidden * slope, 0.0).astype(bf16)
        grad_h2 = grad_h2 + dot_nt(grad_pre, weights[group, :, :256])
        columns[y, :, 0:256] = grad_pre
        columns[y, :, 256:512] = hidden
        columns[y, :, 512:768] = att_low[group]
        sums[pl.ds(12 + group, 1), 0:256] = column_sum(grad_pre.astype(f32))
    normed, scale = normalize(mid[...])
    grad = cot + normalize_back(grad_h2 * as_row(gain), normed, scale)
    grad_mid[...] = grad
    branch = grad.astype(bf16)
    sums[2:3, :] = column_sum(grad)
    sums[3:4, :] = column_sum(grad_h2 * normed)
    sums[4:5, :] = column_sum(grad_h2)
    sums[5:6, :] = column_sum(cot)
    rows_t[0] = h2_value.astype(f32).T.astype(bf16)
    rows_t[1] = grad.T.astype(bf16)
    gap = jnp.zeros((pad, slots), f32)
    for side, y, group in order:
        columns = theirs if side else mine
        grad_att = dot_nn(branch, weights_a[group]).T[pad:]
        grad_att_t[group] = jnp.concatenate([grad_att, gap], 0).astype(bf16)
        out = []
        for head in range(8):
            out.append(
                dot_nt(
                    grad_att[head * depth : (head + 1) * depth].astype(bf16),
                    probs_in[group * 8 + head].astype(bf16),
                )
            )
        low_form = jnp.concatenate(out + [gap], 0).T.astype(bf16)
        grad_values[group] = low_form
        columns[y, :, 768:1024] = jnp.concatenate([gap] + out, 0).T.astype(bf16)
        sums[pl.ds(8 + group, 1), 512:768] = column_sum(low_form.astype(f32))


def feed(place, mid, h2, weights_a, biases, out_bias, gain, cotangent, att_low, probs, parts, after=()):
    slots, features = mid.shape
    groups, width = biases.shape[0], biases.shape[2] // 4
    whole = lambda array: pl.BlockSpec(array.shape, lambda i: (0,) * len(array.shape))
    outs = (
        shape((slots, features), f32),
        shape((slots, features), f32),
        shape((groups, 256, slots), bf16),
        shape((groups, slots, 256), bf16),
        shape((2, slots, 1024), bf16),
        shape((2, slots, 1024), bf16),
        shape((2, features, slots), bf16),
        shape((16, features), f32),
    )
    rest = (biases, out_bias, gain, cotangent, att_low, probs)
    return pl.pallas_call(
        functools.partial(feed_kernel, len(parts)),
        grid=(1,),
        out_shape=outs,
        in_specs=[
            smem,
            whole(mid),
            whole(h2),
            pl.BlockSpec((groups, features, 256), lambda i: (0, 0, 2)),
        ]
        + [whole(a) for a in rest + tuple(parts)]
        + [untouched] * len(after),
        out_specs=[whole(out) for out in outs],
        scratch_shapes=[pltpu.VMEM((groups, features, 2 * width), bf16)],
        cost_estimate=cost(7),
        compiler_params=params(32),
        name="feed",
    )(place, mid, h2, weights_a, *rest, *parts, *after)


def attend_back_kernel(
    place, probs_in, value_win, transposed, grad_att_t, grad_values, weights, layer_in, gain, grad_mid,
    sums_in, after, score_grads, mine, theirs, grad_in, sums,
):
    slots, features = layer_in.shape
    width = transposed.shape[1] // 2
    depth = width // 8
    value_masks = head_masks(256, 0, depth)
    grad_h1 = jnp.zeros((slots, features), f32)
    sums[...] = sums_in[...]
    scale = depth ** (-0.5)
    for side, y, group in group_order(place):
        columns = theirs if side else mine
        values = value_win[group]
        stack = jnp.concatenate([values * mask for mask in value_masks], 0)
        grad_probs = dot_nn(stack, grad_att_t[group])
        held = transposed[group].astype(f32)
        query_out, key_out, score_out = [], [], []
        for head in range(8):
            probs = probs_in[group * 8 + head]
            part = probs * grad_probs[head * slots : (head + 1) * slots]
            exact = part - probs * column_sum(part)
            grads = exact.astype(bf16)
            score_out.append(exact)
            key_rows = held[width + head * depth : width + (head + 1) * depth]
            query_out.append(dot_nn(key_rows.astype(bf16), grads) * scale)
            query_rows = held[head * depth : (head + 1) * depth]
            key_out.append(dot_nt(query_rows.astype(bf16), grads) * scale)
        score_grads[group] = jnp.swapaxes(jnp.stack(score_out), 0, 1)
        natural = jnp.concatenate(query_out + key_out, 0).T.astype(bf16)
        columns[y] = natural
        grad_h1 = grad_h1 + dot_nt(natural, weights[group, :, : 2 * width])
        grad_h1 = grad_h1 + dot_nt(grad_values[group], weights[group, :, 2 * width : 2 * width + 256])
        sums[pl.ds(8 + group, 1), 0 : 2 * width] = column_sum(natural.astype(f32))
    normed, inverse = normalize(layer_in[...])
    grad_in[...] = grad_mid[...] + normalize_back(grad_h1 * as_row(gain), normed, inverse)
    sums[0:1, :] = column_sum(grad_h1 * normed)
    sums[1:2, :] = column_sum(grad_h1)


def attend_back(
    place, probs, value_win, transposed, grad_att_t, grad_values, weights, layer_in, gain, grad_mid, sums, after
):
    slots, features = layer_in.shape
    groups = transposed.shape[0]
    width = transposed.shape[1] // 2
    return pl.pallas_call(
        attend_back_kernel,
        out_shape=(
            shape((groups, slots, 8, slots), f32),
            shape((2, slots, 2 * width), bf16),
            shape((2, slots, 2 * width), bf16),
            shape((slots, features), f32),
            shape(sums.shape, f32),
        ),
        in_specs=[smem] + [vmem] * 10 + [untouched],
        out_specs=[vmem] * 5,
        cost_estimate=cost(7),
        compiler_params=params(24),
        name="attend_back",
    )(
        place, probs, value_win, transposed, grad_att_t, grad_values, weights, layer_in, gain, grad_mid,
        sums, after,
    )


def weight_grads_kernel(plan, n_rows, place, columns_own, columns_other, *refs):
    own_rows, other_rows = refs[:n_rows], refs[n_rows : 2 * n_rows]
    own, across, second, rows_t = refs[-4:]
    kind = 0
    for mine, other in zip(own_rows, other_rows):
        slots = mine.shape[2]
        for i in range(mine.shape[0]):
            rows_t[kind, :, 0:slots] = mine[i]
            rows_t[kind, :, slots : 2 * slots] = other[i]
            kind += 1
    core = place[3]
    height = own.shape[1]
    for which, out, at in ((3, second, 0), (2, second, 4), (1, across, 0), (0, own, 0)):
        y = relative(place, core, which, 0)[1] >> 1
        right = jnp.concatenate([columns_own[y], columns_other[y]], 0)
        for step in range(4):
            row = relative(place, core, which, step)[0]
            start = pl.multiple_of(row * height, height)
            out[at + step] = plan(lambda kind: rows_t[kind, pl.ds(start, height), :], right).astype(bf16)
    for extra in range(8, second.shape[0]):
        second[extra] = jnp.zeros(second.shape[1:], bf16)


def plan_first(rows_of, right):
    return dot_nn(rows_of(0), right)


def plan_second(rows_of, right):
    grad_in = dot_nn(rows_of(2), right[:, 0:256])
    grad_out = dot_nn(rows_of(1), right[:, 256:512])
    grad_o = dot_nn(rows_of(3), right[:, 512:768])
    grad_v = dot_nn(rows_of(0), right[:, 768:1024])
    return jnp.concatenate(
        [
            grad_in[:, :128],
            grad_in[:, 128:] + grad_out[:, :128],
            grad_out[:, 128:],
            grad_o[:, :128],
            grad_o[:, 128:] + grad_v[:, :128],
            grad_v[:, 128:],
        ],
        1,
    )


def weight_grads(
    plan, place, columns_own, columns_other, own_rows, other_rows, height, lanes, microseconds, after=(), blocks=8
):
    features, slots = own_rows[0].shape[1:]
    kinds = sum(rows.shape[0] for rows in own_rows)
    out = shape((4, height, lanes), bf16)
    return pl.pallas_call(
        functools.partial(weight_grads_kernel, plan, len(own_rows)),
        out_shape=(out, out, shape((blocks, height, lanes), bf16)),
        in_specs=[smem] + [vmem] * (2 + 2 * len(own_rows)) + [untouched] * len(after),
        out_specs=[vmem] * 3,
        scratch_shapes=[pltpu.VMEM((kinds, features, 2 * slots), bf16)],
        cost_estimate=cost(microseconds),
        compiler_params=params(20),
        name="weight_grads",
    )(place, columns_own, columns_other, *own_rows, *other_rows, *after)


def table_kernel(digit, start, stop, previous, last, place, grads, ids, buckets, *refs):
    hops = ids.shape[0]
    groups = grads.shape[0]
    heads = groups * 8
    span = 16
    if previous:
        total_in, spatial_in = refs[:2]
    if last:
        sums = refs[2]
        mine, theirs, small, total, spatial = refs[-5:]
    else:
        total, spatial = refs[-2:]
    total[...] = total_in[...] if previous else jnp.zeros_like(total)
    spatial[...] = spatial_in[...] if previous else jnp.zeros_like(spatial)
    high_count = total.shape[0] // heads
    digits = lax.broadcasted_iota(i32, (digit, 128), 0).astype(f32).astype(bf16)
    kinds = lax.broadcasted_iota(i32, (heads, 128), 0).astype(f32).astype(bf16)
    one = jnp.ones((), bf16)
    zero = jnp.zeros((), bf16)

    def body(i, carry):
        lefts, rights, plain, kind_rights = [], [], [], []
        for j in range(span):
            row = i * span + j
            piece = jnp.concatenate([grads[group, row] for group in range(groups)], 0).astype(bf16)
            bucket = buckets[pl.ds(row, 1), :].astype(f32).astype(bf16)
            plain.append(piece)
            kind_rights.append(jnp.where(jnp.broadcast_to(bucket, (heads, 128)) == kinds, one, zero))
            for hop in range(hops):
                value = ids[hop, pl.ds(row, 1), :].astype(f32)
                high = jnp.floor((value + 0.5) * (1.0 / digit))
                low = value - high * digit
                low = jnp.broadcast_to(low.astype(bf16), (digit, 128))
                high = jnp.broadcast_to(high.astype(bf16), (heads, 128))
                rights.append(jnp.where(low == digits, one, zero))
                lefts.append(
                    jnp.concatenate(
                        [jnp.where(high == jnp.full((), k, bf16), piece, zero) for k in range(high_count)], 0
                    )
                )
        total[...] += dot_nt(jnp.concatenate(lefts, 1), jnp.concatenate(rights, 1))
        spatial[...] += dot_nt(jnp.concatenate(plain, 1), jnp.concatenate(kind_rights, 1))
        return carry

    lax.fori_loop(start // span, stop // span, body, 0)
    if last:
        core = place[3]
        for other, out in ((0, mine), (1, theirs)):
            for which in range(4):
                pieces = []
                for step in range(4):
                    row, column = relative(place, core ^ other, which, step)
                    at = pl.multiple_of(row * heads + column * 8, 8)
                    pieces.append(total[pl.ds(at, 8), :] * (1.0 / hops))
                out[which * 16 : which * 16 + 8, :] = jnp.concatenate(pieces[:2], 1)
                out[which * 16 + 8 : which * 16 + 16, :] = jnp.concatenate(pieces[2:], 1)
        half = small.shape[1]
        held = sums[...]
        spread = [jnp.zeros((8, digit), f32)] + [spatial[group * 8 : (group + 1) * 8, :] for group in range(4)]
        spread.append(jnp.zeros((8, half - digit - 4 * heads), f32))
        packed = [jnp.concatenate(spread, 1), held[0:8, :half], held[0:8, half:]]
        packed.append(
            jnp.concatenate(
                [
                    jnp.concatenate([held[8:12, :digit], held[12:16, :digit]], 0),
                    jnp.concatenate([held[8:12, 512 : 512 + digit], jnp.zeros((4, digit), f32)], 0),
                ],
                1,
            )
        )
        packed = jnp.concatenate(packed, 0)
        small[...] = packed
        theirs[64:96, :] = packed


def table_grads(place, grads, ids, buckets, digit, edges, start, stop, previous=(), sums=None, after=()):
    heads = grads.shape[0] * 8
    last = sums is not None
    inner = (shape((edges // digit * heads, digit), f32), shape((heads, heads), f32))
    outs = inner
    if last:
        lanes = sums.shape[1] // 2
        outs = (shape((64, lanes), f32), shape((96, lanes), f32), shape((32, lanes), f32))
    inputs = tuple(previous) + ((sums,) if last else ())
    return pl.pallas_call(
        functools.partial(table_kernel, digit, start, stop, len(previous) > 0, last),
        out_shape=outs,
        in_specs=[smem] + [vmem] * (3 + len(inputs)) + [untouched] * len(after),
        out_specs=[vmem] * len(outs),
        scratch_shapes=[pltpu.VMEM(a.shape, f32) for a in inner] if last else [],
        cost_estimate=cost(15 * (stop - start) / grads.shape[1]),
        compiler_params=params(12),
        name="table_grads",
    )(place, grads, ids, buckets, *inputs, *after)


def meet_core_kernel(mine, small, got, after, out, keep):
    keep[...] = mine[0:32, :] + got[0:32, :]
    out[0:16, :] = mine[48:64, :] + got[48:64, :]
    out[16:32, :] = mine[32:48, :] + got[32:48, :]
    out[32:64, :] = small[...] + got[64:96, :]


def meet_near_kernel(keep, sent, got, out, kept):
    out[0:16, :] = keep[16:32, :] + got[0:16, :]
    out[16:48, :] = sent[32:64, :] + got[32:64, :]
    kept[...] = keep[0:16, :] + got[16:32, :]


def meet_far_kernel(kept, sent, got, own, first_hop, second_hop, *outs):
    table = kept[...] + got[0:16, :]
    small = sent[16:48, :] + got[16:48, :]
    digit = table.shape[1] // 2
    rows = own.shape[1]
    for step, out in enumerate(outs):
        total = own[step].astype(f32) + first_hop[step].astype(f32) + second_hop[step + 4].astype(f32)
        out[0:rows, :] = total.astype(bf16)
        block = table[(step // 2) * 8 : (step // 2) * 8 + 8, (step % 2) * digit : (step % 2 + 1) * digit]
        head = jnp.concatenate([block, small[0:8, digit:]], 1)
        out[rows:, :] = jnp.concatenate([head, small[8:32]], 0).astype(bf16)


def finish_kernel(place, own, first, second, third, after, *outs):
    total = own[...].astype(f32)
    for part in (first, second, third):
        total = total + part[...].astype(f32)
    query, key, edge, spatial = outs[:4]
    outs = outs[4:]
    rows, width = query.shape
    digit = edge.shape[1]
    query[...] = total[0:rows, 0:width]
    key[...] = total[0:rows, width : 2 * width]
    edge[...] = total[rows : rows + 8, 0:digit]
    group = place[4]
    at = rows + 8
    for i, out in enumerate(outs[:6]):
        row = jnp.concatenate([total[at + i : at + i + 1, :], total[at + 8 + i : at + 9 + i, :]], 1)
        out[...] = row.reshape(out.shape)
    at = rows + 24
    heads = total[at : at + 1]
    hidden = total[at + 4 : at + 5]
    kinds = total[rows : rows + 8, digit : digit + 32]
    for other in range(1, 4):
        heads = jnp.where(group == other, total[at + other : at + other + 1], heads)
        hidden = jnp.where(group == other, total[at + 4 + other : at + 5 + other], hidden)
        start = digit + other * 32
        kinds = jnp.where(group == other, total[rows : rows + 8, start : start + 32], kinds)
    outs[6][...] = heads[:, :width].reshape(outs[6].shape)
    outs[7][...] = heads[:, width : 2 * width].reshape(outs[7].shape)
    outs[8][...] = hidden[:, :width].reshape(outs[8].shape)
    spatial[...] = kinds[:, : spatial.shape[1]]


def small_call(kernel, name, outs, *args, waits=0, mebibytes=8):
    return pl.pallas_call(
        kernel,
        out_shape=outs,
        in_specs=[smem if args[i].ndim == 1 else vmem for i in range(len(args) - waits)]
        + [untouched] * waits,
        out_specs=[vmem] * len(outs),
        cost_estimate=cost(1),
        compiler_params=params(mebibytes),
        name=name,
    )(*args)


class Links:
    def __init__(self):
        self.core = self.hop(lambda z, x, y, c: (z, x, y, 1 - c))
        self.first = self.hop(lambda z, x, y, c: (z, x, 1 - y, c) if c else (z, 1 - x, y, c))
        self.second = self.hop(lambda z, x, y, c: (z, 1 - x, y, c) if c else (z, x, 1 - y, c))
        self.along_x = self.hop(lambda z, x, y, c: (z, 1 - x, y, c))
        self.along_y = self.hop(lambda z, x, y, c: (z, x, 1 - y, c))
        self.along_z = [self.hop(lambda z, x, y, c, k=k: (z ^ k, x, y, c)) for k in (1, 2, 3)]

    def hop(self, move):
        index = lambda z, x, y, c: (z * 2 + x) * 4 + y * 2 + c
        spots = [(z, x, y, c) for z in range(4) for x in range(2) for y in range(2) for c in range(2)]
        return [(index(*spot), index(*move(*spot))) for spot in spots]


def send(values, hop):
    return lax.ppermute(values, ("dp", "mp"), hop)


def around(links, own):
    return [own] + [send(own, hop) for hop in links.along_z]


def join_kernel(rows, count, *refs):
    out = refs[-1]
    for i in range(count):
        stop = min((i + 1) * rows, out.shape[0])
        out[i * rows : stop, :] = refs[i][0 : stop - i * rows, :]


def join(parts, rows, after=()):
    total = rows * (len(parts) - 1) + parts[-1].shape[0] if len(parts) == 5 else rows * len(parts)
    return small_call(
        functools.partial(join_kernel, rows, len(parts)), "join",
        (shape((total, parts[0].shape[1]), bf16),), *parts, *after, waits=len(after),
    )[0]


def join_pairs_kernel(rows, own, near, *refs):
    out = refs[-1]
    out[4 * rows :, :] = jnp.zeros((out.shape[0] - 4 * rows, out.shape[1]), bf16)
    for i, (part, at) in enumerate(((own, 0), (near, 0), (own, rows), (near, rows))):
        out[i * rows : (i + 1) * rows, :] = part[at : at + rows, :]


def join_pairs(own, near, rows, after):
    return small_call(
        functools.partial(join_pairs_kernel, rows), "join_pairs",
        (shape((4 * rows + 64, own.shape[1]), bf16),), own, near, *after, waits=len(after),
    )[0]


def add_kernel(count, *refs):
    for step in range(4):
        total = refs[0][step].astype(f32)
        for ref in refs[1:count]:
            total = total + ref[step].astype(f32)
        refs[-1][step] = total.astype(bf16)


def add_rounded(terms, after):
    return small_call(
        functools.partial(add_kernel, len(terms)), "add",
        (shape(terms[0].shape, bf16),), *terms, *after, waits=len(after),
    )[0]


def step_sum(refs, step):
    total = refs[0][step].astype(f32)
    for ref in refs[1:]:
        total = total + ref[step + (4 if ref.shape[0] > 4 else 0)].astype(f32)
    return total.astype(bf16)


def add_pair_kernel(count, *refs):
    stay, go = refs[-2:]
    for i in range(2):
        stay[i] = step_sum(refs[:count], 2 * i)
        go[i] = step_sum(refs[:count], 2 * i + 1)


def add_pair(terms, after):
    out = shape((2,) + terms[0].shape[1:], bf16)
    return small_call(
        functools.partial(add_pair_kernel, len(terms)), "add_pair",
        (out,) * 2, *terms, *after, waits=len(after),
    )


def add_half_kernel(count, stay, got, *refs):
    for i, out in enumerate(refs[-2:]):
        out[...] = (stay[i].astype(f32) + got[i].astype(f32)).astype(bf16)


def add_half(stay, got, after):
    out = shape(stay.shape[1:], bf16)
    return small_call(
        functools.partial(add_half_kernel, 2), "add_half", (out,) * 2, stay, got, *after, waits=len(after)
    )


def settle_kernel(count, *refs):
    total = refs[0][...].astype(f32) + refs[1][...].astype(f32)
    outs = refs[len(refs) - count :]
    width = outs[0].shape[1]
    for i, out in enumerate(outs):
        out[...] = total[:, i * width : (i + 1) * width]


def settle(terms, width, after):
    rows, lanes = terms[0].shape
    count = lanes // width
    return small_call(
        functools.partial(settle_kernel, count), "settle",
        (shape((rows, width), f32),) * count, *terms, *after, waits=len(after), mebibytes=60,
    )


def held_until(values, *others):
    return lax.optimization_barrier((values, others))[0]


def local(
    layer_in,
    node_counts,
    spatial_ids,
    path_ids,
    ln1_gain,
    ln1_bias,
    w_q,
    w_k,
    w_v,
    q_bias,
    v_bias,
    spatial_table,
    edge_table,
    w_o,
    o_bias,
    ln2_gain,
    ln2_bias,
    w_in,
    in_bias,
    w_out,
    out_bias,
    cotangent,
):
    dp_size, mp_size = lax.axis_size("dp"), lax.axis_size("mp")
    dp_index, mp_index = lax.axis_index("dp"), lax.axis_index("mp")
    staged = dp_size == 8 and mp_size == 4
    height, width = w_q.shape
    features = layer_in.shape[1]
    edges = edge_table.shape[0] * dp_size
    heads = spatial_table.shape[1]
    kinds = spatial_table.shape[0]
    hops = path_ids.shape[1]
    share = edges // 4
    digit = edges // 8
    place = jnp.stack([dp_index // 2, dp_index % 2, mp_index // 2, mp_index % 2, mp_index]).astype(i32)
    if staged:
        links = Links()
        table_t = edge_table.T
        second = pack_second(w_in, w_out)
        first, own_biases = pack_first(
            place, w_q, w_k, w_v, w_o, q_bias, v_bias, in_bias, table_t, send(table_t, links.along_x), second
        )
        chunks = around(links, first)
        ids, buckets, h1, rows_early = prepare(
            place, spatial_ids, path_ids, layer_in, ln1_gain, ln1_bias, cotangent, kinds - 1, own_biases
        )
        pair_b = join([second, send(second, links.first)], height, (h1,))
        lookup_place = place
    else:
        gathered = [
            lax.all_gather(lax.all_gather(w, "dp", axis=0, tiled=True), "mp", axis=0)
            for w in (w_q, w_k, w_v, w_o, w_in, w_out)
        ]
        bias_row = jnp.concatenate([q_bias, v_bias, in_bias, jnp.zeros((width,), f32)])
        bias_row = lax.all_gather(bias_row[None], "mp", axis=0)
        parts_a = (jnp.concatenate(gathered[:4], 2), bias_row)
        parts_b = (jnp.concatenate(gathered[4:], 2),)
        table_t = lax.all_gather(edge_table, "dp", axis=0, tiled=True).T
        half = share // 2
        chunks = []
        for i in range(4):
            low, high = (table_t[:, i * share + n * half : i * share + (n + 1) * half] for n in range(2))
            chunks.append(
                jnp.concatenate([low[: heads // 2], low[heads // 2 :], high[: heads // 2], high[heads // 2 :]], 1)
            )
        lookup_place = jnp.zeros((5,), i32)
        ids, buckets, h1, rows_early = prepare(
            place, spatial_ids, path_ids, layer_in, ln1_gain, ln1_bias, cotangent, kinds - 1, spatial_ids
        )
    edge_sums = None
    look = lambda step, after: lookup(lookup_place, chunks[step], ids, edge_sums, step, heads, after)
    if staged:
        edge_sums = look(0, (pair_b,))
        stack_a = join(chunks + [own_biases], height, (edge_sums,))
        across_a, over_a = send(stack_a, links.first), send(stack_a, links.second)
        pair_b = held_until(pair_b, stack_a)
        far_b = send(pair_b, links.along_z[1])
        other_rows_early = send(held_until(rows_early, edge_sums), links.core)
        edge_sums = look(1, (stack_a,))
        four_b = join([pair_b, far_b], 2 * height, (edge_sums,))
        near_b = send(four_b, links.along_z[0])
        edge_sums = look(2, (four_b,))
        eight_b = join_pairs(four_b, near_b, 2 * height, (edge_sums,))
        both_a = send(held_until(across_a, eight_b), links.second)
        over_b = send(eight_b, links.second)
        edge_sums = look(3, (eight_b, other_rows_early))
        mine = (stack_a, across_a, over_a)
        theirs = tuple(send(held_until(part, eight_b), links.core) for part in mine)
        parts_a = mine + (both_a,) + theirs + (send(held_until(both_a, edge_sums), links.core),)
    else:
        for step in range(4):
            edge_sums = look(step, ())

    weights, biases, transposed, value_win, probs, att_low, mid, h2 = attend(
        place, node_counts, h1, edge_sums, buckets, spatial_table,
        layer_in, o_bias, ln2_gain, ln2_bias, parts_a,
    )
    if staged:
        parts_b = (
            eight_b, over_b, send(held_until(eight_b, mid), links.core),
            send(held_until(over_b, mid), links.core),
        )
        feed_after = ()
    else:
        feed_after = ()
    layer_out, grad_mid, grad_att_t, grad_values, mine_b, theirs_b, rows_late, sums = feed(
        place, mid, h2, weights, biases, out_bias, ln2_gain, cotangent, att_low, probs, parts_b, feed_after
    )
    after = sums
    if staged:
        rows_b = (rows_early, rows_late)
        other_rows_b = (other_rows_early, send(rows_late, links.core))
        own_b, across_b, second_b = weight_grads(
            plan_second, place, mine_b, send(theirs_b, links.core), rows_b, other_rows_b, height, 4 * width, 4
        )
        got_second_b = send(second_b, links.second)
        after = own_b
    score_grads, mine_a, theirs_a, grad_layer_in, sums = attend_back(
        place, probs, value_win, transposed, grad_att_t, grad_values, weights,
        layer_in, ln1_gain, grad_mid, sums, after,
    )
    table = functools.partial(table_grads, place, score_grads, ids, buckets, digit, edges)
    slots = ids.shape[1]
    if staged:
        other_columns_a = send(theirs_a, links.core)
        partial = table(0, 16)
        own_a, across_a, second_a = weight_grads(
            plan_first, place, mine_a, other_columns_a,
            (rows_early[0:1],), (other_rows_b[0][0:1],), height, 2 * width, 2, (partial[0],), 9,
        )
        got_second_a = send(second_a, links.second)
        partial = table(16, 64, partial, after=(own_a,))
        across_b = add_rounded((across_b, got_second_b), (partial[0],))
        got_across_b = send(across_b, links.first)
        partial = table(64, 112, partial, after=(across_b,))
        mine, theirs, small = table(112, slots, partial, sums)
        got_core = send(theirs, links.core)
        stay_b, go_b = add_pair((own_b, got_across_b, got_second_b), (small,))
        got_pair_b = send(go_b, links.along_z[0])
        across_a = add_rounded((across_a, got_second_a), (stay_b,))
        got_across_a = send(across_a, links.first)
        half = features // 2
        sent, keep = small_call(
            meet_core_kernel, "meet_core", (shape((64, half), f32), shape((32, half), f32)),
            mine, small, got_core, across_a, waits=1,
        )
        sent, keep = small_call(
            meet_near_kernel, "meet_near", (shape((48, half), f32), shape((16, half), f32)),
            keep, sent, send(sent, links.second),
        )
        got_last = send(sent, links.first)
        own_b, go_b = add_half(stay_b, got_pair_b, (sent,))
        got_b = send(go_b, links.along_z[1])
        own_a = small_call(
            meet_far_kernel, "meet_far", (shape((height + 32, half), bf16),) * 4,
            keep, sent, got_last, own_a, got_across_a, got_second_a,
        )
        got_a = [send(own_a[step + 1], hop) for step, hop in enumerate(links.along_z)]
        grad_w_in, grad_w_out, grad_w_o, grad_w_v = settle([own_b, got_b], width, (own_a[0],))
        grad_w_q, grad_w_k, grad_edge, grad_spatial, *rows = small_call(
            finish_kernel, "finish",
            (shape((height, width), f32),) * 2
            + (shape((8, digit), f32), shape((8, kinds), f32))
            + (shape((features,), f32),) * 6
            + (shape((width,), f32),) * 3,
            place, own_a[0], *got_a, grad_w_in, waits=1, mebibytes=60,
        )
        grad_edge = grad_edge.T
        grad_spatial = grad_spatial.T
    else:
        contract = lambda a, b: lax.dot_general(
            a, b, (((1,), (1,)), ((), ())), preferred_element_type=f32
        )

        def unmix(mine, theirs):
            even = mp_index % 2 == 0
            cores = jnp.where(even, jnp.stack([mine, theirs], 1), jnp.stack([theirs, mine], 1))
            return cores.reshape(4, *mine.shape[1:])

        def scatter(rows_t, columns):
            grads = contract(rows_t, columns)
            grads = jnp.transpose(grads, (1, 0, 2))
            grads = lax.psum_scatter(grads, "mp", scatter_dimension=0, tiled=False)
            return lax.psum_scatter(grads, "dp", scatter_dimension=0, tiled=True)

        columns_a, columns_b = unmix(mine_a, theirs_a), unmix(mine_b, theirs_b)
        grad_w_q, grad_w_k = (
            scatter(rows_early[0], columns_a[:, :, i * width : (i + 1) * width]) for i in range(2)
        )
        grad_w_v = scatter(rows_early[0], columns_b[:, :, 1024 - width :])
        grad_w_in = scatter(rows_late[0], columns_b[:, :, :width])
        grad_w_out = scatter(rows_early[1], columns_b[:, :, 512 - width : 512])
        grad_w_o = scatter(rows_late[1], columns_b[:, :, 512 : 512 + width])
        table, spatial = table(0, slots)
        table = table.reshape(-1, heads, digit).transpose(0, 2, 1).reshape(edges, heads) / hops
        table = lax.psum_scatter(table, "dp", scatter_dimension=0, tiled=True)
        table = lax.psum(table, "mp")
        grad_edge = lax.dynamic_slice_in_dim(table, mp_index * 8, 8, 1)
        totals, spatial = lax.psum((sums, spatial), ("dp", "mp"))
        grad_spatial = lax.dynamic_slice_in_dim(spatial[:, :kinds], mp_index * 8, 8, 0).T
        head_sums = lax.dynamic_slice_in_dim(totals, 8 + mp_index, 1, 0)[0]
        hidden_sums = lax.dynamic_slice_in_dim(totals, 12 + mp_index, 1, 0)[0]
        rows = [totals[i] for i in range(6)]
        rows += [head_sums[:width], head_sums[512 : 512 + width], hidden_sums[:width]]
    return (
        layer_out,
        grad_layer_in,
        rows[0],
        rows[1],
        grad_w_q,
        grad_w_k,
        grad_w_v,
        rows[6],
        rows[7],
        grad_spatial,
        grad_edge,
        grad_w_o,
        rows[2],
        rows[3],
        rows[4],
        grad_w_in,
        rows[8],
        grad_w_out,
        rows[5],
    )


def solution(mesh):
    return jax.shard_map(
        local,
        mesh=mesh,
        in_specs=(
            P(("dp", "mp"), None),
            P("dp"),
            P("dp", None, None),
            P("dp", None, None, None),
            P(),
            P(),
            P("dp", "mp"),
            P("dp", "mp"),
            P("dp", "mp"),
            P("mp"),
            P("mp"),
            P(),
            P("dp", None),
            P("dp", "mp"),
            P(),
            P(),
            P(),
            P("dp", "mp"),
            P("mp"),
            P("dp", "mp"),
            P(),
            P(("dp", "mp"), None),
        ),
        out_specs=(
            P(("dp", "mp"), None),
            P(("dp", "mp"), None),
            P(),
            P(),
            P("dp", "mp"),
            P("dp", "mp"),
            P("dp", "mp"),
            P("mp"),
            P("mp"),
            P(None, "mp"),
            P("dp", "mp"),
            P("dp", "mp"),
            P(),
            P(),
            P(),
            P("dp", "mp"),
            P("mp"),
            P("dp", "mp"),
            P(),
        ),
        check_vma=False,
    )
```

```python
import functools

import jax
import jax.numpy as jnp
from jax import lax
from jax.experimental import pallas as pl
from jax.experimental.pallas import tpu as pltpu
from jax.sharding import PartitionSpec as P

epsilon = 1e-05
masked_score = -1e30
edge_unit = 1638.0
spatial_unit = 4096.0
hurry = 0.02
bf16 = jnp.bfloat16
f32 = jnp.float32
i32 = jnp.int32
vmem = pl.BlockSpec(memory_space=pltpu.VMEM)
smem = pl.BlockSpec(memory_space=pltpu.SMEM)
hbm = pl.BlockSpec(memory_space=pltpu.HBM)
untouched = pl.BlockSpec(memory_space=pl.ANY)


def params(mebibytes):
    return pltpu.CompilerParams(vmem_limit_bytes=mebibytes << 20)


def normalize(values):
    centred = values - jnp.mean(values, axis=-1, keepdims=True)
    scale = lax.rsqrt(jnp.mean(centred * centred, axis=-1, keepdims=True) + epsilon)
    return (centred * scale, scale)


def normalize_back(grad_normed, normed, scale):
    inner = grad_normed - jnp.mean(grad_normed, axis=-1, keepdims=True)
    inner = inner - normed * jnp.mean(grad_normed * normed, axis=-1, keepdims=True)
    return inner * scale


def dot_nn(left, right):
    return lax.dot_general(
        left, right, (((1,), (0,)), ((), ())), preferred_element_type=f32
    )


def dot_nt(left, right):
    return lax.dot_general(
        left, right, (((1,), (1,)), ((), ())), preferred_element_type=f32
    )


def column_sum(values):
    return jnp.sum(values, axis=0, keepdims=True)


def cost(microseconds):
    return pl.CostEstimate(flops=int(microseconds * hurry * 1.15e9), bytes_accessed=1024, transcendentals=0)


def as_row(ref):
    return ref[...].reshape(1, -1)


def shape(dims, kind):
    return jax.ShapeDtypeStruct(dims, kind)


def relative(place, side, which, step):
    z, x, y = place[0], place[1], place[2]
    flip_x = (0, 1 - side, side, 1)[which]
    flip_y = (0, side, 1 - side, 1)[which]
    row = (z ^ step) * 2 + (x ^ flip_x)
    column = (y ^ flip_y) * 2 + side
    return row, column


def three_terms(values):
    terms = []
    for _ in range(3):
        term = values.astype(bf16)
        terms.append(term)
        values = values - term.astype(f32)
    return terms


def pack_first_kernel(place, wq, wk, wv, wo, bq, bv, bi, edge, neighbour, after, weights, biases, held, sems):
    copies = [
        pltpu.make_async_copy(source, held.at[i], sems.at[i]) for i, source in enumerate((wq, wk, wv, wo))
    ]
    for copy in copies:
        copy.start()
    row = jnp.concatenate([as_row(bq), as_row(bv), as_row(bi)], 1)
    lanes = weights.shape[1]
    row = jnp.concatenate([row, jnp.zeros((1, lanes - row.shape[1]), f32)], 1)
    terms = [term.astype(f32) for term in three_terms(row)]
    biases[...] = jnp.concatenate(terms + [jnp.zeros((13, lanes), f32)], 0).astype(bf16)
    even = place[1] == 0
    mine, other = edge[...].astype(f32), neighbour[...].astype(f32)
    low, high = jnp.where(even, mine, other), jnp.where(even, other, mine)
    rows = held.shape[1]
    half = low.shape[0] // 2
    weights[rows:, :] = jnp.concatenate([low[:half], low[half:], high[:half], high[half:]], 1).astype(bf16)
    for copy in copies:
        copy.wait()
    weights[0:rows, :] = jnp.concatenate([held[i] for i in range(4)], 1)


def pack_first(place, wq, wk, wv, wo, bq, bv, bi, edge, neighbour, after):
    rows, width = wq.shape
    return pl.pallas_call(
        pack_first_kernel,
        out_shape=(shape((rows + 16, 4 * width), bf16), shape((16, 4 * width), bf16)),
        in_specs=[smem] + [hbm] * 4 + [vmem] * 5 + [untouched],
        out_specs=[vmem] * 2,
        scratch_shapes=[pltpu.VMEM((4, rows, width), bf16), pltpu.SemaphoreType.DMA((4,))],
        cost_estimate=cost(2),
        compiler_params=params(60),
        name="pack_first",
    )(place, wq, wk, wv, wo, bq, bv, bi, edge, neighbour, after)


def pack_second_kernel(wi, wu, out):
    out[...] = jnp.concatenate([wi[...], wu[...]], 1)


def pack_second(wi, wu):
    rows, width = wi.shape
    return pl.pallas_call(
        pack_second_kernel,
        out_shape=shape((rows, 2 * width), bf16),
        in_specs=[vmem] * 2,
        out_specs=vmem,
        cost_estimate=cost(1),
        compiler_params=params(60),
        name="pack_second",
    )(wi, wu)


def prepare_kernel(
    virtual, place, spatial, path, layer_in, gain, bias, cotangent, after, ids, buckets, h1, rows_t
):
    slots = spatial.shape[1]
    for hop in range(path.shape[1]):
        ids[hop] = path[0, hop].T
    rows = lax.broadcasted_iota(i32, (slots, slots), 0)
    columns = lax.broadcasted_iota(i32, (slots, slots), 1)
    buckets[...] = jnp.where((rows == 0) | (columns == 0), virtual, spatial[0].T)
    normed, scale = normalize(layer_in[...])
    out = normed * as_row(gain) + as_row(bias)
    h1[...] = out.astype(bf16)
    rows_t[0] = out.T.astype(bf16)
    rows_t[1] = cotangent[...].T.astype(bf16)


def prepare(place, spatial, path, layer_in, gain, bias, cotangent, virtual, after):
    hops, slots = path.shape[1], path.shape[2]
    rows, width = layer_in.shape
    whole = lambda dims: pl.BlockSpec(dims, lambda i, s: (0,) * len(dims))
    return pl.pallas_call(
        functools.partial(prepare_kernel, virtual),
        grid_spec=pltpu.PrefetchScalarGridSpec(
            num_scalar_prefetch=1,
            grid=(1,),
            in_specs=[
                pl.BlockSpec((1, slots, slots), lambda i, s: (s[4], 0, 0)),
                pl.BlockSpec((1, hops, slots, slots), lambda i, s: (s[4], 0, 0, 0)),
                whole((rows, width)),
                whole((width,)),
                whole((width,)),
                whole((rows, width)),
                untouched,
            ],
            out_specs=[
                whole((hops, slots, slots)),
                whole((slots, slots)),
                whole((rows, width)),
                whole((2, width, rows)),
            ],
        ),
        out_shape=(
            shape((hops, slots, slots), i32),
            shape((slots, slots), i32),
            shape((rows, width), bf16),
            shape((2, width, rows), bf16),
        ),
        compiler_params=params(62),
        cost_estimate=cost(1),
        name="prepare",
    )(place, spatial, path, layer_in, gain, bias, cotangent, after)


def quantize(table, unit):
    held = jnp.round(table.astype(f32) * unit).astype(i32)
    partner = jnp.concatenate([held[4:], held[:4]], 0)
    return held + partner * 65536


def lanes_gather(table, places):
    return jnp.take_along_axis(table, places, axis=1, mode="promise_in_bounds")


def lookup_kernel(first, step, share, place, chunk, ids, *refs):
    total, table = refs[-2:]
    previous = None if first else refs[0]
    hops, slots = ids.shape[0], ids.shape[1]
    pairs = total.shape[0]
    below = chunk[chunk.shape[0] - 16 :, :]
    half = share // 2
    below = [below[:, i * half : (i + 1) * half] for i in range(4)]
    packed = quantize(
        jnp.concatenate(
            [jnp.concatenate([below[0], below[2]], 1), jnp.concatenate([below[1], below[3]], 1)], 0
        ),
        edge_unit,
    )
    blocks = share // 128
    for pair in range(pairs):
        head = (pair // 4) * 8 + pair % 4
        for block in range(blocks):
            table[pair, block] = jnp.broadcast_to(
                packed[head : head + 1, block * 128 : (block + 1) * 128], (8, 128)
            )
    base = (place[0] ^ step) * share

    def body(i, carry):
        offset = pl.multiple_of(i * 8, 8)
        sums = [None] * pairs
        if not first:
            sums = [previous[pair, pl.ds(offset, 8), :] for pair in range(pairs)]
        for hop in range(hops):
            relative_id = ids[hop, pl.ds(offset, 8), :] - base
            low = relative_id & 127
            high = relative_id >> 7
            masks = [high == block for block in range(blocks)]
            for pair in range(pairs):
                value = jnp.zeros((8, 128), i32)
                for block in range(blocks):
                    value = jnp.where(masks[block], lanes_gather(table[pair, block], low), value)
                sums[pair] = value if sums[pair] is None else sums[pair] + value
        for pair in range(pairs):
            total[pair, pl.ds(offset, 8), :] = sums[pair]
        return carry

    lax.fori_loop(0, slots // 8, body, 0)


def lookup(place, chunk, ids, previous, step, heads, after=()):
    share = chunk.shape[1] // 2
    pairs = heads // 2
    slots = ids.shape[1]
    first = previous is None
    out = shape((pairs, slots, slots), i32)
    return pl.pallas_call(
        functools.partial(lookup_kernel, first, step, share),
        out_shape=out,
        in_specs=[smem] + [vmem] * (2 if first else 3) + [untouched] * len(after),
        out_specs=vmem,
        scratch_shapes=[pltpu.VMEM((pairs, share // 128, 8, 128), i32)],
        input_output_aliases={} if first else {3: 0},
        compiler_params=params(8),
        cost_estimate=cost(6),
        name="lookup",
    )(place, chunk, ids, *(() if first else (previous,)), *after)


def assemble(place, parts, whole, biases=None):
    if len(parts) <= 2:
        whole[...] = parts[0][...]
        return
    core = place[3]
    rows = whole.shape[1] // 8
    each = len(parts) // 2
    for other in range(2):
        for which in range(4):
            for step in range(4):
                row, column = relative(place, core ^ other, which, step)
                start = pl.multiple_of(row * rows, rows)
                part = parts[other * each + which // (4 // each)]
                at = (step * (4 // each) + which % (4 // each)) * rows
                whole[column, pl.ds(start, rows), :] = part[at : at + rows, :]
            if biases is not None:
                terms = parts[other * each + which][4 * rows : 4 * rows + 16, :].astype(f32)
                biases[column] = terms[0:1] + terms[1:2] + terms[2:3]


def head_masks(width, offset, depth):
    lanes = lax.broadcasted_iota(i32, (1, width), 1)
    out = []
    for head in range(8):
        start = offset + head * depth
        out.append(((lanes >= start) & (lanes < start + depth)).astype(f32).astype(bf16))
    return out


def attend_kernel(
    n_parts, place, counts, h1, edge_sums, buckets, spatial_table, layer_in, o_bias, gain, bias, *refs
):
    parts, refs = refs[:n_parts], refs[n_parts:]
    weights, biases, transposed, value_win, probs_out, att_low, mid, h2 = refs
    assemble(place, parts, weights, biases)
    if n_parts == 2:
        biases[...] = parts[1][...]
    slots = h1.shape[0]
    groups, width = biases.shape[0], biases.shape[2] // 4
    depth = width // 8
    pad = 256 - width
    hops = 5
    count = counts[place[4]]
    packed = quantize(spatial_table[...].astype(f32).T, spatial_unit)
    packed = jnp.concatenate([packed, jnp.zeros((packed.shape[0], 128 - packed.shape[1]), i32)], 1)
    hidden_key = lax.broadcasted_iota(i32, (slots, slots), 0) > count
    bucket = buckets[...]
    key_masks = head_masks(256, pad, depth)
    mid[...] = layer_in[...] + as_row(o_bias)
    for group in range(groups):
        natural = dot_nn(h1[...], weights[group, :, : 3 * width + pad])
        row_bias = jnp.concatenate(
            [
                biases[group, 0:1, :width],
                jnp.zeros((1, width), f32),
                biases[group, 0:1, width : 2 * width],
                jnp.zeros((1, pad), f32),
            ],
            1,
        )
        natural = natural + row_bias
        natural_t = natural.T
        transposed[group] = natural_t[: 2 * width].astype(bf16)
        natural = natural.astype(bf16)
        value_win[group] = natural[:, 2 * width : 2 * width + 256]
        keys = natural[:, width - pad : 2 * width]
        stack = jnp.concatenate([keys * mask for mask in key_masks], 0)
        query = jnp.concatenate([jnp.zeros((pad, slots), f32), natural_t[:width]], 0).astype(bf16)
        scores = dot_nn(stack, query) * depth ** (-0.5)
        out = [None] * 8
        for pair in range(4):
            word = edge_sums[group * 4 + pair]
            head = group * 8 + pair
            spatial_word = lanes_gather(
                jnp.broadcast_to(packed[head : head + 1], (slots, 128)), bucket
            )
            low = (word << 16) >> 16
            spatial_low = (spatial_word << 16) >> 16
            high = (word - low) >> 16
            spatial_high = (spatial_word - spatial_low) >> 16
            for part, spatial_part, spot in ((low, spatial_low, pair), (high, spatial_high, pair + 4)):
                pair_bias = part.astype(f32) * (1.0 / (edge_unit * hops))
                pair_bias = pair_bias + spatial_part.astype(f32) * (1.0 / spatial_unit)
                score = scores[spot * slots : (spot + 1) * slots] + pair_bias
                score = jnp.where(hidden_key, masked_score, score)
                weight = jnp.exp(score - jnp.max(score, axis=0, keepdims=True))
                probs = weight * (1.0 / column_sum(weight))
                probs_out[group * 8 + spot] = probs
                values = natural_t[2 * width + spot * depth : 2 * width + (spot + 1) * depth]
                out[spot] = dot_nn(values.astype(bf16), probs.astype(bf16))
        gap = jnp.zeros((pad, slots), f32)
        att_low[group] = jnp.concatenate(out + [gap], 0).T.astype(bf16)
        high_form = jnp.concatenate([gap] + out, 0).T.astype(bf16)
        mid[...] += dot_nt(high_form, weights[group, :, 3 * width - pad : 4 * width])
    normed, scale = normalize(mid[...])
    h2[...] = (normed * as_row(gain) + as_row(bias)).astype(bf16)


def attend(place, counts, h1, edge_sums, buckets, spatial_table, layer_in, o_bias, gain, bias, parts):
    slots, features = h1.shape
    width = parts[0].shape[-1] // 4
    heads = spatial_table.shape[1]
    groups = heads // 8
    return pl.pallas_call(
        functools.partial(attend_kernel, len(parts)),
        out_shape=(
            shape((groups, features, 4 * width), bf16),
            shape((groups, 1, 4 * width), f32),
            shape((groups, 2 * width, slots), bf16),
            shape((groups, slots, 256), bf16),
            shape((heads, slots, slots), f32),
            shape((groups, slots, 256), bf16),
            shape((slots, features), f32),
            shape((slots, features), bf16),
        ),
        in_specs=[smem, smem] + [vmem] * (8 + len(parts)),
        out_specs=[vmem] * 8,
        cost_estimate=cost(7),
        compiler_params=params(28),
        name="attend",
    )(
        place, counts, h1, edge_sums, buckets, spatial_table, layer_in, o_bias, gain, bias,
        *parts,
    )


def group_order(place):
    return [
        (theirs, y, y * 2 + (place[3] ^ theirs)) for theirs in (1, 0) for y in (0, 1)
    ]


def feed_kernel(
    n_parts, place, mid, h2, weights_a, biases, out_bias, gain, cotangent, att_low, probs_in, *refs
):
    parts = refs[:n_parts]
    layer_out, grad_mid, grad_att_t, grad_values, mine, theirs, rows_t, sums, weights = refs[-9:]
    assemble(place, parts, weights)
    slots, features = mid.shape
    width = biases.shape[2] // 4
    depth = width // 8
    pad = 256 - width
    lanes = lax.broadcasted_iota(i32, (1, 256), 1)
    cot = cotangent[...]
    grad_ffn = cot.astype(bf16)
    h2_value = h2[...]
    layer_out[...] = mid[...] + as_row(out_bias)
    grad_h2 = jnp.zeros((slots, features), f32)
    sums[...] = jnp.zeros_like(sums)
    order = group_order(place)
    for side, y, group in order:
        columns = theirs if side else mine
        in_bias = jnp.concatenate(
            [biases[group, 0:1, 2 * width : 3 * width], jnp.zeros((1, pad), f32)], 1
        )
        pre = dot_nn(h2_value, weights[group, :, :256]) + in_bias
        cdf = 0.5 * (1.0 + lax.erf(pre * (0.5**0.5)))
        slope = cdf + pre * jnp.exp(-0.5 * pre * pre) * 0.3989422804014327
        hidden = pltpu.roll(pre * cdf, pad, 1)
        hidden = jnp.where(lanes >= pad, hidden, 0.0).astype(bf16)
        layer_out[...] += dot_nt(hidden, weights[group, :, width - pad : 2 * width])
        grad_hidden = dot_nn(grad_ffn, weights[group, :, width - pad : 2 * width])
        grad_hidden = pltpu.roll(grad_hidden, width, 1)
        grad_pre = jnp.where(lanes < width, grad_hidden * slope, 0.0).astype(bf16)
        grad_h2 = grad_h2 + dot_nt(grad_pre, weights[group, :, :256])
        columns[y, :, 0:256] = grad_pre
        columns[y, :, 256:512] = hidden
        columns[y, :, 512:768] = att_low[group]
        sums[pl.ds(12 + group, 1), 0:256] = column_sum(grad_pre.astype(f32))
    normed, scale = normalize(mid[...])
    grad = cot + normalize_back(grad_h2 * as_row(gain), normed, scale)
    grad_mid[...] = grad
    branch = grad.astype(bf16)
    sums[2:3, :] = column_sum(grad)
    sums[3:4, :] = column_sum(grad_h2 * normed)
    sums[4:5, :] = column_sum(grad_h2)
    sums[5:6, :] = column_sum(cot)
    rows_t[0] = h2_value.astype(f32).T.astype(bf16)
    rows_t[1] = grad.T.astype(bf16)
    gap = jnp.zeros((pad, slots), f32)
    for side, y, group in order:
        columns = theirs if side else mine
        grad_att = dot_nn(branch, weights_a[group]).T[pad:]
        grad_att_t[group] = jnp.concatenate([grad_att, gap], 0).astype(bf16)
        out = []
        for head in range(8):
            out.append(
                dot_nt(
                    grad_att[head * depth : (head + 1) * depth].astype(bf16),
                    probs_in[group * 8 + head].astype(bf16),
                )
            )
        low_form = jnp.concatenate(out + [gap], 0).T.astype(bf16)
        grad_values[group] = low_form
        columns[y, :, 768:1024] = jnp.concatenate([gap] + out, 0).T.astype(bf16)
        sums[pl.ds(8 + group, 1), 512:768] = column_sum(low_form.astype(f32))


def feed(place, mid, h2, weights_a, biases, out_bias, gain, cotangent, att_low, probs, parts, after=()):
    slots, features = mid.shape
    groups, width = biases.shape[0], biases.shape[2] // 4
    whole = lambda array: pl.BlockSpec(array.shape, lambda i: (0,) * len(array.shape))
    outs = (
        shape((slots, features), f32),
        shape((slots, features), f32),
        shape((groups, 256, slots), bf16),
        shape((groups, slots, 256), bf16),
        shape((2, slots, 1024), bf16),
        shape((2, slots, 1024), bf16),
        shape((2, features, slots), bf16),
        shape((16, features), f32),
    )
    rest = (biases, out_bias, gain, cotangent, att_low, probs)
    return pl.pallas_call(
        functools.partial(feed_kernel, len(parts)),
        grid=(1,),
        out_shape=outs,
        in_specs=[
            smem,
            whole(mid),
            whole(h2),
            pl.BlockSpec((groups, features, 256), lambda i: (0, 0, 2)),
        ]
        + [whole(a) for a in rest + tuple(parts)]
        + [untouched] * len(after),
        out_specs=[whole(out) for out in outs],
        scratch_shapes=[pltpu.VMEM((groups, features, 2 * width), bf16)],
        cost_estimate=cost(7),
        compiler_params=params(32),
        name="feed",
    )(place, mid, h2, weights_a, *rest, *parts, *after)


def attend_back_kernel(
    place, probs_in, value_win, transposed, grad_att_t, grad_values, weights, layer_in, gain, grad_mid,
    sums_in, after, score_grads, mine, theirs, grad_in, sums,
):
    slots, features = layer_in.shape
    width = transposed.shape[1] // 2
    depth = width // 8
    value_masks = head_masks(256, 0, depth)
    grad_h1 = jnp.zeros((slots, features), f32)
    sums[...] = sums_in[...]
    scale = depth ** (-0.5)
    for side, y, group in group_order(place):
        columns = theirs if side else mine
        values = value_win[group]
        stack = jnp.concatenate([values * mask for mask in value_masks], 0)
        grad_probs = dot_nn(stack, grad_att_t[group])
        held = transposed[group].astype(f32)
        query_out, key_out, score_out = [], [], []
        for head in range(8):
            probs = probs_in[group * 8 + head]
            part = probs * grad_probs[head * slots : (head + 1) * slots]
            exact = part - probs * column_sum(part)
            grads = exact.astype(bf16)
            score_out.append(exact)
            key_rows = held[width + head * depth : width + (head + 1) * depth]
            query_out.append(dot_nn(key_rows.astype(bf16), grads) * scale)
            query_rows = held[head * depth : (head + 1) * depth]
            key_out.append(dot_nt(query_rows.astype(bf16), grads) * scale)
        score_grads[group] = jnp.swapaxes(jnp.stack(score_out), 0, 1)
        natural = jnp.concatenate(query_out + key_out, 0).T.astype(bf16)
        columns[y] = natural
        grad_h1 = grad_h1 + dot_nt(natural, weights[group, :, : 2 * width])
        grad_h1 = grad_h1 + dot_nt(grad_values[group], weights[group, :, 2 * width : 2 * width + 256])
        sums[pl.ds(8 + group, 1), 0 : 2 * width] = column_sum(natural.astype(f32))
    normed, inverse = normalize(layer_in[...])
    grad_in[...] = grad_mid[...] + normalize_back(grad_h1 * as_row(gain), normed, inverse)
    sums[0:1, :] = column_sum(grad_h1 * normed)
    sums[1:2, :] = column_sum(grad_h1)


def attend_back(
    place, probs, value_win, transposed, grad_att_t, grad_values, weights, layer_in, gain, grad_mid, sums, after
):
    slots, features = layer_in.shape
    groups = transposed.shape[0]
    width = transposed.shape[1] // 2
    return pl.pallas_call(
        attend_back_kernel,
        out_shape=(
            shape((groups, slots, 8, slots), f32),
            shape((2, slots, 2 * width), bf16),
            shape((2, slots, 2 * width), bf16),
            shape((slots, features), f32),
            shape(sums.shape, f32),
        ),
        in_specs=[smem] + [vmem] * 10 + [untouched],
        out_specs=[vmem] * 5,
        cost_estimate=cost(7),
        compiler_params=params(24),
        name="attend_back",
    )(
        place, probs, value_win, transposed, grad_att_t, grad_values, weights, layer_in, gain, grad_mid,
        sums, after,
    )


def weight_grads_kernel(plan, n_rows, place, columns_own, columns_other, *refs):
    own_rows, other_rows = refs[:n_rows], refs[n_rows : 2 * n_rows]
    own, across, second, rows_t = refs[-4:]
    kind = 0
    for mine, other in zip(own_rows, other_rows):
        slots = mine.shape[2]
        for i in range(mine.shape[0]):
            rows_t[kind, :, 0:slots] = mine[i]
            rows_t[kind, :, slots : 2 * slots] = other[i]
            kind += 1
    core = place[3]
    height = own.shape[1]
    for which, out, at in ((3, second, 0), (2, second, 4), (1, across, 0), (0, own, 0)):
        y = relative(place, core, which, 0)[1] >> 1
        right = jnp.concatenate([columns_own[y], columns_other[y]], 0)
        for step in range(4):
            row = relative(place, core, which, step)[0]
            start = pl.multiple_of(row * height, height)
            out[at + step] = plan(lambda kind: rows_t[kind, pl.ds(start, height), :], right).astype(bf16)
    for extra in range(8, second.shape[0]):
        second[extra] = jnp.zeros(second.shape[1:], bf16)


def plan_first(rows_of, right):
    return dot_nn(rows_of(0), right)


def plan_second(rows_of, right):
    grad_in = dot_nn(rows_of(2), right[:, 0:256])
    grad_out = dot_nn(rows_of(1), right[:, 256:512])
    grad_o = dot_nn(rows_of(3), right[:, 512:768])
    grad_v = dot_nn(rows_of(0), right[:, 768:1024])
    return jnp.concatenate(
        [
            grad_in[:, :128],
            grad_in[:, 128:] + grad_out[:, :128],
            grad_out[:, 128:],
            grad_o[:, :128],
            grad_o[:, 128:] + grad_v[:, :128],
            grad_v[:, 128:],
        ],
        1,
    )


def weight_grads(
    plan, place, columns_own, columns_other, own_rows, other_rows, height, lanes, microseconds, after=(), blocks=8
):
    features, slots = own_rows[0].shape[1:]
    kinds = sum(rows.shape[0] for rows in own_rows)
    out = shape((4, height, lanes), bf16)
    return pl.pallas_call(
        functools.partial(weight_grads_kernel, plan, len(own_rows)),
        out_shape=(out, out, shape((blocks, height, lanes), bf16)),
        in_specs=[smem] + [vmem] * (2 + 2 * len(own_rows)) + [untouched] * len(after),
        out_specs=[vmem] * 3,
        scratch_shapes=[pltpu.VMEM((kinds, features, 2 * slots), bf16)],
        cost_estimate=cost(microseconds),
        compiler_params=params(20),
        name="weight_grads",
    )(place, columns_own, columns_other, *own_rows, *other_rows, *after)


def table_kernel(digit, start, stop, previous, last, place, grads, ids, buckets, *refs):
    hops = ids.shape[0]
    groups = grads.shape[0]
    heads = groups * 8
    span = 16
    if previous:
        total_in, spatial_in = refs[:2]
    if last:
        sums = refs[2]
        mine, theirs, small, total, spatial = refs[-5:]
    else:
        total, spatial = refs[-2:]
    total[...] = total_in[...] if previous else jnp.zeros_like(total)
    spatial[...] = spatial_in[...] if previous else jnp.zeros_like(spatial)
    high_count = total.shape[0] // heads
    digits = lax.broadcasted_iota(i32, (digit, 128), 0).astype(f32).astype(bf16)
    kinds = lax.broadcasted_iota(i32, (heads, 128), 0).astype(f32).astype(bf16)
    one = jnp.ones((), bf16)
    zero = jnp.zeros((), bf16)

    def body(i, carry):
        lefts, rights, plain, kind_rights = [], [], [], []
        for j in range(span):
            row = i * span + j
            piece = jnp.concatenate([grads[group, row] for group in range(groups)], 0).astype(bf16)
            bucket = buckets[pl.ds(row, 1), :].astype(f32).astype(bf16)
            plain.append(piece)
            kind_rights.append(jnp.where(jnp.broadcast_to(bucket, (heads, 128)) == kinds, one, zero))
            for hop in range(hops):
                value = ids[hop, pl.ds(row, 1), :].astype(f32)
                high = jnp.floor((value + 0.5) * (1.0 / digit))
                low = value - high * digit
                low = jnp.broadcast_to(low.astype(bf16), (digit, 128))
                high = jnp.broadcast_to(high.astype(bf16), (heads, 128))
                rights.append(jnp.where(low == digits, one, zero))
                lefts.append(
                    jnp.concatenate(
                        [jnp.where(high == jnp.full((), k, bf16), piece, zero) for k in range(high_count)], 0
                    )
                )
        total[...] += dot_nt(jnp.concatenate(lefts, 1), jnp.concatenate(rights, 1))
        spatial[...] += dot_nt(jnp.concatenate(plain, 1), jnp.concatenate(kind_rights, 1))
        return carry

    lax.fori_loop(start // span, stop // span, body, 0)
    if last:
        core = place[3]
        for other, out in ((0, mine), (1, theirs)):
            for which in range(4):
                pieces = []
                for step in range(4):
                    row, column = relative(place, core ^ other, which, step)
                    at = pl.multiple_of(row * heads + column * 8, 8)
                    pieces.append(total[pl.ds(at, 8), :] * (1.0 / hops))
                out[which * 16 : which * 16 + 8, :] = jnp.concatenate(pieces[:2], 1)
                out[which * 16 + 8 : which * 16 + 16, :] = jnp.concatenate(pieces[2:], 1)
        half = small.shape[1]
        held = sums[...]
        spread = [jnp.zeros((8, digit), f32)] + [spatial[group * 8 : (group + 1) * 8, :] for group in range(4)]
        spread.append(jnp.zeros((8, half - digit - 4 * heads), f32))
        packed = [jnp.concatenate(spread, 1), held[0:8, :half], held[0:8, half:]]
        packed.append(
            jnp.concatenate(
                [
                    jnp.concatenate([held[8:12, :digit], held[12:16, :digit]], 0),
                    jnp.concatenate([held[8:12, 512 : 512 + digit], jnp.zeros((4, digit), f32)], 0),
                ],
                1,
            )
        )
        packed = jnp.concatenate(packed, 0)
        small[...] = packed
        theirs[64:96, :] = packed


def table_grads(place, grads, ids, buckets, digit, edges, start, stop, previous=(), sums=None, after=()):
    heads = grads.shape[0] * 8
    last = sums is not None
    inner = (shape((edges // digit * heads, digit), f32), shape((heads, heads), f32))
    outs = inner
    if last:
        lanes = sums.shape[1] // 2
        outs = (shape((64, lanes), f32), shape((96, lanes), f32), shape((32, lanes), f32))
    inputs = tuple(previous) + ((sums,) if last else ())
    return pl.pallas_call(
        functools.partial(table_kernel, digit, start, stop, len(previous) > 0, last),
        out_shape=outs,
        in_specs=[smem] + [vmem] * (3 + len(inputs)) + [untouched] * len(after),
        out_specs=[vmem] * len(outs),
        scratch_shapes=[pltpu.VMEM(a.shape, f32) for a in inner] if last else [],
        cost_estimate=cost(15 * (stop - start) / grads.shape[1]),
        compiler_params=params(12),
        name="table_grads",
    )(place, grads, ids, buckets, *inputs, *after)


def meet_core_kernel(mine, small, got, after, out, keep):
    keep[...] = mine[0:32, :] + got[0:32, :]
    out[0:16, :] = mine[48:64, :] + got[48:64, :]
    out[16:32, :] = mine[32:48, :] + got[32:48, :]
    out[32:64, :] = small[...] + got[64:96, :]


def meet_near_kernel(keep, sent, got, after, out, kept):
    out[0:16, :] = keep[16:32, :] + got[0:16, :]
    out[16:48, :] = sent[32:64, :] + got[32:64, :]
    kept[...] = keep[0:16, :] + got[16:32, :]


def meet_far_kernel(kept, sent, got, own, first_hop, second_hop, *outs):
    table = kept[...] + got[0:16, :]
    small = sent[16:48, :] + got[16:48, :]
    digit = table.shape[1] // 2
    rows = own.shape[1]
    for step, out in enumerate(outs):
        total = own[step].astype(f32) + first_hop[step].astype(f32) + second_hop[step + 4].astype(f32)
        out[0:rows, :] = total.astype(bf16)
        block = table[(step // 2) * 8 : (step // 2) * 8 + 8, (step % 2) * digit : (step % 2 + 1) * digit]
        head = jnp.concatenate([block, small[0:8, digit:]], 1)
        out[rows:, :] = jnp.concatenate([head, small[8:32]], 0).astype(bf16)


def finish_kernel(place, own, first, second, third, after, *outs):
    total = own[...].astype(f32)
    for part in (first, second, third):
        total = total + part[...].astype(f32)
    query, key, edge, spatial = outs[:4]
    outs = outs[4:]
    rows, width = query.shape
    digit = edge.shape[1]
    query[...] = total[0:rows, 0:width]
    key[...] = total[0:rows, width : 2 * width]
    edge[...] = total[rows : rows + 8, 0:digit]
    group = place[4]
    at = rows + 8
    for i, out in enumerate(outs[:6]):
        row = jnp.concatenate([total[at + i : at + i + 1, :], total[at + 8 + i : at + 9 + i, :]], 1)
        out[...] = row.reshape(out.shape)
    at = rows + 24
    heads = total[at : at + 1]
    hidden = total[at + 4 : at + 5]
    kinds = total[rows : rows + 8, digit : digit + 32]
    for other in range(1, 4):
        heads = jnp.where(group == other, total[at + other : at + other + 1], heads)
        hidden = jnp.where(group == other, total[at + 4 + other : at + 5 + other], hidden)
        start = digit + other * 32
        kinds = jnp.where(group == other, total[rows : rows + 8, start : start + 32], kinds)
    outs[6][...] = heads[:, :width].reshape(outs[6].shape)
    outs[7][...] = heads[:, width : 2 * width].reshape(outs[7].shape)
    outs[8][...] = hidden[:, :width].reshape(outs[8].shape)
    spatial[...] = kinds[:, : spatial.shape[1]]


def small_call(kernel, name, outs, *args, waits=0, mebibytes=8):
    return pl.pallas_call(
        kernel,
        out_shape=outs,
        in_specs=[smem if args[i].ndim == 1 else vmem for i in range(len(args) - waits)]
        + [untouched] * waits,
        out_specs=[vmem] * len(outs),
        cost_estimate=cost(1),
        compiler_params=params(mebibytes),
        name=name,
    )(*args)


class Links:
    def __init__(self):
        self.core = self.hop(lambda z, x, y, c: (z, x, y, 1 - c))
        self.first = self.hop(lambda z, x, y, c: (z, x, 1 - y, c) if c else (z, 1 - x, y, c))
        self.second = self.hop(lambda z, x, y, c: (z, 1 - x, y, c) if c else (z, x, 1 - y, c))
        self.along_x = self.hop(lambda z, x, y, c: (z, 1 - x, y, c))
        self.along_y = self.hop(lambda z, x, y, c: (z, x, 1 - y, c))
        self.along_z = [self.hop(lambda z, x, y, c, k=k: (z ^ k, x, y, c)) for k in (1, 2, 3)]

    def hop(self, move):
        index = lambda z, x, y, c: (z * 2 + x) * 4 + y * 2 + c
        spots = [(z, x, y, c) for z in range(4) for x in range(2) for y in range(2) for c in range(2)]
        return [(index(*spot), index(*move(*spot))) for spot in spots]


def send(values, hop):
    return lax.ppermute(values, ("dp", "mp"), hop)


def around(links, own):
    return [own] + [send(own, hop) for hop in links.along_z]


def join_kernel(rows, count, *refs):
    out = refs[-1]
    for i in range(count):
        stop = min((i + 1) * rows, out.shape[0])
        out[i * rows : stop, :] = refs[i][0 : stop - i * rows, :]


def join(parts, rows, after=()):
    total = rows * (len(parts) - 1) + parts[-1].shape[0] if len(parts) == 5 else rows * len(parts)
    return small_call(
        functools.partial(join_kernel, rows, len(parts)), "join",
        (shape((total, parts[0].shape[1]), bf16),), *parts, *after, waits=len(after),
    )[0]


def join_pairs_kernel(rows, own, near, *refs):
    out = refs[-1]
    out[4 * rows :, :] = jnp.zeros((out.shape[0] - 4 * rows, out.shape[1]), bf16)
    for i, (part, at) in enumerate(((own, 0), (near, 0), (own, rows), (near, rows))):
        out[i * rows : (i + 1) * rows, :] = part[at : at + rows, :]


def join_pairs(own, near, rows, after):
    return small_call(
        functools.partial(join_pairs_kernel, rows), "join_pairs",
        (shape((4 * rows + 64, own.shape[1]), bf16),), own, near, *after, waits=len(after),
    )[0]


def add_kernel(count, *refs):
    for step in range(4):
        total = refs[0][step].astype(f32)
        for ref in refs[1:count]:
            total = total + ref[step].astype(f32)
        refs[-1][step] = total.astype(bf16)


def add_rounded(terms, after):
    return small_call(
        functools.partial(add_kernel, len(terms)), "add",
        (shape(terms[0].shape, bf16),), *terms, *after, waits=len(after),
    )[0]


def step_sum(refs, step):
    total = refs[0][step].astype(f32)
    for ref in refs[1:]:
        total = total + ref[step + (4 if ref.shape[0] > 4 else 0)].astype(f32)
    return total.astype(bf16)


def add_pair_kernel(count, *refs):
    stay, go = refs[-2:]
    for i in range(2):
        stay[i] = step_sum(refs[:count], 2 * i)
        go[i] = step_sum(refs[:count], 2 * i + 1)


def add_pair(terms, after):
    out = shape((2,) + terms[0].shape[1:], bf16)
    return small_call(
        functools.partial(add_pair_kernel, len(terms)), "add_pair",
        (out,) * 2, *terms, *after, waits=len(after),
    )


def add_half_kernel(count, stay, got, *refs):
    for i, out in enumerate(refs[-2:]):
        out[...] = (stay[i].astype(f32) + got[i].astype(f32)).astype(bf16)


def add_half(stay, got, after):
    out = shape(stay.shape[1:], bf16)
    return small_call(
        functools.partial(add_half_kernel, 2), "add_half", (out,) * 2, stay, got, *after, waits=len(after)
    )


def settle_kernel(count, *refs):
    total = refs[0][...].astype(f32) + refs[1][...].astype(f32)
    outs = refs[len(refs) - count :]
    width = outs[0].shape[1]
    for i, out in enumerate(outs):
        out[...] = total[:, i * width : (i + 1) * width]


def settle(terms, width, after):
    rows, lanes = terms[0].shape
    count = lanes // width
    return small_call(
        functools.partial(settle_kernel, count), "settle",
        (shape((rows, width), f32),) * count, *terms, *after, waits=len(after), mebibytes=20,
    )


def held_until(values, *others):
    return lax.optimization_barrier((values, others))[0]


def local(
    layer_in,
    node_counts,
    spatial_ids,
    path_ids,
    ln1_gain,
    ln1_bias,
    w_q,
    w_k,
    w_v,
    q_bias,
    v_bias,
    spatial_table,
    edge_table,
    w_o,
    o_bias,
    ln2_gain,
    ln2_bias,
    w_in,
    in_bias,
    w_out,
    out_bias,
    cotangent,
):
    dp_size, mp_size = lax.axis_size("dp"), lax.axis_size("mp")
    dp_index, mp_index = lax.axis_index("dp"), lax.axis_index("mp")
    staged = dp_size == 8 and mp_size == 4
    height, width = w_q.shape
    features = layer_in.shape[1]
    edges = edge_table.shape[0] * dp_size
    heads = spatial_table.shape[1]
    kinds = spatial_table.shape[0]
    hops = path_ids.shape[1]
    share = edges // 4
    digit = edges // 8
    place = jnp.stack([dp_index // 2, dp_index % 2, mp_index // 2, mp_index % 2, mp_index]).astype(i32)
    if staged:
        links = Links()
        table_t = edge_table.T
        second = pack_second(w_in, w_out)
        first, own_biases = pack_first(
            place, w_q, w_k, w_v, w_o, q_bias, v_bias, in_bias, table_t, send(table_t, links.along_x), second
        )
        chunks = around(links, first)
        ids, buckets, h1, rows_early = prepare(
            place, spatial_ids, path_ids, layer_in, ln1_gain, ln1_bias, cotangent, kinds - 1, own_biases
        )
        pair_b = join([second, send(second, links.first)], height, (h1,))
        lookup_place = place
    else:
        gathered = [
            lax.all_gather(lax.all_gather(w, "dp", axis=0, tiled=True), "mp", axis=0)
            for w in (w_q, w_k, w_v, w_o, w_in, w_out)
        ]
        bias_row = jnp.concatenate([q_bias, v_bias, in_bias, jnp.zeros((width,), f32)])
        bias_row = lax.all_gather(bias_row[None], "mp", axis=0)
        parts_a = (jnp.concatenate(gathered[:4], 2), bias_row)
        parts_b = (jnp.concatenate(gathered[4:], 2),)
        table_t = lax.all_gather(edge_table, "dp", axis=0, tiled=True).T
        half = share // 2
        chunks = []
        for i in range(4):
            low, high = (table_t[:, i * share + n * half : i * share + (n + 1) * half] for n in range(2))
            chunks.append(
                jnp.concatenate([low[: heads // 2], low[heads // 2 :], high[: heads // 2], high[heads // 2 :]], 1)
            )
        lookup_place = jnp.zeros((5,), i32)
        ids, buckets, h1, rows_early = prepare(
            place, spatial_ids, path_ids, layer_in, ln1_gain, ln1_bias, cotangent, kinds - 1, spatial_ids
        )
    edge_sums = None
    look = lambda step, after: lookup(lookup_place, chunks[step], ids, edge_sums, step, heads, after)
    if staged:
        edge_sums = look(0, (pair_b,))
        stack_a = join(chunks + [own_biases], height, (edge_sums,))
        across_a, over_a = send(stack_a, links.first), send(stack_a, links.second)
        pair_b = held_until(pair_b, stack_a)
        far_b = send(pair_b, links.along_z[1])
        other_rows_early = send(held_until(rows_early, edge_sums), links.core)
        edge_sums = look(1, (stack_a,))
        four_b = join([pair_b, far_b], 2 * height, (edge_sums,))
        near_b = send(four_b, links.along_z[0])
        edge_sums = look(2, (four_b,))
        eight_b = join_pairs(four_b, near_b, 2 * height, (edge_sums,))
        both_a = send(held_until(across_a, eight_b), links.second)
        over_b = send(eight_b, links.second)
        edge_sums = look(3, (eight_b, other_rows_early))
        mine = (stack_a, across_a, over_a)
        theirs = tuple(send(held_until(part, eight_b), links.core) for part in mine)
        parts_a = mine + (both_a,) + theirs + (send(held_until(both_a, edge_sums), links.core),)
    else:
        for step in range(4):
            edge_sums = look(step, ())

    weights, biases, transposed, value_win, probs, att_low, mid, h2 = attend(
        place, node_counts, h1, edge_sums, buckets, spatial_table,
        layer_in, o_bias, ln2_gain, ln2_bias, parts_a,
    )
    if staged:
        parts_b = (
            eight_b, over_b, send(held_until(eight_b, edge_sums), links.core),
            send(held_until(over_b, mid), links.core),
        )
        feed_after = ()
    else:
        feed_after = ()
    layer_out, grad_mid, grad_att_t, grad_values, mine_b, theirs_b, rows_late, sums = feed(
        place, mid, h2, weights, biases, out_bias, ln2_gain, cotangent, att_low, probs, parts_b, feed_after
    )
    after = sums
    if staged:
        rows_b = (rows_early, rows_late)
        other_rows_b = (other_rows_early, send(rows_late, links.core))
        own_b, across_b, second_b = weight_grads(
            plan_second, place, mine_b, send(theirs_b, links.core), rows_b, other_rows_b, height, 4 * width, 4
        )
        got_second_b = send(second_b, links.second)
        after = own_b
    score_grads, mine_a, theirs_a, grad_layer_in, sums = attend_back(
        place, probs, value_win, transposed, grad_att_t, grad_values, weights,
        layer_in, ln1_gain, grad_mid, sums, after,
    )
    table = functools.partial(table_grads, place, score_grads, ids, buckets, digit, edges)
    slots = ids.shape[1]
    if staged:
        other_columns_a = send(theirs_a, links.core)
        partial = table(0, 16)
        own_a, across_a, second_a = weight_grads(
            plan_first, place, mine_a, other_columns_a,
            (rows_early[0:1],), (other_rows_b[0][0:1],), height, 2 * width, 2, (partial[0],), 9,
        )
        got_second_a = send(second_a, links.second)
        partial = table(16, 64, partial, after=(own_a,))
        across_b = add_rounded((across_b, got_second_b), (partial[0],))
        got_across_b = send(across_b, links.first)
        partial = table(64, 112, partial, after=(across_b,))
        mine, theirs, small = table(112, slots, partial, sums)
        got_core = send(theirs, links.core)
        half = features // 2
        sent, keep = small_call(
            meet_core_kernel, "meet_core", (shape((64, half), f32), shape((32, half), f32)),
            mine, small, got_core, small, waits=1,
        )
        stay_b, go_b = add_pair((own_b, got_across_b, got_second_b), (sent,))
        got_pair_b = send(go_b, links.along_z[0])
        across_a = add_rounded((across_a, got_second_a), (stay_b,))
        got_across_a = send(across_a, links.first)
        sent, keep = small_call(
            meet_near_kernel, "meet_near", (shape((48, half), f32), shape((16, half), f32)),
            keep, sent, send(sent, links.second), across_a, waits=1,
        )
        got_last = send(sent, links.first)
        own_b, go_b = add_half(stay_b, got_pair_b, (sent,))
        got_b = send(go_b, links.along_z[1])
        own_a = small_call(
            meet_far_kernel, "meet_far", (shape((height + 32, half), bf16),) * 4,
            keep, sent, got_last, own_a, got_across_a, got_second_a,
        )
        got_a = [send(own_a[step + 1], hop) for step, hop in enumerate(links.along_z)]
        grad_w_in, grad_w_out, grad_w_o, grad_w_v = settle([own_b, got_b], width, (own_a[0],))
        grad_w_q, grad_w_k, grad_edge, grad_spatial, *rows = small_call(
            finish_kernel, "finish",
            (shape((height, width), f32),) * 2
            + (shape((8, digit), f32), shape((8, kinds), f32))
            + (shape((features,), f32),) * 6
            + (shape((width,), f32),) * 3,
            place, own_a[0], *got_a, grad_w_in, waits=1, mebibytes=30,
        )
        grad_edge = grad_edge.T
        grad_spatial = grad_spatial.T
    else:
        contract = lambda a, b: lax.dot_general(
            a, b, (((1,), (1,)), ((), ())), preferred_element_type=f32
        )

        def unmix(mine, theirs):
            even = mp_index % 2 == 0
            cores = jnp.where(even, jnp.stack([mine, theirs], 1), jnp.stack([theirs, mine], 1))
            return cores.reshape(4, *mine.shape[1:])

        def scatter(rows_t, columns):
            grads = contract(rows_t, columns)
            grads = jnp.transpose(grads, (1, 0, 2))
            grads = lax.psum_scatter(grads, "mp", scatter_dimension=0, tiled=False)
            return lax.psum_scatter(grads, "dp", scatter_dimension=0, tiled=True)

        columns_a, columns_b = unmix(mine_a, theirs_a), unmix(mine_b, theirs_b)
        grad_w_q, grad_w_k = (
            scatter(rows_early[0], columns_a[:, :, i * width : (i + 1) * width]) for i in range(2)
        )
        grad_w_v = scatter(rows_early[0], columns_b[:, :, 1024 - width :])
        grad_w_in = scatter(rows_late[0], columns_b[:, :, :width])
        grad_w_out = scatter(rows_early[1], columns_b[:, :, 512 - width : 512])
        grad_w_o = scatter(rows_late[1], columns_b[:, :, 512 : 512 + width])
        table, spatial = table(0, slots)
        table = table.reshape(-1, heads, digit).transpose(0, 2, 1).reshape(edges, heads) / hops
        table = lax.psum_scatter(table, "dp", scatter_dimension=0, tiled=True)
        table = lax.psum(table, "mp")
        grad_edge = lax.dynamic_slice_in_dim(table, mp_index * 8, 8, 1)
        totals, spatial = lax.psum((sums, spatial), ("dp", "mp"))
        grad_spatial = lax.dynamic_slice_in_dim(spatial[:, :kinds], mp_index * 8, 8, 0).T
        head_sums = lax.dynamic_slice_in_dim(totals, 8 + mp_index, 1, 0)[0]
        hidden_sums = lax.dynamic_slice_in_dim(totals, 12 + mp_index, 1, 0)[0]
        rows = [totals[i] for i in range(6)]
        rows += [head_sums[:width], head_sums[512 : 512 + width], hidden_sums[:width]]
    return (
        layer_out,
        grad_layer_in,
        rows[0],
        rows[1],
        grad_w_q,
        grad_w_k,
        grad_w_v,
        rows[6],
        rows[7],
        grad_spatial,
        grad_edge,
        grad_w_o,
        rows[2],
        rows[3],
        rows[4],
        grad_w_in,
        rows[8],
        grad_w_out,
        rows[5],
    )


def solution(mesh):
    return jax.shard_map(
        local,
        mesh=mesh,
        in_specs=(
            P(("dp", "mp"), None),
            P("dp"),
            P("dp", None, None),
            P("dp", None, None, None),
            P(),
            P(),
            P("dp", "mp"),
            P("dp", "mp"),
            P("dp", "mp"),
            P("mp"),
            P("mp"),
            P(),
            P("dp", None),
            P("dp", "mp"),
            P(),
            P(),
            P(),
            P("dp", "mp"),
            P("mp"),
            P("dp", "mp"),
            P(),
            P(("dp", "mp"), None),
        ),
        out_specs=(
            P(("dp", "mp"), None),
            P(("dp", "mp"), None),
            P(),
            P(),
            P("dp", "mp"),
            P("dp", "mp"),
            P("dp", "mp"),
            P("mp"),
            P("mp"),
            P(None, "mp"),
            P("dp", "mp"),
            P("dp", "mp"),
            P(),
            P(),
            P(),
            P("dp", "mp"),
            P("mp"),
            P("dp", "mp"),
            P(),
        ),
        check_vma=False,
    )
```

```python
import functools

import jax
import jax.numpy as jnp
from jax import lax
from jax.experimental import pallas as pl
from jax.experimental.pallas import tpu as pltpu
from jax.sharding import PartitionSpec as P

epsilon = 1e-05
masked_score = -1e30
edge_unit = 1638.0
spatial_unit = 4096.0
hurry = 0.02
bf16 = jnp.bfloat16
f32 = jnp.float32
i32 = jnp.int32
vmem = pl.BlockSpec(memory_space=pltpu.VMEM)
smem = pl.BlockSpec(memory_space=pltpu.SMEM)
hbm = pl.BlockSpec(memory_space=pltpu.HBM)
untouched = pl.BlockSpec(memory_space=pl.ANY)


def params(mebibytes):
    return pltpu.CompilerParams(vmem_limit_bytes=mebibytes << 20)


def normalize(values):
    centred = values - jnp.mean(values, axis=-1, keepdims=True)
    scale = lax.rsqrt(jnp.mean(centred * centred, axis=-1, keepdims=True) + epsilon)
    return (centred * scale, scale)


def normalize_back(grad_normed, normed, scale):
    inner = grad_normed - jnp.mean(grad_normed, axis=-1, keepdims=True)
    inner = inner - normed * jnp.mean(grad_normed * normed, axis=-1, keepdims=True)
    return inner * scale


def dot_nn(left, right):
    return lax.dot_general(
        left, right, (((1,), (0,)), ((), ())), preferred_element_type=f32
    )


def dot_nt(left, right):
    return lax.dot_general(
        left, right, (((1,), (1,)), ((), ())), preferred_element_type=f32
    )


def column_sum(values):
    return jnp.sum(values, axis=0, keepdims=True)


def cost(microseconds):
    return pl.CostEstimate(flops=int(microseconds * hurry * 1.15e9), bytes_accessed=1024, transcendentals=0)


def as_row(ref):
    return ref[...].reshape(1, -1)


def shape(dims, kind):
    return jax.ShapeDtypeStruct(dims, kind)


def relative(place, side, which, step):
    z, x, y = place[0], place[1], place[2]
    flip_x = (0, 1 - side, side, 1)[which]
    flip_y = (0, side, 1 - side, 1)[which]
    row = (z ^ step) * 2 + (x ^ flip_x)
    column = (y ^ flip_y) * 2 + side
    return row, column


def three_terms(values):
    terms = []
    for _ in range(3):
        term = values.astype(bf16)
        terms.append(term)
        values = values - term.astype(f32)
    return terms


def pack_first_kernel(
    place, wq, wk, wv, wo, bq, bv, bi, edge, neighbour, after, weights, biases, held, sems, table, table_sems
):
    copies = [
        pltpu.make_async_copy(source, held.at[i], sems.at[i]) for i, source in enumerate((wq, wk, wv, wo))
    ]
    table_copies = [
        pltpu.make_async_copy(source, table.at[i], table_sems.at[i]) for i, source in enumerate((edge, neighbour))
    ]
    for copy in copies + table_copies:
        copy.start()
    row = jnp.concatenate([as_row(bq), as_row(bv), as_row(bi)], 1)
    lanes = weights.shape[1]
    row = jnp.concatenate([row, jnp.zeros((1, lanes - row.shape[1]), f32)], 1)
    terms = [term.astype(f32) for term in three_terms(row)]
    biases[...] = jnp.concatenate(terms + [jnp.zeros((13, lanes), f32)], 0).astype(bf16)
    even = place[1] == 0
    for copy in table_copies:
        copy.wait()
    mine, other = table[0].astype(f32), table[1].astype(f32)
    low, high = jnp.where(even, mine, other), jnp.where(even, other, mine)
    rows = held.shape[1]
    half = low.shape[0] // 2
    weights[rows:, :] = jnp.concatenate([low[:half], low[half:], high[:half], high[half:]], 1).astype(bf16)
    for copy in copies:
        copy.wait()
    weights[0:rows, :] = jnp.concatenate([held[i] for i in range(4)], 1)


def pack_first(place, wq, wk, wv, wo, bq, bv, bi, edge, neighbour, after):
    rows, width = wq.shape
    return pl.pallas_call(
        pack_first_kernel,
        out_shape=(shape((rows + 16, 4 * width), bf16), shape((16, 4 * width), bf16)),
        in_specs=[smem] + [hbm] * 4 + [vmem] * 3 + [hbm] * 2 + [untouched],
        out_specs=[vmem] * 2,
        scratch_shapes=[
            pltpu.VMEM((4, rows, width), bf16),
            pltpu.SemaphoreType.DMA((4,)),
            pltpu.VMEM((2,) + edge.shape, bf16),
            pltpu.SemaphoreType.DMA((2,)),
        ],
        cost_estimate=cost(2),
        compiler_params=params(60),
        name="pack_first",
    )(place, wq, wk, wv, wo, bq, bv, bi, edge, neighbour, after)


def pack_second_kernel(wi, wu, out):
    out[...] = jnp.concatenate([wi[...], wu[...]], 1)


def pack_second(wi, wu):
    rows, width = wi.shape
    return pl.pallas_call(
        pack_second_kernel,
        out_shape=shape((rows, 2 * width), bf16),
        in_specs=[vmem] * 2,
        out_specs=vmem,
        cost_estimate=cost(1),
        compiler_params=params(60),
        name="pack_second",
    )(wi, wu)


def prepare_kernel(
    virtual, place, spatial, path, layer_in, gain, bias, cotangent, after, ids, buckets, h1, rows_t
):
    slots = spatial.shape[1]
    for hop in range(path.shape[1]):
        ids[hop] = path[0, hop].T
    rows = lax.broadcasted_iota(i32, (slots, slots), 0)
    columns = lax.broadcasted_iota(i32, (slots, slots), 1)
    buckets[...] = jnp.where((rows == 0) | (columns == 0), virtual, spatial[0].T)
    normed, scale = normalize(layer_in[...])
    out = normed * as_row(gain) + as_row(bias)
    h1[...] = out.astype(bf16)
    rows_t[0] = out.T.astype(bf16)
    rows_t[1] = cotangent[...].T.astype(bf16)


def prepare(place, spatial, path, layer_in, gain, bias, cotangent, virtual, after):
    hops, slots = path.shape[1], path.shape[2]
    rows, width = layer_in.shape
    whole = lambda dims: pl.BlockSpec(dims, lambda i, s: (0,) * len(dims))
    return pl.pallas_call(
        functools.partial(prepare_kernel, virtual),
        grid_spec=pltpu.PrefetchScalarGridSpec(
            num_scalar_prefetch=1,
            grid=(1,),
            in_specs=[
                pl.BlockSpec((1, slots, slots), lambda i, s: (s[4], 0, 0)),
                pl.BlockSpec((1, hops, slots, slots), lambda i, s: (s[4], 0, 0, 0)),
                whole((rows, width)),
                whole((width,)),
                whole((width,)),
                whole((rows, width)),
                untouched,
            ],
            out_specs=[
                whole((hops, slots, slots)),
                whole((slots, slots)),
                whole((rows, width)),
                whole((2, width, rows)),
            ],
        ),
        out_shape=(
            shape((hops, slots, slots), i32),
            shape((slots, slots), i32),
            shape((rows, width), bf16),
            shape((2, width, rows), bf16),
        ),
        compiler_params=params(62),
        cost_estimate=cost(1),
        name="prepare",
    )(place, spatial, path, layer_in, gain, bias, cotangent, after)


def quantize(table, unit):
    held = jnp.round(table.astype(f32) * unit).astype(i32)
    partner = jnp.concatenate([held[4:], held[:4]], 0)
    return held + partner * 65536


def lanes_gather(table, places):
    return jnp.take_along_axis(table, places, axis=1, mode="promise_in_bounds")


def lookup_kernel(first, step, share, place, chunk, ids, *refs):
    total, table = refs[-2:]
    previous = None if first else refs[0]
    hops, slots = ids.shape[0], ids.shape[1]
    pairs = total.shape[0]
    below = chunk[chunk.shape[0] - 16 :, :]
    half = share // 2
    below = [below[:, i * half : (i + 1) * half] for i in range(4)]
    packed = quantize(
        jnp.concatenate(
            [jnp.concatenate([below[0], below[2]], 1), jnp.concatenate([below[1], below[3]], 1)], 0
        ),
        edge_unit,
    )
    blocks = share // 128
    for pair in range(pairs):
        head = (pair // 4) * 8 + pair % 4
        for block in range(blocks):
            table[pair, block] = jnp.broadcast_to(
                packed[head : head + 1, block * 128 : (block + 1) * 128], (8, 128)
            )
    base = (place[0] ^ step) * share

    def body(i, carry):
        offset = pl.multiple_of(i * 8, 8)
        sums = [None] * pairs
        if not first:
            sums = [previous[pair, pl.ds(offset, 8), :] for pair in range(pairs)]
        for hop in range(hops):
            relative_id = ids[hop, pl.ds(offset, 8), :] - base
            low = relative_id & 127
            high = relative_id >> 7
            masks = [high == block for block in range(blocks)]
            for pair in range(pairs):
                value = jnp.zeros((8, 128), i32)
                for block in range(blocks):
                    value = jnp.where(masks[block], lanes_gather(table[pair, block], low), value)
                sums[pair] = value if sums[pair] is None else sums[pair] + value
        for pair in range(pairs):
            total[pair, pl.ds(offset, 8), :] = sums[pair]
        return carry

    lax.fori_loop(0, slots // 8, body, 0)


def lookup(place, chunk, ids, previous, step, heads, after=()):
    share = chunk.shape[1] // 2
    pairs = heads // 2
    slots = ids.shape[1]
    first = previous is None
    out = shape((pairs, slots, slots), i32)
    return pl.pallas_call(
        functools.partial(lookup_kernel, first, step, share),
        out_shape=out,
        in_specs=[smem] + [vmem] * (2 if first else 3) + [untouched] * len(after),
        out_specs=vmem,
        scratch_shapes=[pltpu.VMEM((pairs, share // 128, 8, 128), i32)],
        input_output_aliases={} if first else {3: 0},
        compiler_params=params(8),
        cost_estimate=cost(6),
        name="lookup",
    )(place, chunk, ids, *(() if first else (previous,)), *after)


def assemble(place, parts, whole, biases=None):
    if len(parts) <= 2:
        whole[...] = parts[0][...]
        return
    core = place[3]
    rows = whole.shape[1] // 8
    each = len(parts) // 2
    for other in range(2):
        for which in range(4):
            for step in range(4):
                row, column = relative(place, core ^ other, which, step)
                start = pl.multiple_of(row * rows, rows)
                part = parts[other * each + which // (4 // each)]
                at = (step * (4 // each) + which % (4 // each)) * rows
                whole[column, pl.ds(start, rows), :] = part[at : at + rows, :]
            if biases is not None:
                terms = parts[other * each + which][4 * rows : 4 * rows + 16, :].astype(f32)
                biases[column] = terms[0:1] + terms[1:2] + terms[2:3]


def head_masks(width, offset, depth):
    lanes = lax.broadcasted_iota(i32, (1, width), 1)
    out = []
    for head in range(8):
        start = offset + head * depth
        out.append(((lanes >= start) & (lanes < start + depth)).astype(f32).astype(bf16))
    return out


def attend_kernel(
    n_parts, place, counts, h1, edge_sums, buckets, spatial_table, layer_in, o_bias, gain, bias, *refs
):
    parts, refs = refs[:n_parts], refs[n_parts:]
    weights, biases, transposed, value_win, probs_out, att_low, mid, h2 = refs
    assemble(place, parts, weights, biases)
    if n_parts == 2:
        biases[...] = parts[1][...]
    slots = h1.shape[0]
    groups, width = biases.shape[0], biases.shape[2] // 4
    depth = width // 8
    pad = 256 - width
    hops = 5
    count = counts[place[4]]
    packed = quantize(spatial_table[...].astype(f32).T, spatial_unit)
    packed = jnp.concatenate([packed, jnp.zeros((packed.shape[0], 128 - packed.shape[1]), i32)], 1)
    hidden_key = lax.broadcasted_iota(i32, (slots, slots), 0) > count
    bucket = buckets[...]
    key_masks = head_masks(256, pad, depth)
    mid[...] = layer_in[...] + as_row(o_bias)
    for group in range(groups):
        natural = dot_nn(h1[...], weights[group, :, : 3 * width + pad])
        row_bias = jnp.concatenate(
            [
                biases[group, 0:1, :width],
                jnp.zeros((1, width), f32),
                biases[group, 0:1, width : 2 * width],
                jnp.zeros((1, pad), f32),
            ],
            1,
        )
        natural = natural + row_bias
        natural_t = natural.T
        transposed[group] = natural_t[: 2 * width].astype(bf16)
        natural = natural.astype(bf16)
        value_win[group] = natural[:, 2 * width : 2 * width + 256]
        keys = natural[:, width - pad : 2 * width]
        stack = jnp.concatenate([keys * mask for mask in key_masks], 0)
        query = jnp.concatenate([jnp.zeros((pad, slots), f32), natural_t[:width]], 0).astype(bf16)
        scores = dot_nn(stack, query) * depth ** (-0.5)
        out = [None] * 8
        for pair in range(4):
            word = edge_sums[group * 4 + pair]
            head = group * 8 + pair
            spatial_word = lanes_gather(
                jnp.broadcast_to(packed[head : head + 1], (slots, 128)), bucket
            )
            low = (word << 16) >> 16
            spatial_low = (spatial_word << 16) >> 16
            high = (word - low) >> 16
            spatial_high = (spatial_word - spatial_low) >> 16
            for part, spatial_part, spot in ((low, spatial_low, pair), (high, spatial_high, pair + 4)):
                pair_bias = part.astype(f32) * (1.0 / (edge_unit * hops))
                pair_bias = pair_bias + spatial_part.astype(f32) * (1.0 / spatial_unit)
                score = scores[spot * slots : (spot + 1) * slots] + pair_bias
                score = jnp.where(hidden_key, masked_score, score)
                weight = jnp.exp(score - jnp.max(score, axis=0, keepdims=True))
                probs = weight * (1.0 / column_sum(weight))
                probs_out[group * 8 + spot] = probs
                values = natural_t[2 * width + spot * depth : 2 * width + (spot + 1) * depth]
                out[spot] = dot_nn(values.astype(bf16), probs.astype(bf16))
        gap = jnp.zeros((pad, slots), f32)
        att_low[group] = jnp.concatenate(out + [gap], 0).T.astype(bf16)
        high_form = jnp.concatenate([gap] + out, 0).T.astype(bf16)
        mid[...] += dot_nt(high_form, weights[group, :, 3 * width - pad : 4 * width])
    normed, scale = normalize(mid[...])
    h2[...] = (normed * as_row(gain) + as_row(bias)).astype(bf16)


def attend(place, counts, h1, edge_sums, buckets, spatial_table, layer_in, o_bias, gain, bias, parts):
    slots, features = h1.shape
    width = parts[0].shape[-1] // 4
    heads = spatial_table.shape[1]
    groups = heads // 8
    return pl.pallas_call(
        functools.partial(attend_kernel, len(parts)),
        out_shape=(
            shape((groups, features, 4 * width), bf16),
            shape((groups, 1, 4 * width), f32),
            shape((groups, 2 * width, slots), bf16),
            shape((groups, slots, 256), bf16),
            shape((heads, slots, slots), f32),
            shape((groups, slots, 256), bf16),
            shape((slots, features), f32),
            shape((slots, features), bf16),
        ),
        in_specs=[smem, smem] + [vmem] * (8 + len(parts)),
        out_specs=[vmem] * 8,
        cost_estimate=cost(7),
        compiler_params=params(28),
        name="attend",
    )(
        place, counts, h1, edge_sums, buckets, spatial_table, layer_in, o_bias, gain, bias,
        *parts,
    )


def group_order(place):
    return [
        (theirs, y, y * 2 + (place[3] ^ theirs)) for theirs in (1, 0) for y in (0, 1)
    ]


def feed_kernel(
    n_parts, place, mid, h2, weights_a, biases, out_bias, gain, cotangent, att_low, probs_in, *refs
):
    parts = refs[:n_parts]
    layer_out, grad_mid, grad_att_t, grad_values, mine, theirs, rows_t, sums, weights = refs[-9:]
    assemble(place, parts, weights)
    slots, features = mid.shape
    width = biases.shape[2] // 4
    depth = width // 8
    pad = 256 - width
    lanes = lax.broadcasted_iota(i32, (1, 256), 1)
    cot = cotangent[...]
    grad_ffn = cot.astype(bf16)
    h2_value = h2[...]
    layer_out[...] = mid[...] + as_row(out_bias)
    grad_h2 = jnp.zeros((slots, features), f32)
    sums[...] = jnp.zeros_like(sums)
    order = group_order(place)
    for side, y, group in order:
        columns = theirs if side else mine
        in_bias = jnp.concatenate(
            [biases[group, 0:1, 2 * width : 3 * width], jnp.zeros((1, pad), f32)], 1
        )
        pre = dot_nn(h2_value, weights[group, :, :256]) + in_bias
        cdf = 0.5 * (1.0 + lax.erf(pre * (0.5**0.5)))
        slope = cdf + pre * jnp.exp(-0.5 * pre * pre) * 0.3989422804014327
        hidden = pltpu.roll(pre * cdf, pad, 1)
        hidden = jnp.where(lanes >= pad, hidden, 0.0).astype(bf16)
        layer_out[...] += dot_nt(hidden, weights[group, :, width - pad : 2 * width])
        grad_hidden = dot_nn(grad_ffn, weights[group, :, width - pad : 2 * width])
        grad_hidden = pltpu.roll(grad_hidden, width, 1)
        grad_pre = jnp.where(lanes < width, grad_hidden * slope, 0.0).astype(bf16)
        grad_h2 = grad_h2 + dot_nt(grad_pre, weights[group, :, :256])
        columns[y, :, 0:256] = grad_pre
        columns[y, :, 256:512] = hidden
        columns[y, :, 512:768] = att_low[group]
        sums[pl.ds(12 + group, 1), 0:256] = column_sum(grad_pre.astype(f32))
    normed, scale = normalize(mid[...])
    grad = cot + normalize_back(grad_h2 * as_row(gain), normed, scale)
    grad_mid[...] = grad
    branch = grad.astype(bf16)
    sums[2:3, :] = column_sum(grad)
    sums[3:4, :] = column_sum(grad_h2 * normed)
    sums[4:5, :] = column_sum(grad_h2)
    sums[5:6, :] = column_sum(cot)
    rows_t[0] = h2_value.astype(f32).T.astype(bf16)
    rows_t[1] = grad.T.astype(bf16)
    gap = jnp.zeros((pad, slots), f32)
    for side, y, group in order:
        columns = theirs if side else mine
        grad_att = dot_nn(branch, weights_a[group]).T[pad:]
        grad_att_t[group] = jnp.concatenate([grad_att, gap], 0).astype(bf16)
        out = []
        for head in range(8):
            out.append(
                dot_nt(
                    grad_att[head * depth : (head + 1) * depth].astype(bf16),
                    probs_in[group * 8 + head].astype(bf16),
                )
            )
        low_form = jnp.concatenate(out + [gap], 0).T.astype(bf16)
        grad_values[group] = low_form
        columns[y, :, 768:1024] = jnp.concatenate([gap] + out, 0).T.astype(bf16)
        sums[pl.ds(8 + group, 1), 512:768] = column_sum(low_form.astype(f32))


def feed(place, mid, h2, weights_a, biases, out_bias, gain, cotangent, att_low, probs, parts, after=()):
    slots, features = mid.shape
    groups, width = biases.shape[0], biases.shape[2] // 4
    whole = lambda array: pl.BlockSpec(array.shape, lambda i: (0,) * len(array.shape))
    outs = (
        shape((slots, features), f32),
        shape((slots, features), f32),
        shape((groups, 256, slots), bf16),
        shape((groups, slots, 256), bf16),
        shape((2, slots, 1024), bf16),
        shape((2, slots, 1024), bf16),
        shape((2, features, slots), bf16),
        shape((16, features), f32),
    )
    rest = (biases, out_bias, gain, cotangent, att_low, probs)
    return pl.pallas_call(
        functools.partial(feed_kernel, len(parts)),
        grid=(1,),
        out_shape=outs,
        in_specs=[
            smem,
            whole(mid),
            whole(h2),
            pl.BlockSpec((groups, features, 256), lambda i: (0, 0, 2)),
        ]
        + [whole(a) for a in rest + tuple(parts)]
        + [untouched] * len(after),
        out_specs=[whole(out) for out in outs],
        scratch_shapes=[pltpu.VMEM((groups, features, 2 * width), bf16)],
        cost_estimate=cost(7),
        compiler_params=params(32),
        name="feed",
    )(place, mid, h2, weights_a, *rest, *parts, *after)


def attend_back_kernel(
    place, probs_in, value_win, transposed, grad_att_t, grad_values, weights, layer_in, gain, grad_mid,
    sums_in, after, score_grads, mine, theirs, grad_in, sums,
):
    slots, features = layer_in.shape
    width = transposed.shape[1] // 2
    depth = width // 8
    value_masks = head_masks(256, 0, depth)
    grad_h1 = jnp.zeros((slots, features), f32)
    sums[...] = sums_in[...]
    scale = depth ** (-0.5)
    for side, y, group in group_order(place):
        columns = theirs if side else mine
        values = value_win[group]
        stack = jnp.concatenate([values * mask for mask in value_masks], 0)
        grad_probs = dot_nn(stack, grad_att_t[group])
        held = transposed[group].astype(f32)
        query_out, key_out, score_out = [], [], []
        for head in range(8):
            probs = probs_in[group * 8 + head]
            part = probs * grad_probs[head * slots : (head + 1) * slots]
            exact = part - probs * column_sum(part)
            grads = exact.astype(bf16)
            score_out.append(exact)
            key_rows = held[width + head * depth : width + (head + 1) * depth]
            query_out.append(dot_nn(key_rows.astype(bf16), grads) * scale)
            query_rows = held[head * depth : (head + 1) * depth]
            key_out.append(dot_nt(query_rows.astype(bf16), grads) * scale)
        score_grads[group] = jnp.swapaxes(jnp.stack(score_out), 0, 1)
        natural = jnp.concatenate(query_out + key_out, 0).T.astype(bf16)
        columns[y] = natural
        grad_h1 = grad_h1 + dot_nt(natural, weights[group, :, : 2 * width])
        grad_h1 = grad_h1 + dot_nt(grad_values[group], weights[group, :, 2 * width : 2 * width + 256])
        sums[pl.ds(8 + group, 1), 0 : 2 * width] = column_sum(natural.astype(f32))
    normed, inverse = normalize(layer_in[...])
    grad_in[...] = grad_mid[...] + normalize_back(grad_h1 * as_row(gain), normed, inverse)
    sums[0:1, :] = column_sum(grad_h1 * normed)
    sums[1:2, :] = column_sum(grad_h1)


def attend_back(
    place, probs, value_win, transposed, grad_att_t, grad_values, weights, layer_in, gain, grad_mid, sums, after
):
    slots, features = layer_in.shape
    groups = transposed.shape[0]
    width = transposed.shape[1] // 2
    return pl.pallas_call(
        attend_back_kernel,
        out_shape=(
            shape((groups, slots, 8, slots), f32),
            shape((2, slots, 2 * width), bf16),
            shape((2, slots, 2 * width), bf16),
            shape((slots, features), f32),
            shape(sums.shape, f32),
        ),
        in_specs=[smem] + [vmem] * 10 + [untouched],
        out_specs=[vmem] * 5,
        cost_estimate=cost(7),
        compiler_params=params(24),
        name="attend_back",
    )(
        place, probs, value_win, transposed, grad_att_t, grad_values, weights, layer_in, gain, grad_mid,
        sums, after,
    )


def weight_grads_kernel(plan, n_rows, hops, place, columns_own, columns_other, *refs):
    own_rows, other_rows = refs[:n_rows], refs[n_rows : 2 * n_rows]
    rows_t = refs[-1]
    if hops == 2:
        second = refs[-2]
    elif hops == 1:
        own, across = refs[-3:-1]
    else:
        own, across, second = refs[-4:-1]
    targets = []
    if hops != 1:
        targets += [(3, second, 0), (2, second, 4)]
    if hops != 2:
        targets += [(1, across, 0), (0, own, 0)]
    kind = 0
    for mine, other in zip(own_rows, other_rows):
        slots = mine.shape[2]
        for i in range(mine.shape[0]):
            rows_t[kind, :, 0:slots] = mine[i]
            rows_t[kind, :, slots : 2 * slots] = other[i]
            kind += 1
    core = place[3]
    height = targets[0][1].shape[1]
    for which, out, at in targets:
        y = relative(place, core, which, 0)[1] >> 1
        right = jnp.concatenate([columns_own[y], columns_other[y]], 0)
        for step in range(4):
            row = relative(place, core, which, step)[0]
            start = pl.multiple_of(row * height, height)
            out[at + step] = plan(lambda kind: rows_t[kind, pl.ds(start, height), :], right).astype(bf16)
    for extra in range(8, targets[0][1].shape[0]):
        second[extra] = jnp.zeros(second.shape[1:], bf16)


def plan_first(rows_of, right):
    return dot_nn(rows_of(0), right)


def plan_second(rows_of, right):
    grad_in = dot_nn(rows_of(2), right[:, 0:256])
    grad_out = dot_nn(rows_of(1), right[:, 256:512])
    grad_o = dot_nn(rows_of(3), right[:, 512:768])
    grad_v = dot_nn(rows_of(0), right[:, 768:1024])
    return jnp.concatenate(
        [
            grad_in[:, :128],
            grad_in[:, 128:] + grad_out[:, :128],
            grad_out[:, 128:],
            grad_o[:, :128],
            grad_o[:, 128:] + grad_v[:, :128],
            grad_v[:, 128:],
        ],
        1,
    )


def weight_grads(
    plan, place, columns_own, columns_other, own_rows, other_rows, height, lanes, microseconds, after=(), blocks=8, hops=0
):
    features, slots = own_rows[0].shape[1:]
    kinds = sum(rows.shape[0] for rows in own_rows)
    out = shape((4, height, lanes), bf16)
    far = shape((blocks, height, lanes), bf16)
    outs = ((out, out, far), (out, out), (far,))[hops]
    return pl.pallas_call(
        functools.partial(weight_grads_kernel, plan, len(own_rows), hops),
        out_shape=outs,
        in_specs=[smem] + [vmem] * (2 + 2 * len(own_rows)) + [untouched] * len(after),
        out_specs=[vmem] * len(outs),
        scratch_shapes=[pltpu.VMEM((kinds, features, 2 * slots), bf16)],
        cost_estimate=cost(microseconds),
        compiler_params=params(20),
        name="weight_grads",
    )(place, columns_own, columns_other, *own_rows, *other_rows, *after)


def table_kernel(digit, start, stop, previous, last, place, grads, ids, buckets, *refs):
    hops = ids.shape[0]
    groups = grads.shape[0]
    heads = groups * 8
    span = 16
    if previous:
        total_in, spatial_in = refs[:2]
    if last:
        sums = refs[2]
        mine, theirs, small, total, spatial = refs[-5:]
    else:
        total, spatial = refs[-2:]
    total[...] = total_in[...] if previous else jnp.zeros_like(total)
    spatial[...] = spatial_in[...] if previous else jnp.zeros_like(spatial)
    high_count = total.shape[0] // heads
    digits = lax.broadcasted_iota(i32, (digit, 128), 0).astype(f32).astype(bf16)
    kinds = lax.broadcasted_iota(i32, (heads, 128), 0).astype(f32).astype(bf16)
    one = jnp.ones((), bf16)
    zero = jnp.zeros((), bf16)

    def body(i, carry):
        lefts, rights, plain, kind_rights = [], [], [], []
        for j in range(span):
            row = i * span + j
            piece = jnp.concatenate([grads[group, row] for group in range(groups)], 0).astype(bf16)
            bucket = buckets[pl.ds(row, 1), :].astype(f32).astype(bf16)
            plain.append(piece)
            kind_rights.append(jnp.where(jnp.broadcast_to(bucket, (heads, 128)) == kinds, one, zero))
            for hop in range(hops):
                value = ids[hop, pl.ds(row, 1), :].astype(f32)
                high = jnp.floor((value + 0.5) * (1.0 / digit))
                low = value - high * digit
                low = jnp.broadcast_to(low.astype(bf16), (digit, 128))
                high = jnp.broadcast_to(high.astype(bf16), (heads, 128))
                rights.append(jnp.where(low == digits, one, zero))
                lefts.append(
                    jnp.concatenate(
                        [jnp.where(high == jnp.full((), k, bf16), piece, zero) for k in range(high_count)], 0
                    )
                )
        total[...] += dot_nt(jnp.concatenate(lefts, 1), jnp.concatenate(rights, 1))
        spatial[...] += dot_nt(jnp.concatenate(plain, 1), jnp.concatenate(kind_rights, 1))
        return carry

    lax.fori_loop(start // span, stop // span, body, 0)
    if last:
        core = place[3]
        for other, out in ((0, mine), (1, theirs)):
            for which in range(4):
                pieces = []
                for step in range(4):
                    row, column = relative(place, core ^ other, which, step)
                    at = pl.multiple_of(row * heads + column * 8, 8)
                    pieces.append(total[pl.ds(at, 8), :] * (1.0 / hops))
                out[which * 16 : which * 16 + 8, :] = jnp.concatenate(pieces[:2], 1)
                out[which * 16 + 8 : which * 16 + 16, :] = jnp.concatenate(pieces[2:], 1)
        half = small.shape[1]
        held = sums[...]
        spread = [jnp.zeros((8, digit), f32)] + [spatial[group * 8 : (group + 1) * 8, :] for group in range(4)]
        spread.append(jnp.zeros((8, half - digit - 4 * heads), f32))
        packed = [jnp.concatenate(spread, 1), held[0:8, :half], held[0:8, half:]]
        packed.append(
            jnp.concatenate(
                [
                    jnp.concatenate([held[8:12, :digit], held[12:16, :digit]], 0),
                    jnp.concatenate([held[8:12, 512 : 512 + digit], jnp.zeros((4, digit), f32)], 0),
                ],
                1,
            )
        )
        packed = jnp.concatenate(packed, 0)
        small[...] = packed
        theirs[64:96, :] = packed


def table_grads(place, grads, ids, buckets, digit, edges, start, stop, previous=(), sums=None, after=()):
    heads = grads.shape[0] * 8
    last = sums is not None
    inner = (shape((edges // digit * heads, digit), f32), shape((heads, heads), f32))
    outs = inner
    if last:
        lanes = sums.shape[1] // 2
        outs = (shape((64, lanes), f32), shape((96, lanes), f32), shape((32, lanes), f32))
    inputs = tuple(previous) + ((sums,) if last else ())
    return pl.pallas_call(
        functools.partial(table_kernel, digit, start, stop, len(previous) > 0, last),
        out_shape=outs,
        in_specs=[smem] + [vmem] * (3 + len(inputs)) + [untouched] * len(after),
        out_specs=[vmem] * len(outs),
        scratch_shapes=[pltpu.VMEM(a.shape, f32) for a in inner] if last else [],
        cost_estimate=cost(15 * (stop - start) / grads.shape[1]),
        compiler_params=params(12),
        name="table_grads",
    )(place, grads, ids, buckets, *inputs, *after)


def meet_core_kernel(mine, small, got, after, out, keep):
    keep[...] = mine[0:32, :] + got[0:32, :]
    out[0:16, :] = mine[48:64, :] + got[48:64, :]
    out[16:32, :] = mine[32:48, :] + got[32:48, :]
    out[32:64, :] = small[...] + got[64:96, :]


def meet_near_kernel(keep, sent, got, after, out, kept):
    out[0:16, :] = keep[16:32, :] + got[0:16, :]
    out[16:48, :] = sent[32:64, :] + got[32:64, :]
    kept[...] = keep[0:16, :] + got[16:32, :]


def meet_far_kernel(kept, sent, got, own, first_hop, second_hop, *outs):
    table = kept[...] + got[0:16, :]
    small = sent[16:48, :] + got[16:48, :]
    digit = table.shape[1] // 2
    rows = own.shape[1]
    for step, out in enumerate(outs):
        total = own[step].astype(f32) + first_hop[step].astype(f32) + second_hop[step + 4].astype(f32)
        out[0:rows, :] = total.astype(bf16)
        block = table[(step // 2) * 8 : (step // 2) * 8 + 8, (step % 2) * digit : (step % 2 + 1) * digit]
        head = jnp.concatenate([block, small[0:8, digit:]], 1)
        out[rows:, :] = jnp.concatenate([head, small[8:32]], 0).astype(bf16)


def finish_kernel(place, own, first, second, third, after, *outs):
    total = own[...].astype(f32)
    for part in (first, second, third):
        total = total + part[...].astype(f32)
    query, key, edge, spatial = outs[:4]
    outs = outs[4:]
    rows, width = query.shape
    digit = edge.shape[1]
    query[...] = total[0:rows, 0:width]
    key[...] = total[0:rows, width : 2 * width]
    edge[...] = total[rows : rows + 8, 0:digit]
    group = place[4]
    at = rows + 8
    for i, out in enumerate(outs[:6]):
        row = jnp.concatenate([total[at + i : at + i + 1, :], total[at + 8 + i : at + 9 + i, :]], 1)
        out[...] = row.reshape(out.shape)
    at = rows + 24
    heads = total[at : at + 1]
    hidden = total[at + 4 : at + 5]
    kinds = total[rows : rows + 8, digit : digit + 32]
    for other in range(1, 4):
        heads = jnp.where(group == other, total[at + other : at + other + 1], heads)
        hidden = jnp.where(group == other, total[at + 4 + other : at + 5 + other], hidden)
        start = digit + other * 32
        kinds = jnp.where(group == other, total[rows : rows + 8, start : start + 32], kinds)
    outs[6][...] = heads[:, :width].reshape(outs[6].shape)
    outs[7][...] = heads[:, width : 2 * width].reshape(outs[7].shape)
    outs[8][...] = hidden[:, :width].reshape(outs[8].shape)
    spatial[...] = kinds[:, : spatial.shape[1]]


def small_call(kernel, name, outs, *args, waits=0, mebibytes=8):
    return pl.pallas_call(
        kernel,
        out_shape=outs,
        in_specs=[smem if args[i].ndim == 1 else vmem for i in range(len(args) - waits)]
        + [untouched] * waits,
        out_specs=[vmem] * len(outs),
        cost_estimate=cost(1),
        compiler_params=params(mebibytes),
        name=name,
    )(*args)


class Links:
    def __init__(self):
        self.core = self.hop(lambda z, x, y, c: (z, x, y, 1 - c))
        self.first = self.hop(lambda z, x, y, c: (z, x, 1 - y, c) if c else (z, 1 - x, y, c))
        self.second = self.hop(lambda z, x, y, c: (z, 1 - x, y, c) if c else (z, x, 1 - y, c))
        self.along_x = self.hop(lambda z, x, y, c: (z, 1 - x, y, c))
        self.along_y = self.hop(lambda z, x, y, c: (z, x, 1 - y, c))
        self.along_z = [self.hop(lambda z, x, y, c, k=k: (z ^ k, x, y, c)) for k in (1, 2, 3)]

    def hop(self, move):
        index = lambda z, x, y, c: (z * 2 + x) * 4 + y * 2 + c
        spots = [(z, x, y, c) for z in range(4) for x in range(2) for y in range(2) for c in range(2)]
        return [(index(*spot), index(*move(*spot))) for spot in spots]


def send(values, hop):
    return lax.ppermute(values, ("dp", "mp"), hop)


def around(links, own):
    return [own] + [send(own, hop) for hop in links.along_z]


def join_kernel(rows, count, *refs):
    out = refs[-1]
    for i in range(count):
        stop = min((i + 1) * rows, out.shape[0])
        out[i * rows : stop, :] = refs[i][0 : stop - i * rows, :]


def join(parts, rows, after=()):
    total = rows * (len(parts) - 1) + parts[-1].shape[0] if len(parts) == 5 else rows * len(parts)
    return small_call(
        functools.partial(join_kernel, rows, len(parts)), "join",
        (shape((total, parts[0].shape[1]), bf16),), *parts, *after, waits=len(after),
    )[0]


def join_pairs_kernel(rows, own, near, *refs):
    out = refs[-1]
    out[4 * rows :, :] = jnp.zeros((out.shape[0] - 4 * rows, out.shape[1]), bf16)
    for i, (part, at) in enumerate(((own, 0), (near, 0), (own, rows), (near, rows))):
        out[i * rows : (i + 1) * rows, :] = part[at : at + rows, :]


def join_pairs(own, near, rows, after):
    return small_call(
        functools.partial(join_pairs_kernel, rows), "join_pairs",
        (shape((4 * rows + 64, own.shape[1]), bf16),), own, near, *after, waits=len(after),
    )[0]


def add_kernel(count, *refs):
    for step in range(4):
        total = refs[0][step].astype(f32)
        for ref in refs[1:count]:
            total = total + ref[step].astype(f32)
        refs[-1][step] = total.astype(bf16)


def add_rounded(terms, after):
    return small_call(
        functools.partial(add_kernel, len(terms)), "add",
        (shape(terms[0].shape, bf16),), *terms, *after, waits=len(after),
    )[0]


def step_sum(refs, step):
    total = refs[0][step].astype(f32)
    for ref in refs[1:]:
        total = total + ref[step + (4 if ref.shape[0] > 4 else 0)].astype(f32)
    return total.astype(bf16)


def add_pair_kernel(count, *refs):
    stay, go = refs[-2:]
    for i in range(2):
        stay[i] = step_sum(refs[:count], 2 * i)
        go[i] = step_sum(refs[:count], 2 * i + 1)


def add_pair(terms, after):
    out = shape((2,) + terms[0].shape[1:], bf16)
    return small_call(
        functools.partial(add_pair_kernel, len(terms)), "add_pair",
        (out,) * 2, *terms, *after, waits=len(after),
    )


def add_half_kernel(count, stay, got, *refs):
    for i, out in enumerate(refs[-2:]):
        out[...] = (stay[i].astype(f32) + got[i].astype(f32)).astype(bf16)


def add_half(stay, got, after):
    out = shape(stay.shape[1:], bf16)
    return small_call(
        functools.partial(add_half_kernel, 2), "add_half", (out,) * 2, stay, got, *after, waits=len(after)
    )


def settle_kernel(count, *refs):
    total = refs[0][...].astype(f32) + refs[1][...].astype(f32)
    outs = refs[len(refs) - count :]
    width = outs[0].shape[1]
    for i, out in enumerate(outs):
        out[...] = total[:, i * width : (i + 1) * width]


def settle(terms, width, after):
    rows, lanes = terms[0].shape
    count = lanes // width
    return small_call(
        functools.partial(settle_kernel, count), "settle",
        (shape((rows, width), f32),) * count, *terms, *after, waits=len(after), mebibytes=20,
    )


def held_until(values, *others):
    return lax.optimization_barrier((values, others))[0]


def local(
    layer_in,
    node_counts,
    spatial_ids,
    path_ids,
    ln1_gain,
    ln1_bias,
    w_q,
    w_k,
    w_v,
    q_bias,
    v_bias,
    spatial_table,
    edge_table,
    w_o,
    o_bias,
    ln2_gain,
    ln2_bias,
    w_in,
    in_bias,
    w_out,
    out_bias,
    cotangent,
):
    dp_size, mp_size = lax.axis_size("dp"), lax.axis_size("mp")
    dp_index, mp_index = lax.axis_index("dp"), lax.axis_index("mp")
    staged = dp_size == 8 and mp_size == 4
    height, width = w_q.shape
    features = layer_in.shape[1]
    edges = edge_table.shape[0] * dp_size
    heads = spatial_table.shape[1]
    kinds = spatial_table.shape[0]
    hops = path_ids.shape[1]
    share = edges // 4
    digit = edges // 8
    place = jnp.stack([dp_index // 2, dp_index % 2, mp_index // 2, mp_index % 2, mp_index]).astype(i32)
    if staged:
        links = Links()
        table_t = edge_table.T
        second = pack_second(w_in, w_out)
        first, own_biases = pack_first(
            place, w_q, w_k, w_v, w_o, q_bias, v_bias, in_bias, table_t, send(table_t, links.along_x), second
        )
        chunks = around(links, first)
        ids, buckets, h1, rows_early = prepare(
            place, spatial_ids, path_ids, layer_in, ln1_gain, ln1_bias, cotangent, kinds - 1, own_biases
        )
        pair_b = join([second, send(second, links.first)], height, (h1,))
        lookup_place = place
    else:
        gathered = [
            lax.all_gather(lax.all_gather(w, "dp", axis=0, tiled=True), "mp", axis=0)
            for w in (w_q, w_k, w_v, w_o, w_in, w_out)
        ]
        bias_row = jnp.concatenate([q_bias, v_bias, in_bias, jnp.zeros((width,), f32)])
        bias_row = lax.all_gather(bias_row[None], "mp", axis=0)
        parts_a = (jnp.concatenate(gathered[:4], 2), bias_row)
        parts_b = (jnp.concatenate(gathered[4:], 2),)
        table_t = lax.all_gather(edge_table, "dp", axis=0, tiled=True).T
        half = share // 2
        chunks = []
        for i in range(4):
            low, high = (table_t[:, i * share + n * half : i * share + (n + 1) * half] for n in range(2))
            chunks.append(
                jnp.concatenate([low[: heads // 2], low[heads // 2 :], high[: heads // 2], high[heads // 2 :]], 1)
            )
        lookup_place = jnp.zeros((5,), i32)
        ids, buckets, h1, rows_early = prepare(
            place, spatial_ids, path_ids, layer_in, ln1_gain, ln1_bias, cotangent, kinds - 1, spatial_ids
        )
    edge_sums = None
    look = lambda step, after: lookup(lookup_place, chunks[step], ids, edge_sums, step, heads, after)
    if staged:
        edge_sums = look(0, (pair_b,))
        stack_a = join(chunks + [own_biases], height, (edge_sums,))
        across_a, over_a = send(stack_a, links.first), send(stack_a, links.second)
        pair_b = held_until(pair_b, stack_a)
        far_b = send(pair_b, links.along_z[1])
        other_rows_early = send(held_until(rows_early, edge_sums), links.core)
        edge_sums = look(1, (stack_a,))
        four_b = join([pair_b, far_b], 2 * height, (edge_sums,))
        near_b = send(four_b, links.along_z[0])
        edge_sums = look(2, (four_b,))
        eight_b = join_pairs(four_b, near_b, 2 * height, (edge_sums,))
        both_a = send(held_until(across_a, eight_b), links.second)
        over_b = send(eight_b, links.second)
        edge_sums = look(3, (eight_b, other_rows_early))
        mine = (stack_a, across_a, over_a)
        theirs = tuple(send(held_until(part, eight_b), links.core) for part in mine)
        parts_a = mine + (both_a,) + theirs + (send(held_until(both_a, edge_sums), links.core),)
    else:
        for step in range(4):
            edge_sums = look(step, ())

    weights, biases, transposed, value_win, probs, att_low, mid, h2 = attend(
        place, node_counts, h1, edge_sums, buckets, spatial_table,
        layer_in, o_bias, ln2_gain, ln2_bias, parts_a,
    )
    if staged:
        parts_b = (
            eight_b, over_b, send(held_until(eight_b, edge_sums), links.core),
            send(held_until(over_b, mid), links.core),
        )
        feed_after = ()
    else:
        feed_after = ()
    layer_out, grad_mid, grad_att_t, grad_values, mine_b, theirs_b, rows_late, sums = feed(
        place, mid, h2, weights, biases, out_bias, ln2_gain, cotangent, att_low, probs, parts_b, feed_after
    )
    after = sums
    if staged:
        rows_b = (rows_early, rows_late)
        other_rows_b = (other_rows_early, send(rows_late, links.core))
        grads_of = functools.partial(
            weight_grads, plan_second, place, mine_b, send(theirs_b, links.core), rows_b, other_rows_b,
            height, 4 * width, 2,
        )
        (second_b,) = grads_of(hops=2)
        got_second_b = send(second_b, links.second)
        own_b, across_b = grads_of((second_b,), hops=1)
        after = own_b
    score_grads, mine_a, theirs_a, grad_layer_in, sums = attend_back(
        place, probs, value_win, transposed, grad_att_t, grad_values, weights,
        layer_in, ln1_gain, grad_mid, sums, after,
    )
    table = functools.partial(table_grads, place, score_grads, ids, buckets, digit, edges)
    slots = ids.shape[1]
    if staged:
        other_columns_a = send(theirs_a, links.core)
        partial = table(0, 16)
        own_a, across_a, second_a = weight_grads(
            plan_first, place, mine_a, other_columns_a,
            (rows_early[0:1],), (other_rows_b[0][0:1],), height, 2 * width, 2, (partial[0],), 9,
        )
        got_second_a = send(second_a, links.second)
        partial = table(16, 64, partial, after=(own_a,))
        across_b = add_rounded((across_b, got_second_b), (partial[0],))
        got_across_b = send(across_b, links.first)
        partial = table(64, 112, partial, after=(across_b,))
        mine, theirs, small = table(112, slots, partial, sums)
        got_core = send(theirs, links.core)
        half = features // 2
        sent, keep = small_call(
            meet_core_kernel, "meet_core", (shape((64, half), f32), shape((32, half), f32)),
            mine, small, got_core, small, waits=1,
        )
        stay_b, go_b = add_pair((own_b, got_across_b, got_second_b), (sent,))
        got_pair_b = send(go_b, links.along_z[0])
        across_a = add_rounded((across_a, got_second_a), (stay_b,))
        got_across_a = send(across_a, links.first)
        sent, keep = small_call(
            meet_near_kernel, "meet_near", (shape((48, half), f32), shape((16, half), f32)),
            keep, sent, send(sent, links.second), across_a, waits=1,
        )
        got_last = send(sent, links.first)
        own_b, go_b = add_half(stay_b, got_pair_b, (sent,))
        got_b = send(go_b, links.along_z[1])
        own_a = small_call(
            meet_far_kernel, "meet_far", (shape((height + 32, half), bf16),) * 4,
            keep, sent, got_last, own_a, got_across_a, got_second_a,
        )
        got_a = [send(own_a[step + 1], hop) for step, hop in enumerate(links.along_z)]
        grad_w_in, grad_w_out, grad_w_o, grad_w_v = settle([own_b, got_b], width, (own_a[0],))
        grad_w_q, grad_w_k, grad_edge, grad_spatial, *rows = small_call(
            finish_kernel, "finish",
            (shape((height, width), f32),) * 2
            + (shape((8, digit), f32), shape((8, kinds), f32))
            + (shape((features,), f32),) * 6
            + (shape((width,), f32),) * 3,
            place, own_a[0], *got_a, grad_w_in, waits=1, mebibytes=30,
        )
        grad_edge = grad_edge.T
        grad_spatial = grad_spatial.T
    else:
        contract = lambda a, b: lax.dot_general(
            a, b, (((1,), (1,)), ((), ())), preferred_element_type=f32
        )

        def unmix(mine, theirs):
            even = mp_index % 2 == 0
            cores = jnp.where(even, jnp.stack([mine, theirs], 1), jnp.stack([theirs, mine], 1))
            return cores.reshape(4, *mine.shape[1:])

        def scatter(rows_t, columns):
            grads = contract(rows_t, columns)
            grads = jnp.transpose(grads, (1, 0, 2))
            grads = lax.psum_scatter(grads, "mp", scatter_dimension=0, tiled=False)
            return lax.psum_scatter(grads, "dp", scatter_dimension=0, tiled=True)

        columns_a, columns_b = unmix(mine_a, theirs_a), unmix(mine_b, theirs_b)
        grad_w_q, grad_w_k = (
            scatter(rows_early[0], columns_a[:, :, i * width : (i + 1) * width]) for i in range(2)
        )
        grad_w_v = scatter(rows_early[0], columns_b[:, :, 1024 - width :])
        grad_w_in = scatter(rows_late[0], columns_b[:, :, :width])
        grad_w_out = scatter(rows_early[1], columns_b[:, :, 512 - width : 512])
        grad_w_o = scatter(rows_late[1], columns_b[:, :, 512 : 512 + width])
        table, spatial = table(0, slots)
        table = table.reshape(-1, heads, digit).transpose(0, 2, 1).reshape(edges, heads) / hops
        table = lax.psum_scatter(table, "dp", scatter_dimension=0, tiled=True)
        table = lax.psum(table, "mp")
        grad_edge = lax.dynamic_slice_in_dim(table, mp_index * 8, 8, 1)
        totals, spatial = lax.psum((sums, spatial), ("dp", "mp"))
        grad_spatial = lax.dynamic_slice_in_dim(spatial[:, :kinds], mp_index * 8, 8, 0).T
        head_sums = lax.dynamic_slice_in_dim(totals, 8 + mp_index, 1, 0)[0]
        hidden_sums = lax.dynamic_slice_in_dim(totals, 12 + mp_index, 1, 0)[0]
        rows = [totals[i] for i in range(6)]
        rows += [head_sums[:width], head_sums[512 : 512 + width], hidden_sums[:width]]
    return (
        layer_out,
        grad_layer_in,
        rows[0],
        rows[1],
        grad_w_q,
        grad_w_k,
        grad_w_v,
        rows[6],
        rows[7],
        grad_spatial,
        grad_edge,
        grad_w_o,
        rows[2],
        rows[3],
        rows[4],
        grad_w_in,
        rows[8],
        grad_w_out,
        rows[5],
    )


def solution(mesh):
    return jax.shard_map(
        local,
        mesh=mesh,
        in_specs=(
            P(("dp", "mp"), None),
            P("dp"),
            P("dp", None, None),
            P("dp", None, None, None),
            P(),
            P(),
            P("dp", "mp"),
            P("dp", "mp"),
            P("dp", "mp"),
            P("mp"),
            P("mp"),
            P(),
            P("dp", None),
            P("dp", "mp"),
            P(),
            P(),
            P(),
            P("dp", "mp"),
            P("mp"),
            P("dp", "mp"),
            P(),
            P(("dp", "mp"), None),
        ),
        out_specs=(
            P(("dp", "mp"), None),
            P(("dp", "mp"), None),
            P(),
            P(),
            P("dp", "mp"),
            P("dp", "mp"),
            P("dp", "mp"),
            P("mp"),
            P("mp"),
            P(None, "mp"),
            P("dp", "mp"),
            P("dp", "mp"),
            P(),
            P(),
            P(),
            P("dp", "mp"),
            P("mp"),
            P("dp", "mp"),
            P(),
        ),
        check_vma=False,
    )
```
